256 devices in a mesh: ctx: 32 (over y, x, core), head: 8 (over z).
Axes of the slice: x: 4, y: 4, z: 8, core: 2. Of those that a mesh axis runs over, the one named last changes fastest.
Arguments:
- query_in: bfloat16 [8192, 2048], P('ctx', 'head'), may hold values from -6 to 6
- key_in: bfloat16 [8192, 2048], P('ctx', 'head'), may hold values from -3 to 3
- value_in: bfloat16 [8192, 4096], P('ctx', 'head'), may hold values from -6 to 6
- out_gate: bfloat16 [8192, 4096], P('ctx', 'head'), may hold values from -6 to 6
- log_decay: float32 [32, 8192], P('head', 'ctx'), may hold values from -1 to 0
- beta_gate: float32 [32, 8192], P('head', 'ctx'), may hold values from 0.05 to 1
- doc_start: int32 [8192], P('ctx'), may hold values from 0 to 8064, as said below
- conv_query: float32 [4, 2048], P(None, 'head'), may hold values from -3 to 3
- conv_key: float32 [4, 2048], P(None, 'head'), may hold values from -3 to 3
- conv_value: float32 [4, 4096], P(None, 'head'), may hold values from -3 to 3
- norm_gain: float32 [128], replicated, may hold values from 0.1 to 1.9
- out_weight: bfloat16 [4096, 2048], P('head'), may hold values from -0.09375 to 0.09375
Outputs:
- mixed: bfloat16 [8192, 2048], P(('ctx', 'head'))
The draws below stay inside these ranges and needn't reach their ends.
Inputs may be any that keep to these rules, and one draw needn't show every extreme that they name: doc_start[t] is the position of the first token of the document holding token t: it never falls, doc_start[t] <= t and doc_start[0] = 0; the sequence holds at most 8 documents, and the last one begins at 8064.
All inputs are finite; a program needn't handle non-finite values.
Results may differ from the reference program's by a relative error of at most 0.02.
Values may be sent and summed in bfloat16 or wider, within the bound.
No kernel may reach another device: no remote copies, remote signals or barrier semaphores. Data moves between devices by JAX's collectives and lax.ppermute only.
A program may use at most 128 MiB of HBM per device.

```python
import math
import jax
import jax.numpy as jnp
from jax import lax

D = 2048
HK = 16
HV = 32
DK = 128
DV = 128
CONV = 4
DOCS = 8
TOK_DEV = 256
TOKENS = 8192
N_HEAD = 8


def draw_log_decay(key, part):
    key = jax.random.fold_in(key, 11)
    keys = jax.random.split(key, 7)
    shard_count = TOKENS // TOK_DEV
    fast_share = 0.5
    jitter = jnp.exp(jax.random.uniform(keys[0], (HV, TOKENS), jnp.float32, -0.6, 0.6))
    shard_scale = jnp.exp(jax.random.uniform(keys[1], (HV, shard_count), jnp.float32, -0.45, 0.45))
    shard_scale = jnp.repeat(shard_scale, TOK_DEV, axis=1)
    fast_heads = jax.random.uniform(keys[2], (HV, 1), jnp.float32) < fast_share
    fast_rate = jax.random.uniform(keys[3], (HV, 1), jnp.float32, 1.0 / 50.0, 1.0 / 30.0)
    slow_rate = jnp.exp(jax.random.uniform(keys[4], (HV, 1), jnp.float32, math.log(0.05), math.log(0.6))) / TOKENS
    beta_rates_full = jnp.where(fast_heads, fast_rate, slow_rate) * jitter * shard_scale
    start_positions = jax.random.randint(keys[5], (HV, 2), 0, TOKENS)
    decay_factors = jnp.log(jax.random.uniform(keys[6], (HV, 2), jnp.float32, 0.55, 0.8))
    token_position = jnp.arange(TOKENS, dtype=jnp.int32)
    document_segments = jnp.sum(jnp.where(start_positions[:, :, None] == token_position[None, None, :], decay_factors[:, :, None], 0.0), axis=1)
    return (document_segments - beta_rates_full).astype(jnp.float32)


def head_ranks(head_key):
    return jax.random.permutation(head_key, DK)


def draw_key_in(key, part):
    key = jax.random.fold_in(key, 7)
    keys = jax.random.split(key, 2)
    active_count = max(2, DK // 8)
    active_power = 0.35
    base = jnp.clip(jax.random.normal(keys[0], (TOKENS, HK * DK), jnp.float32), -3.0, 3.0)
    faint = math.sqrt(6.0 * active_count * active_power / TOKENS)
    ranks = jax.vmap(head_ranks)(jax.random.split(keys[1], HK))
    active = (ranks < active_count).reshape(1, HK * DK)
    scale = jnp.where(active, 1.0, faint)
    return (base * scale).astype(jnp.bfloat16)


def draw_doc_start(key, part):
    key = jax.random.fold_in(key, 5)
    last_start = TOKENS - TOK_DEV // 2
    inner = jax.random.randint(key, (DOCS - 2,), 1, last_start)
    bounds = jnp.concatenate([inner, jnp.full((1,), last_start, jnp.int32)])
    token_position = jnp.arange(TOKENS, dtype=jnp.int32)
    chosen = jnp.where(bounds[:, None] <= token_position[None, :], bounds[:, None], 0)
    return jnp.max(chosen, axis=0).astype(jnp.int32)


def steps_of(key, shape, shards, smallest, top_value):
    def one(axis_at, blocks):
        steps = jax.random.uniform(jax.random.fold_in(jax.random.fold_in(key, 6), axis_at), (blocks,), jnp.float32, smallest / len(shards), top_value / len(shards))
        return jnp.repeat(jnp.exp(steps), shape[axis_at] // blocks).reshape((-1,) + (1,) * (len(shape) - axis_at - 1))

    gain = one(*shards[0])
    for cut in shards[1:]:
        gain = gain * one(*cut)
    return gain


def bell_draw(own_key, dims, deviation, limit, pieces=(), kind=jnp.bfloat16):
    values = jax.random.normal(own_key, dims, jnp.float32) * deviation
    if len(pieces) > 0:
        values = steps_of(own_key, dims, pieces, -0.22, 0.18) * values
    return jnp.clip(values, min=-limit, max=limit).astype(kind)


def setup_inputs(seed: int = 0) -> dict:
    key_of = jax.random.split(jax.random.key(seed), 13)
    query_in = bell_draw(key_of[0], (TOKENS, HK * DK), 1.0, 6.0, ((0, 32), (1, 8)))
    key_in = draw_key_in(jax.random.fold_in(key_of[12], 71), 0)
    value_in = bell_draw(key_of[2], (TOKENS, HV * DV), 1.0, 6.0, ((0, 32), (1, 8)))
    out_gate = bell_draw(key_of[3], (TOKENS, HV * DV), 1.0, 6.0, ((0, 32), (1, 8)))
    log_decay = draw_log_decay(jax.random.fold_in(key_of[12], 71), 0)
    beta_gate = jnp.clip(0.05 + 0.95 * jax.random.uniform(key_of[5], (HV, TOKENS), jnp.float32) ** steps_of(key_of[5], (HV, TOKENS), ((0, 8), (1, 32)), -0.2, 0.2), 0.05, 1.0)
    doc_start = draw_doc_start(jax.random.fold_in(key_of[12], 71), 0)
    conv_query = bell_draw(key_of[7], (CONV, HK * DK), CONV ** -0.5, 3.0, ((1, 8),), jnp.float32)
    conv_key = bell_draw(key_of[8], (CONV, HK * DK), CONV ** -0.5, 3.0, ((1, 8),), jnp.float32)
    conv_value = bell_draw(key_of[9], (CONV, HV * DV), CONV ** -0.5, 3.0, ((1, 8),), jnp.float32)
    norm_gain = jnp.clip(1.0 + 0.18 * jax.random.normal(key_of[10], (DV,), jnp.float32), 0.1, 1.9)
    out_weight = bell_draw(key_of[11], (HV * DV, D), (HV * DV) ** -0.5, 0.09375, ((0, 8),))
    return {"query_in": query_in, "key_in": key_in, "value_in": value_in, "out_gate": out_gate, "log_decay": log_decay, "beta_gate": beta_gate, "doc_start": doc_start, "conv_query": conv_query, "conv_key": conv_key, "conv_value": conv_value, "norm_gain": norm_gain, "out_weight": out_weight}


EXACT_PRECISION = lax.Precision.HIGHEST
epsilon = 1e-06

def short_conv(signal, weight, doc_start):
    length_all = signal.shape[0]
    token_position = jnp.arange(length_all, dtype=jnp.int32)
    source = signal.astype(jnp.float32)
    accum = jnp.zeros(source.shape, jnp.float32)
    for tap_index in range(CONV):
        shifted = jnp.concatenate([jnp.zeros((tap_index, source.shape[1]), jnp.float32), source[:length_all - tap_index]], axis=0)
        valid = (doc_start <= token_position - tap_index).astype(jnp.float32)
        accum = accum + shifted * weight[tap_index][None, :] * valid[:, None]
    return jax.nn.silu(accum)

def reference(query_in, key_in, value_in, out_gate, log_decay, beta_gate, doc_start, conv_query, conv_key, conv_value, norm_gain, out_weight):
    length_all = doc_start.shape[0]
    query_conv = short_conv(query_in, conv_query, doc_start).reshape(length_all, HK, DK)
    key_conv = short_conv(key_in, conv_key, doc_start).reshape(length_all, HK, DK)
    value_conv = short_conv(value_in, conv_value, doc_start).reshape(length_all, HV, DV)
    key_unit = key_conv * lax.rsqrt(lax.optimization_barrier(jnp.sum(key_conv * key_conv, axis=-1, keepdims=True)) + epsilon)
    group_ratio = HV // HK
    token_position = jnp.arange(length_all, dtype=jnp.int32)
    keep_factor = jnp.exp(log_decay) * (doc_start < token_position).astype(jnp.float32)[None, :]

    def advance_token(current_state, inputs):
        query_at_step, key_at_step, value_t, keep_t, beta_t = inputs
        query_at_step = jnp.repeat(query_at_step, group_ratio, axis=0)
        key_at_step = jnp.repeat(key_at_step, group_ratio, axis=0)
        current_state = current_state * keep_t[:, None, None]
        retrieved_values = jnp.einsum('io,ioe->ie', key_at_step, current_state, precision=EXACT_PRECISION)
        update = beta_t[:, None] * (value_t - retrieved_values)
        current_state = current_state + key_at_step[:, :, None] * update[:, None, :]
        return (current_state, jnp.einsum('io,ioe->ie', query_at_step, current_state, precision=EXACT_PRECISION))
    initial = jnp.zeros((HV, DK, DV), jnp.float32)
    _, heads_out = lax.scan(advance_token, initial, (query_conv, key_unit, value_conv, keep_factor.T, beta_gate.T))
    gate_float = out_gate.reshape(length_all, HV, DV).astype(jnp.float32)
    inv_rms = lax.rsqrt(lax.optimization_barrier(jnp.mean(heads_out * heads_out, axis=-1, keepdims=True)) + epsilon)
    normed = (heads_out * inv_rms * norm_gain * jax.nn.silu(gate_float)).reshape(length_all, HV * DV).astype(jnp.bfloat16)
    group_width = HV * DV // N_HEAD
    mixed = jnp.zeros((length_all, D), jnp.float32)
    for group_index in range(N_HEAD):
        lo_col = group_index * group_width
        part_sum = jnp.dot(normed[:, lo_col:lo_col + group_width], out_weight[lo_col:lo_col + group_width], preferred_element_type=jnp.float32)
        part_sum = lax.optimization_barrier(part_sum.astype(jnp.bfloat16))
        mixed = mixed + part_sum.astype(jnp.float32)
    return mixed.astype(jnp.bfloat16)
```

```python
import jax
import jax.numpy as jnp
from jax import lax
from jax.experimental import pallas as pl
from jax.experimental.pallas import tpu as pltpu
from jax.sharding import PartitionSpec as P

DK = 128
DV = 128
TOK = 256
HEADS = 4
GROUPS = 2
TAPS = 4
RIM = 16
EPS = 1e-6
F32 = jnp.float32
BF16 = jnp.bfloat16
FAR = -1e30
MIB = 1 << 20

CTX = 32
CORES = 2
CHIPS_X = 4
CHIPS_Y = 4


def core_swap():
    return [(i, i ^ 1) for i in range(CTX)]


def along_x(step):
    return [
        ((y * 4 + x) * 2 + c, (y * 4 + (x + step) % 4) * 2 + c)
        for y in range(4)
        for x in range(4)
        for c in range(2)
    ]


def along_y(step):
    return [
        ((y * 4 + x) * 2 + c, (((y + step) % 4) * 4 + x) * 2 + c)
        for y in range(4)
        for x in range(4)
        for c in range(2)
    ]


def mm(left, right):
    return jnp.dot(left, right, preferred_element_type=F32)


def mm_t(left, right):
    return lax.dot_general(left, right, (((1,), (1,)), ((), ())), preferred_element_type=F32)


def parts(value, count):
    out = []
    for _ in range(count):
        piece = value.astype(BF16)
        out.append(piece)
        value = value - piece.astype(F32)
    return out


def rows_and_columns(shape=(TOK, TOK)):
    return lax.broadcasted_iota(jnp.int32, shape, 0), lax.broadcasted_iota(jnp.int32, shape, 1)


def spread(rows_list, pattern, count):
    out = []
    for pair in range(0, len(rows_list), 2):
        chosen = rows_list[pair : pair + 2]
        wide = jnp.concatenate([jnp.broadcast_to(r, (128, TOK)) for r in chosen], axis=0)
        total = None
        for piece in parts(wide, count):
            term = mm_t(pattern, piece)
            total = term if total is None else total + term
        for k in range(len(chosen)):
            out.append(total[:, k * 128 : (k + 1) * 128])
    return out


def local_start(doc_ref):
    first = lax.axis_index("ctx") * TOK
    return jnp.maximum(doc_ref[...] - first, -TAPS).astype(F32)


def short_conv(ext_ref, x_ref, rim, w_ref, valid):
    width = x_ref.shape[1]
    own = x_ref[...].astype(F32)
    ext_ref[0:8, :width] = rim
    ext_ref[8 : 8 + TOK, :width] = own
    total = own * w_ref[0:1, :]
    for tap in range(1, TAPS):
        shifted = ext_ref[8 - tap : 8 - tap + TOK, :width]
        mask = jnp.concatenate([valid[tap - 1]] * (width // 128), axis=1)
        total = total + jnp.where(mask, shifted * w_ref[tap : tap + 1, :], 0.0)
    return total * jax.nn.sigmoid(total)


def tap_masks(start):
    token = lax.broadcasted_iota(jnp.int32, (TOK, 128), 0).astype(F32)
    return [start <= token - tap for tap in range(1, TAPS)]


def unit_keys(key_conv):
    out = []
    for g in range(GROUPS):
        k = key_conv[:, g * DK : (g + 1) * DK]
        out.append(k * lax.rsqrt(jnp.sum(k * k, axis=-1, keepdims=True) + EPS))
    return out


def fading(cum_col, cum_row, start, keep):
    gap = jnp.concatenate([cum_col, cum_col], axis=1) - cum_row
    return jnp.exp(jnp.where(keep, gap, FAR))


def linked_mask(start):
    row, col = rows_and_columns()
    begin = jnp.concatenate([start, start], axis=1)
    return (col <= row) & (begin <= col.astype(F32))


def unit_lower_inverse(a, row, col):
    apart = row ^ col
    eye = (row == col).astype(F32)
    d = jnp.where(apart < 8, a, 0.0)
    db = d.astype(BF16)
    square = mm(db, db).astype(BF16)
    t = eye - d
    t = t + mm(t.astype(BF16), square)
    fourth = mm(square, square).astype(BF16)
    t = t + mm(t.astype(BF16), fourth)
    size = 8
    while size < TOK:
        e = jnp.where((apart >= size) & (apart < 2 * size), a, 0.0).astype(BF16)
        tb = t.astype(BF16)
        t = t - mm(mm(tb, e).astype(BF16), tb)
        size *= 2
    guess = t.astype(BF16)
    high, low = parts(a, 2)
    rest = eye - guess.astype(F32) - mm(high, guess) - mm(low, guess)
    return guess.astype(F32) + mm(guess, rest.astype(BF16))


def pack_kernel(q_ref, k_ref, v_ref, out_ref):
    out_ref[:, 0:256] = q_ref[...]
    out_ref[:, 256:512] = k_ref[...]
    out_ref[:, 512:1024] = v_ref[...]


def map_kernel(
    k_ref, v_ref, rim_ref, decay_ref, beta_ref, doc_ref, wk_ref, wv_ref,
    wu_ref, kb_ref, own_ref, give_ref, ext_ref,
):
    row, col = rows_and_columns()
    lower = (col <= row).astype(BF16)
    eye = (col == row).astype(BF16)
    rim = rim_ref[...].astype(F32)[8:16]
    start = spread([local_start(doc_ref)], eye, 1)[0]
    valid = tap_masks(start)
    key_conv = short_conv(ext_ref, k_ref, rim[:, 256:512], wk_ref, valid)
    value_conv = short_conv(ext_ref, v_ref, rim[:, 512:1024], wv_ref, valid)
    keys = [k.astype(BF16) for k in unit_keys(key_conv)]
    decay = decay_ref[...]
    beta = beta_ref[...]
    cum_row = sum(mm_t(piece, lower) for piece in parts(decay, 3))
    cum_col = spread([decay[h : h + 1] for h in range(HEADS)], lower, 3)
    beta_col = spread([beta[h : h + 1] for h in range(HEADS)], eye, 2)
    keep = linked_mask(start)
    gram = [mm_t(k, k) for k in keys]
    flipped = [k.astype(F32).T for k in keys]
    core = lax.axis_index("ctx") % CORES
    for g in range(GROUPS):
        kb_ref[g] = keys[g]
    for h in range(HEADS):
        g = h // 2
        key = keys[g].astype(F32)
        fade = fading(cum_col[h], cum_row[h : h + 1], start, keep)
        beta_wide = jnp.concatenate([beta_col[h], beta_col[h]], axis=1)
        a = jnp.where(col < row, beta_wide * fade * gram[g], 0.0)
        t = unit_lower_inverse(a, row, col) * beta[h : h + 1]
        carry = jnp.where(start < 0.0, jnp.exp(cum_col[h]), 0.0)
        right = jnp.concatenate(
            [(carry * key).astype(BF16), value_conv[:, h * DV : (h + 1) * DV].astype(BF16)], axis=1
        )
        high, low = parts(t, 2)
        solved = (mm(high, right) + mm(low, right)).astype(BF16)
        wu_ref[h] = solved
        faded = (flipped[g] * fade[TOK - 1 : TOK, :]).astype(BF16)
        both = mm(faded, solved)
        r, c = rows_and_columns((DK, DK))
        diagonal = jnp.where(r == c, jnp.broadcast_to(carry[TOK - 1 : TOK, :], (DK, DK)), 0.0)
        step = jnp.concatenate([diagonal - both[:, :DK], both[:, DK:]], axis=1).astype(BF16)

        @pl.when(core == h // 2)
        def _():
            own_ref[h % 2] = step

        @pl.when(core != h // 2)
        def _():
            give_ref[h % 2] = step


def output_kernel(
    q_ref, rim_ref, decay_ref, doc_ref, wq_ref, kb_ref, wu_ref, out_ref, reach_ref, ext_ref
):
    row, col = rows_and_columns()
    lower = (col <= row).astype(BF16)
    eye = (col == row).astype(BF16)
    rim = rim_ref[...].astype(F32)[8:16]
    start = spread([local_start(doc_ref)], eye, 1)[0]
    query_conv = short_conv(ext_ref, q_ref, rim[:, 0:256], wq_ref, tap_masks(start))
    decay = decay_ref[...]
    cum_row = sum(mm_t(piece, lower) for piece in parts(decay, 3))
    cum_col = spread([decay[h : h + 1] for h in range(HEADS)], lower, 3)
    keep = linked_mask(start)
    scores = []
    for g in range(GROUPS):
        query = query_conv[:, g * DK : (g + 1) * DK].astype(BF16)
        scores.append(mm_t(query, kb_ref[g]))
    for h in range(HEADS):
        g = h // 2
        fade = fading(cum_col[h], cum_row[h : h + 1], start, keep)
        both = mm((fade * scores[g]).astype(BF16), wu_ref[h])
        carry = jnp.where(start < 0.0, jnp.exp(cum_col[h]), 0.0)
        reach = carry * query_conv[:, g * DK : (g + 1) * DK] - both[:, :DK]
        reach_ref[h] = reach.astype(BF16)
        out_ref[h] = both[:, DK:]


def joined(first, later):
    moved = mm(later[:, :DK], first)
    return jnp.concatenate([moved[:, :DK], moved[:, DK:] + later[:, DK:].astype(F32)], axis=1)


def pair_kernel(own_ref, got_ref, out_ref):
    core = lax.axis_index("ctx") % CORES
    for k in range(2):
        own = own_ref[k]
        got = got_ref[k]
        first = jnp.where(core == 0, own, got)
        later = jnp.where(core == 0, got, own)
        out_ref[k] = joined(first, later).astype(BF16)


def row_kernel(own_ref, one_ref, two_ref, three_ref, before_ref, total_ref, slots):
    x = (lax.axis_index("ctx") // CORES) % CHIPS_X
    for step, ref in enumerate((own_ref, one_ref, two_ref, three_ref)):
        slots[(x + CHIPS_X - step) % CHIPS_X] = ref[...]
    r, c = rows_and_columns((DK, DK + DV))
    start = (r == c).astype(BF16)
    for k in range(2):
        run = slots[0, k]
        before_ref[k] = jnp.where(x == 0, start, run)
        for place in range(1, CHIPS_X):
            run = joined(run, slots[place, k]).astype(BF16)
            if place < CHIPS_X - 1:
                before_ref[k] = jnp.where(x == place + 1, run, before_ref[k])
        total_ref[k] = run


def state_kernel(
    own_ref, one_ref, two_ref, three_ref, before_ref, mine_ref, other_ref, keep_ref, give_ref, slots
):
    index = lax.axis_index("ctx")
    core = index % CORES
    y = index // (CORES * CHIPS_X)
    for step, ref in enumerate((own_ref, one_ref, two_ref, three_ref)):
        slots[(y + CHIPS_Y - step) % CHIPS_Y] = ref[...]
    for k in range(2):
        state = jnp.where(y > 0, slots[0, k][:, DK:].astype(F32), 0.0)
        for place in range(1, CHIPS_Y - 1):
            block = slots[place, k]
            moved = mm(block[:, :DK], state.astype(BF16)) + block[:, DK:].astype(F32)
            state = jnp.where(place < y, moved, state)
        block = before_ref[k]
        state = mm(block[:, :DK], state.astype(BF16)) + block[:, DK:].astype(F32)
        block = jnp.where(core == 0, mine_ref[k], other_ref[k])
        after = mm(block[:, :DK], state.astype(BF16)) + block[:, DK:].astype(F32)
        keep_ref[k] = jnp.where(core == 0, state, after).astype(BF16)
        give_ref[k] = jnp.where(core == 0, after, state).astype(BF16)


def project_kernel(
    local_ref, reach_ref, mine_ref, got_ref, gate_ref, gain_ref, weight_ref, out_ref,
    weight_buf, normed_buf, sem,
):
    load = pltpu.make_async_copy(weight_ref, weight_buf, sem)
    load.start()
    core = lax.axis_index("ctx") % CORES
    for h in range(HEADS):
        state = jnp.where(core == h // 2, mine_ref[h % 2], got_ref[h % 2])
        heads = local_ref[h] + mm(reach_ref[h], state)
        inv = lax.rsqrt(jnp.mean(heads * heads, axis=-1, keepdims=True) + EPS)
        gate = gate_ref[:, h * DV : (h + 1) * DV].astype(F32)
        gate = gate * jax.nn.sigmoid(gate)
        normed_buf[:, h * DV : (h + 1) * DV] = (heads * inv * gain_ref[...] * gate).astype(BF16)
    load.wait()
    normed = normed_buf[...]
    for part in range(0, weight_buf.shape[1], 512):
        out_ref[:, part : part + 512] = mm(normed, weight_buf[:, part : part + 512]).astype(BF16)


def sum_kernel(in_ref, out_ref):
    total = in_ref[0].astype(F32)
    for k in range(1, in_ref.shape[0]):
        total = total + in_ref[k].astype(F32)
    out_ref[...] = total.astype(BF16)


VMEM = pl.BlockSpec(memory_space=pltpu.VMEM)


def call(kernel, outs, inputs, scratch=(), flops=0, moved=0, limit=32, specs=None):
    return pl.pallas_call(
        kernel,
        out_shape=[jax.ShapeDtypeStruct(s, t) for s, t in outs],
        in_specs=[VMEM] * len(inputs) if specs is None else specs,
        out_specs=[VMEM] * len(outs),
        scratch_shapes=list(scratch),
        compiler_params=pltpu.CompilerParams(vmem_limit_bytes=limit * MIB),
        cost_estimate=pl.CostEstimate(flops=flops, bytes_accessed=moved, transcendentals=0),
    )(*inputs)


def on_device(
    query_in, key_in, value_in, out_gate, log_decay, beta_gate, doc_start,
    conv_query, conv_key, conv_value, norm_gain, out_weight,
):
    doc_row = doc_start.reshape(1, TOK)
    gain_row = norm_gain.reshape(1, DV)
    last = TOK // RIM - 1
    rim = pl.pallas_call(
        pack_kernel,
        grid=(1,),
        out_shape=jax.ShapeDtypeStruct((RIM, 1024), BF16),
        in_specs=[
            pl.BlockSpec((RIM, 256), lambda i: (last, 0)),
            pl.BlockSpec((RIM, 256), lambda i: (last, 0)),
            pl.BlockSpec((RIM, 512), lambda i: (last, 0)),
        ],
        out_specs=pl.BlockSpec((RIM, 1024), lambda i: (0, 0)),
    )(query_in, key_in, value_in)
    rim = lax.ppermute(rim, "ctx", [(i, i + 1) for i in range(CTX - 1)])
    wide = (2, DK, DK + DV)
    solved, keys, own, give = call(
        map_kernel,
        [((HEADS, TOK, DK + DV), BF16), ((GROUPS, TOK, DK), BF16), (wide, BF16), (wide, BF16)],
        [key_in, value_in, rim, log_decay, beta_gate, doc_row, conv_key, conv_value],
        [pltpu.VMEM((8 + TOK, 512), F32)],
        flops=4_000_000_000, moved=2_000_000,
    )
    other = lax.ppermute(give, "ctx", core_swap())
    (pair,) = call(pair_kernel, [(wide, BF16)], [own, other], flops=20_000_000, moved=400_000)
    near = [lax.ppermute(pair, "ctx", along_x(k)) for k in (1, 2, 3)]
    local, reach = call(
        output_kernel,
        [((HEADS, TOK, DV), F32), ((HEADS, TOK, DK), BF16)],
        [query_in, rim, log_decay, doc_row, conv_query, keys, solved],
        [pltpu.VMEM((8 + TOK, 256), F32)],
        flops=2_000_000_000, moved=2_000_000,
    )
    before, total = call(
        row_kernel, [(wide, BF16), (wide, BF16)], [pair] + near,
        [pltpu.VMEM((CHIPS_X,) + wide, BF16)], flops=60_000_000, moved=800_000,
    )
    far = [lax.ppermute(total, "ctx", along_y(k)) for k in (1, 2, 3)]
    narrow = (2, DK, DV)
    mine, to_other = call(
        state_kernel, [(narrow, BF16), (narrow, BF16)], [total] + far + [before, own, other],
        [pltpu.VMEM((CHIPS_Y,) + wide, BF16)], flops=60_000_000, moved=1_000_000,
    )
    got = lax.ppermute(to_other, "ctx", core_swap())
    width = out_weight.shape[1]
    (partial,) = call(
        project_kernel,
        [((TOK, width), BF16)],
        [local, reach, mine, got, out_gate, gain_row, out_weight],
        [
            pltpu.VMEM(out_weight.shape, BF16),
            pltpu.VMEM((TOK, HEADS * DV), BF16),
            pltpu.SemaphoreType.DMA,
        ],
        flops=600_000_000, moved=4_000_000,
        specs=[VMEM] * 6 + [pl.BlockSpec(memory_space=pl.ANY)],
    )
    groups = lax.axis_size("head")
    blocks = lax.all_to_all(
        partial.reshape(groups, TOK // groups, width), "head", 0, 0
    )
    (mixed,) = call(
        sum_kernel, [((TOK // groups, width), BF16)], [blocks], flops=1_000_000, moved=1_200_000
    )
    return mixed


def solution(mesh):
    placed = (
        P("ctx", "head"),
        P("ctx", "head"),
        P("ctx", "head"),
        P("ctx", "head"),
        P("head", "ctx"),
        P("head", "ctx"),
        P("ctx"),
        P(None, "head"),
        P(None, "head"),
        P(None, "head"),
        P(),
        P("head", None),
    )
    return jax.shard_map(
        on_device, mesh=mesh, in_specs=placed, out_specs=P(("ctx", "head"), None), check_vma=False
    )
```

```python
import jax
import jax.numpy as jnp
from jax import lax
from jax.experimental import pallas as pl
from jax.experimental.pallas import tpu as pltpu
from jax.sharding import PartitionSpec as P

DK = 128
DV = 128
TOK = 256
HEADS = 4
GROUPS = 2
TAPS = 4
RIM = 16
EPS = 1e-6
F32 = jnp.float32
BF16 = jnp.bfloat16
FAR = -1e30
MIB = 1 << 20

CTX = 32
CORES = 2
CHIPS_X = 4
CHIPS_Y = 4


def core_swap():
    return [(i, i ^ 1) for i in range(CTX)]


def along_x(step):
    return [
        ((y * 4 + x) * 2 + c, (y * 4 + (x + step) % 4) * 2 + c)
        for y in range(4)
        for x in range(4)
        for c in range(2)
    ]


def along_y(step):
    return [
        ((y * 4 + x) * 2 + c, (((y + step) % 4) * 4 + x) * 2 + c)
        for y in range(4)
        for x in range(4)
        for c in range(2)
    ]


def mm(left, right):
    return jnp.dot(left, right, preferred_element_type=F32)


def mm_t(left, right):
    return lax.dot_general(left, right, (((1,), (1,)), ((), ())), preferred_element_type=F32)


def parts(value, count):
    out = []
    for _ in range(count):
        piece = value.astype(BF16)
        out.append(piece)
        value = value - piece.astype(F32)
    return out


def rows_and_columns(shape=(TOK, TOK)):
    return lax.broadcasted_iota(jnp.int32, shape, 0), lax.broadcasted_iota(jnp.int32, shape, 1)


def spread(rows_list, pattern, count):
    out = []
    for pair in range(0, len(rows_list), 2):
        chosen = rows_list[pair : pair + 2]
        wide = jnp.concatenate([jnp.broadcast_to(r, (128, TOK)) for r in chosen], axis=0)
        total = None
        for piece in parts(wide, count):
            term = mm_t(pattern, piece)
            total = term if total is None else total + term
        for k in range(len(chosen)):
            out.append(total[:, k * 128 : (k + 1) * 128])
    return out


def local_start(doc_ref):
    first = lax.axis_index("ctx") * TOK
    return jnp.maximum(doc_ref[...] - first, -TAPS).astype(F32)


def short_conv(ext_ref, x_ref, rim, w_ref, valid):
    width = x_ref.shape[1]
    own = x_ref[...].astype(F32)
    ext_ref[0:8, :width] = rim
    ext_ref[8 : 8 + TOK, :width] = own
    total = own * w_ref[0:1, :]
    for tap in range(1, TAPS):
        shifted = ext_ref[8 - tap : 8 - tap + TOK, :width]
        mask = jnp.concatenate([valid[tap - 1]] * (width // 128), axis=1)
        total = total + jnp.where(mask, shifted * w_ref[tap : tap + 1, :], 0.0)
    return total * jax.nn.sigmoid(total)


def tap_masks(start):
    token = lax.broadcasted_iota(jnp.int32, (TOK, 128), 0).astype(F32)
    return [start <= token - tap for tap in range(1, TAPS)]


def unit_keys(key_conv):
    out = []
    for g in range(GROUPS):
        k = key_conv[:, g * DK : (g + 1) * DK]
        out.append(k * lax.rsqrt(jnp.sum(k * k, axis=-1, keepdims=True) + EPS))
    return out


def fading(cum_col, cum_row, start, keep):
    gap = jnp.concatenate([cum_col, cum_col], axis=1) - cum_row
    return jnp.exp(jnp.where(keep, gap, FAR))


def linked_mask(start):
    row, col = rows_and_columns()
    begin = jnp.concatenate([start, start], axis=1)
    return (col <= row) & (begin <= col.astype(F32))


def unit_lower_inverse(a, row, col):
    apart = row ^ col
    eye = (row == col).astype(F32)
    d = jnp.where(apart < 8, a, 0.0)
    db = d.astype(BF16)
    square = mm(db, db).astype(BF16)
    t = eye - d
    t = t + mm(t.astype(BF16), square)
    fourth = mm(square, square).astype(BF16)
    t = t + mm(t.astype(BF16), fourth)
    size = 8
    while size < TOK:
        e = jnp.where((apart >= size) & (apart < 2 * size), a, 0.0).astype(BF16)
        tb = t.astype(BF16)
        t = t - mm(mm(tb, e).astype(BF16), tb)
        size *= 2
    guess = t.astype(BF16)
    high, low = parts(a, 2)
    rest = eye - guess.astype(F32) - mm(high, guess) - mm(low, guess)
    return guess.astype(F32) + mm(guess, rest.astype(BF16))


def pack_kernel(k_ref, v_ref, q_ref, out_ref, sems):
    rows = pl.ds(TOK - RIM, RIM)
    copies = [
        pltpu.make_async_copy(k_ref.at[rows], out_ref.at[:, 0:256], sems.at[0]),
        pltpu.make_async_copy(v_ref.at[rows], out_ref.at[:, 256:768], sems.at[1]),
        pltpu.make_async_copy(q_ref.at[rows], out_ref.at[:, 768:1024], sems.at[2]),
    ]
    for copy in copies:
        copy.start()
    for copy in copies:
        copy.wait()


def half_kernel(weight_ref, after_ref, out_ref, sem):
    core = lax.axis_index("ctx") % CORES
    rows = weight_ref.shape[0] // CORES
    copy = pltpu.make_async_copy(weight_ref.at[pl.ds(core * rows, rows)], out_ref, sem)
    copy.start()
    copy.wait()


def early_kernel(
    k_hbm, v_hbm, decay_hbm, beta_hbm, doc_hbm, wk_hbm, wv_hbm,
    key_ref, value_ref, factor_ref, carry_ref, last_ref, start_ref, head_ref,
    k_ref, v_ref, decay_ref, beta_ref, doc_ref, wk_ref, wv_ref, ext_ref, sems,
):
    moves = (
        (doc_hbm, doc_ref), (decay_hbm, decay_ref), (beta_hbm, beta_ref), (k_hbm, k_ref),
        (wk_hbm, wk_ref), (v_hbm, v_ref), (wv_hbm, wv_ref),
    )
    copies = [pltpu.make_async_copy(a, b, sems.at[i]) for i, (a, b) in enumerate(moves)]
    for copy in copies:
        copy.start()
    row, col = rows_and_columns()
    lower = (col <= row).astype(BF16)
    eye = (col == row).astype(BF16)
    for copy in copies[:3]:
        copy.wait()
    start = spread([local_start(doc_ref)], eye, 1)[0]
    start_ref[...] = start[0:RIM]
    decay = decay_ref[...]
    beta = beta_ref[...]
    cum_row = sum(mm_t(piece, lower) for piece in parts(decay, 3))
    cum_col = spread([decay[h : h + 1] for h in range(HEADS)], lower, 3)
    beta_col = spread([beta[h : h + 1] for h in range(HEADS)], eye, 2)
    keep = linked_mask(start)
    for h in range(HEADS):
        fade = fading(cum_col[h], cum_row[h : h + 1], start, keep)
        beta_wide = jnp.concatenate([beta_col[h], beta_col[h]], axis=1)
        factor_ref[h] = jnp.where(col < row, beta_wide * fade, 0.0)
        carry_ref[h] = jnp.where(start < 0.0, jnp.exp(cum_col[h]), 0.0)
        last_ref[h : h + 1] = fade[TOK - 1 : TOK, :]
    for copy in copies[3:]:
        copy.wait()
    valid = tap_masks(start)
    key_conv = short_conv(ext_ref, k_ref, jnp.zeros((8, 256), F32), wk_ref, valid)
    for g, key in enumerate(unit_keys(key_conv)):
        key_ref[g] = key.astype(BF16)
    value_conv = short_conv(ext_ref, v_ref, jnp.zeros((8, 512), F32), wv_ref, valid)
    value_ref[...] = value_conv.astype(BF16)
    head_ref[:, 0:256] = k_ref[0:RIM, :]
    head_ref[:, 256:768] = v_ref[0:RIM, :]


def first_rows(rim, own, w_ref, start):
    width = own.shape[1]
    ext = jnp.concatenate([rim, own], axis=0)
    token = lax.broadcasted_iota(jnp.int32, (8, 128), 0).astype(F32)
    total = own * w_ref[0:1, :]
    for tap in range(1, TAPS):
        mask = jnp.concatenate([start <= token - tap] * (width // 128), axis=1)
        total = total + jnp.where(mask, ext[8 - tap : 16 - tap] * w_ref[tap : tap + 1, :], 0.0)
    return total * jax.nn.sigmoid(total)


def map_kernel(
    rim_ref, head_ref, start_ref, key_ref, value_ref, factor_ref, carry_ref, last_ref, beta_ref,
    wk_ref, wv_ref, wu_ref, kb_ref, own_ref, give_ref,
):
    row, col = rows_and_columns()
    rim = rim_ref[...].astype(F32)[8:16]
    head = head_ref[...].astype(F32)[0:8]
    start = start_ref[0:8]
    first_keys = unit_keys(first_rows(rim[:, 0:256], head[:, 0:256], wk_ref, start))
    first_values = first_rows(rim[:, 256:768], head[:, 256:768], wv_ref, start)

    def patched(first, whole):
        whole = whole.astype(F32)
        return jnp.concatenate([first, whole[8:]], axis=0)

    keys = [patched(first_keys[g], key_ref[g]).astype(BF16) for g in range(GROUPS)]
    values = patched(first_values, value_ref[...]).astype(BF16)
    beta = beta_ref[...]
    gram = [mm_t(k, k) for k in keys]
    flipped = [k.astype(F32).T for k in keys]
    core = lax.axis_index("ctx") % CORES
    for g in range(GROUPS):
        kb_ref[g] = keys[g]
    for h in range(HEADS):
        g = h // 2
        key = keys[g].astype(F32)
        t = unit_lower_inverse(factor_ref[h] * gram[g], row, col) * beta[h : h + 1]
        carry = carry_ref[h]
        right = jnp.concatenate([(carry * key).astype(BF16), values[:, h * DV : (h + 1) * DV]], axis=1)
        high, low = parts(t, 2)
        solved = (mm(high, right) + mm(low, right)).astype(BF16)
        wu_ref[h] = solved
        faded = (flipped[g] * last_ref[h : h + 1, :]).astype(BF16)
        both = mm(faded, solved)
        r, c = rows_and_columns((DK, DK))
        diagonal = jnp.where(r == c, jnp.broadcast_to(carry[TOK - 1 : TOK, :], (DK, DK)), 0.0)
        step = jnp.concatenate([diagonal - both[:, :DK], both[:, DK:]], axis=1).astype(BF16)

        @pl.when(core == h // 2)
        def _():
            own_ref[h % 2] = step

        @pl.when(core != h // 2)
        def _():
            give_ref[h % 2] = step


def output_kernel(
    q_ref, rim_ref, decay_ref, doc_ref, wq_ref, kb_ref, wu_ref, out_ref, reach_ref, ext_ref
):
    row, col = rows_and_columns()
    lower = (col <= row).astype(BF16)
    eye = (col == row).astype(BF16)
    rim = rim_ref[...].astype(F32)[8:16]
    start = spread([local_start(doc_ref)], eye, 1)[0]
    query_conv = short_conv(ext_ref, q_ref, rim[:, 768:1024], wq_ref, tap_masks(start))
    decay = decay_ref[...]
    cum_row = sum(mm_t(piece, lower) for piece in parts(decay, 3))
    cum_col = spread([decay[h : h + 1] for h in range(HEADS)], lower, 3)
    keep = linked_mask(start)
    scores = []
    for g in range(GROUPS):
        query = query_conv[:, g * DK : (g + 1) * DK].astype(BF16)
        scores.append(mm_t(query, kb_ref[g]))
    for h in range(HEADS):
        g = h // 2
        fade = fading(cum_col[h], cum_row[h : h + 1], start, keep)
        both = mm((fade * scores[g]).astype(BF16), wu_ref[h])
        carry = jnp.where(start < 0.0, jnp.exp(cum_col[h]), 0.0)
        reach = carry * query_conv[:, g * DK : (g + 1) * DK] - both[:, :DK]
        reach_ref[h] = reach.astype(BF16)
        out_ref[h] = both[:, DK:]


def joined(first, later):
    moved = mm(later[:, :DK], first)
    return jnp.concatenate([moved[:, :DK], moved[:, DK:] + later[:, DK:].astype(F32)], axis=1)


def pair_kernel(own_ref, got_ref, out_ref):
    core = lax.axis_index("ctx") % CORES
    for k in range(2):
        own = own_ref[k]
        got = got_ref[k]
        first = jnp.where(core == 0, own, got)
        later = jnp.where(core == 0, got, own)
        out_ref[k] = joined(first, later).astype(BF16)


def row_kernel(own_ref, one_ref, two_ref, three_ref, after_ref, before_ref, total_ref, slots):
    x = (lax.axis_index("ctx") // CORES) % CHIPS_X
    for step, ref in enumerate((own_ref, one_ref, two_ref, three_ref)):
        slots[(x + CHIPS_X - step) % CHIPS_X] = ref[...]
    r, c = rows_and_columns((DK, DK + DV))
    start = (r == c).astype(BF16)
    for k in range(2):
        run = slots[0, k]
        before_ref[k] = jnp.where(x == 0, start, run)
        for place in range(1, CHIPS_X):
            run = joined(run, slots[place, k]).astype(BF16)
            if place < CHIPS_X - 1:
                before_ref[k] = jnp.where(x == place + 1, run, before_ref[k])
        total_ref[k] = run


def state_kernel(
    own_ref, one_ref, two_ref, three_ref, before_ref, mine_ref, other_ref, keep_ref, give_ref, slots
):
    index = lax.axis_index("ctx")
    core = index % CORES
    y = index // (CORES * CHIPS_X)
    for step, ref in enumerate((own_ref, one_ref, two_ref, three_ref)):
        slots[(y + CHIPS_Y - step) % CHIPS_Y] = ref[...]
    for k in range(2):
        state = jnp.where(y > 0, slots[0, k][:, DK:].astype(F32), 0.0)
        for place in range(1, CHIPS_Y - 1):
            block = slots[place, k]
            moved = mm(block[:, :DK], state.astype(BF16)) + block[:, DK:].astype(F32)
            state = jnp.where(place < y, moved, state)
        block = before_ref[k]
        state = mm(block[:, :DK], state.astype(BF16)) + block[:, DK:].astype(F32)
        block = jnp.where(core == 0, mine_ref[k], other_ref[k])
        after = mm(block[:, :DK], state.astype(BF16)) + block[:, DK:].astype(F32)
        keep_ref[k] = jnp.where(core == 0, state, after).astype(BF16)
        give_ref[k] = jnp.where(core == 0, after, state).astype(BF16)


def norm_kernel(local_ref, reach_ref, mine_ref, got_ref, gate_ref, gain_ref, keep_ref, give_ref):
    core = lax.axis_index("ctx") % CORES
    side = lax.axis_index("head") % 2
    for h in range(HEADS):
        state = jnp.where(core == h // 2, mine_ref[h % 2], got_ref[h % 2])
        heads = local_ref[h] + mm(reach_ref[h], state)
        inv = lax.rsqrt(jnp.mean(heads * heads, axis=-1, keepdims=True) + EPS)
        gate = gate_ref[:, h * DV : (h + 1) * DV].astype(F32)
        gate = gate * jax.nn.sigmoid(gate)
        normed = (heads * inv * gain_ref[...] * gate).astype(BF16)
        rows = TOK // 8
        for block in range(4):
            even = normed[2 * block * rows : (2 * block + 1) * rows]
            odd = normed[(2 * block + 1) * rows : (2 * block + 2) * rows]
            at = (slice(block * rows, (block + 1) * rows), slice(h * DV, (h + 1) * DV))
            keep_ref[at] = jnp.where(side == 0, even, odd)
            give_ref[at] = jnp.where(side == 0, odd, even)


def project_kernel(keep_ref, got_ref, own_ref, near_ref, far_ref, out_ref):
    core = lax.axis_index("ctx") % CORES
    keep = keep_ref[...]
    got = got_ref[...]
    half = got.shape[1] // 2
    first = jnp.where(core == 0, got[:, :half], got[:, half:])
    second = jnp.where(core == 0, got[:, half:], got[:, :half])
    for part in range(0, own_ref.shape[1], 512):
        at = slice(part, part + 512)
        total = mm(keep, own_ref[:, at]) + mm(first, near_ref[:, at]) + mm(second, far_ref[:, at])
        out_ref[:, at] = total.astype(BF16)


def sum_kernel(in_ref, out_ref):
    total = in_ref[0].astype(F32)
    for k in range(1, in_ref.shape[0]):
        total = total + in_ref[k].astype(F32)
    out_ref[...] = total.astype(BF16)


VMEM = pl.BlockSpec(memory_space=pltpu.VMEM)
HBM = pl.BlockSpec(memory_space=pltpu.HBM)


def call(kernel, outs, inputs, scratch=(), flops=0, moved=0, limit=32, specs=None, out_specs=None):
    return pl.pallas_call(
        kernel,
        out_shape=[jax.ShapeDtypeStruct(s, t) for s, t in outs],
        in_specs=[VMEM] * len(inputs) if specs is None else specs,
        out_specs=[VMEM] * len(outs) if out_specs is None else out_specs,
        scratch_shapes=list(scratch),
        compiler_params=pltpu.CompilerParams(vmem_limit_bytes=limit * MIB),
        cost_estimate=pl.CostEstimate(flops=flops, bytes_accessed=moved, transcendentals=0),
    )(*inputs)


def on_device(
    query_in, key_in, value_in, out_gate, log_decay, beta_gate, doc_start,
    conv_query, conv_key, conv_value, norm_gain, out_weight,
):
    doc_row = doc_start.reshape(1, TOK)
    gain_row = norm_gain.reshape(1, DV)
    width = out_weight.shape[1]
    (edge,) = call(
        pack_kernel, [((RIM, 1024), BF16)], [key_in, value_in, query_in],
        [pltpu.SemaphoreType.DMA((3,))], specs=[HBM] * 3, out_specs=[HBM], limit=60,
    )
    rim = lax.ppermute(edge, "ctx", [(i, i + 1) for i in range(CTX - 1)])
    (half,) = call(
        half_kernel, [((out_weight.shape[0] // CORES, width), BF16)], [out_weight, edge],
        [pltpu.SemaphoreType.DMA], specs=[HBM] * 2, out_specs=[HBM], limit=60,
    )
    near_weight = lax.ppermute(half, "head", [(i, i ^ 1) for i in range(8)])
    wide = (2, DK, DK + DV)
    early = call(
        early_kernel,
        [
            ((GROUPS, TOK, DK), BF16), ((TOK, HEADS * DV), BF16), ((HEADS, TOK, TOK), F32),
            ((HEADS, TOK, 128), F32), ((HEADS, TOK), F32), ((RIM, 128), F32), ((RIM, 768), BF16),
        ],
        [key_in, value_in, log_decay, beta_gate, doc_row, conv_key, conv_value],
        [
            pltpu.VMEM((TOK, 256), BF16), pltpu.VMEM((TOK, 512), BF16),
            pltpu.VMEM((HEADS, TOK), F32), pltpu.VMEM((HEADS, TOK), F32),
            pltpu.VMEM((1, TOK), jnp.int32), pltpu.VMEM((TAPS, 256), F32),
            pltpu.VMEM((TAPS, 512), F32), pltpu.VMEM((8 + TOK, 512), F32),
            pltpu.SemaphoreType.DMA((7,)),
        ],
        flops=500_000_000, moved=1_500_000, specs=[HBM] * 7, limit=50,
    )
    keys, values, factor, carry, last, start, head = early
    solved, keys, own, give = call(
        map_kernel,
        [((HEADS, TOK, DK + DV), BF16), ((GROUPS, TOK, DK), BF16), (wide, BF16), (wide, BF16)],
        [rim, head, start, keys, values, factor, carry, last, beta_gate, conv_key, conv_value],
        flops=4_000_000_000, moved=2_000_000,
    )
    other = lax.ppermute(give, "ctx", core_swap())
    (pair,) = call(pair_kernel, [(wide, BF16)], [own, other], flops=20_000_000, moved=400_000)
    near = [lax.ppermute(pair, "ctx", along_x(k)) for k in (1, 2, 3)]
    local, reach = call(
        output_kernel,
        [((HEADS, TOK, DV), F32), ((HEADS, TOK, DK), BF16)],
        [query_in, rim, log_decay, doc_row, conv_query, keys, solved],
        [pltpu.VMEM((8 + TOK, 256), F32)],
        flops=2_000_000_000, moved=2_000_000,
    )
    before, total = call(
        row_kernel, [(wide, BF16), (wide, BF16)], [pair] + near + [reach],
        [pltpu.VMEM((CHIPS_X,) + wide, BF16)], flops=60_000_000, moved=800_000,
        specs=[VMEM] * 4 + [HBM],
    )
    far = [lax.ppermute(total, "ctx", along_y(k)) for k in (1, 2, 3)]
    late_weight, _ = lax.optimization_barrier((near_weight, total))
    far_weight = lax.ppermute(late_weight, "ctx", core_swap())
    narrow = (2, DK, DV)
    mine, to_other = call(
        state_kernel, [(narrow, BF16), (narrow, BF16)], [total] + far + [before, own, other],
        [pltpu.VMEM((CHIPS_Y,) + wide, BF16)], flops=60_000_000, moved=1_000_000,
    )
    got = lax.ppermute(to_other, "ctx", core_swap())
    rows = (TOK // 2, HEADS * DV)
    keep, to_near = call(
        norm_kernel, [(rows, BF16), (rows, BF16)],
        [local, reach, mine, got, out_gate, gain_row],
        flops=100_000_000, moved=1_500_000,
    )
    brought = lax.ppermute(to_near, "head", [(i, i ^ 1) for i in range(8)])
    (partial,) = call(
        project_kernel, [((TOK // 2, width), BF16)],
        [keep, brought, out_weight, near_weight, far_weight],
        flops=600_000_000, moved=4_000_000,
    )
    blocks = lax.all_to_all(
        partial.reshape(4, TOK // 8, width), "head", 0, 0,
        axis_index_groups=[[0, 2, 4, 6], [1, 3, 5, 7]],
    )
    (mixed,) = call(
        sum_kernel, [((TOK // 8, width), BF16)], [blocks], flops=1_000_000, moved=1_200_000
    )
    return mixed


def solution(mesh):
    placed = (
        P("ctx", "head"),
        P("ctx", "head"),
        P("ctx", "head"),
        P("ctx", "head"),
        P("head", "ctx"),
        P("head", "ctx"),
        P("ctx"),
        P(None, "head"),
        P(None, "head"),
        P(None, "head"),
        P(),
        P("head", None),
    )
    return jax.shard_map(
        on_device, mesh=mesh, in_specs=placed, out_specs=P(("ctx", "head"), None), check_vma=False
    )
```

```python
import jax
import jax.numpy as jnp
from jax import lax
from jax.experimental import pallas as pl
from jax.experimental.pallas import tpu as pltpu
from jax.sharding import PartitionSpec as P

DK = 128
DV = 128
TOK = 256
HEADS = 4
GROUPS = 2
TAPS = 4
RIM = 16
EPS = 1e-6
F32 = jnp.float32
BF16 = jnp.bfloat16
FAR = -1e30
MIB = 1 << 20

CTX = 32
CORES = 2
CHIPS_X = 4
CHIPS_Y = 4


def core_swap():
    return [(i, i ^ 1) for i in range(CTX)]


def along_x(step):
    return [
        ((y * 4 + x) * 2 + c, (y * 4 + (x + step) % 4) * 2 + c)
        for y in range(4)
        for x in range(4)
        for c in range(2)
    ]


def along_y(step):
    return [
        ((y * 4 + x) * 2 + c, (((y + step) % 4) * 4 + x) * 2 + c)
        for y in range(4)
        for x in range(4)
        for c in range(2)
    ]


def mm(left, right):
    return jnp.dot(left, right, preferred_element_type=F32)


def mm_t(left, right):
    return lax.dot_general(left, right, (((1,), (1,)), ((), ())), preferred_element_type=F32)


def parts(value, count):
    out = []
    for _ in range(count):
        piece = value.astype(BF16)
        out.append(piece)
        value = value - piece.astype(F32)
    return out


def rows_and_columns(shape=(TOK, TOK)):
    return lax.broadcasted_iota(jnp.int32, shape, 0), lax.broadcasted_iota(jnp.int32, shape, 1)


def spread(rows_list, pattern, count):
    out = []
    for pair in range(0, len(rows_list), 2):
        chosen = rows_list[pair : pair + 2]
        wide = jnp.concatenate([jnp.broadcast_to(r, (128, TOK)) for r in chosen], axis=0)
        total = None
        for piece in parts(wide, count):
            term = mm_t(pattern, piece)
            total = term if total is None else total + term
        for k in range(len(chosen)):
            out.append(total[:, k * 128 : (k + 1) * 128])
    return out


def local_start(doc_ref):
    first = lax.axis_index("ctx") * TOK
    return jnp.maximum(doc_ref[...] - first, -TAPS).astype(F32)


def short_conv(ext_ref, x_ref, rim, w_ref, valid):
    width = x_ref.shape[1]
    own = x_ref[...].astype(F32)
    ext_ref[0:8, :width] = rim
    ext_ref[8 : 8 + TOK, :width] = own
    total = own * w_ref[0:1, :]
    for tap in range(1, TAPS):
        shifted = ext_ref[8 - tap : 8 - tap + TOK, :width]
        mask = jnp.concatenate([valid[tap - 1]] * (width // 128), axis=1)
        total = total + jnp.where(mask, shifted * w_ref[tap : tap + 1, :], 0.0)
    return total * jax.nn.sigmoid(total)


def tap_masks(start):
    token = lax.broadcasted_iota(jnp.int32, (TOK, 128), 0).astype(F32)
    return [start <= token - tap for tap in range(1, TAPS)]


def unit_keys(key_conv):
    out = []
    for g in range(GROUPS):
        k = key_conv[:, g * DK : (g + 1) * DK]
        out.append(k * lax.rsqrt(jnp.sum(k * k, axis=-1, keepdims=True) + EPS))
    return out


def fading(cum_col, cum_row, start, keep):
    gap = jnp.concatenate([cum_col, cum_col], axis=1) - cum_row
    return jnp.exp(jnp.where(keep, gap, FAR))


def linked_mask(start):
    row, col = rows_and_columns()
    begin = jnp.concatenate([start, start], axis=1)
    return (col <= row) & (begin <= col.astype(F32))


def unit_lower_inverse(a, row, col):
    apart = row ^ col
    eye = (row == col).astype(F32)
    d = jnp.where(apart < 8, a, 0.0)
    db = d.astype(BF16)
    square = mm(db, db).astype(BF16)
    t = eye - d
    t = t + mm(t.astype(BF16), square)
    fourth = mm(square, square).astype(BF16)
    t = t + mm(t.astype(BF16), fourth)
    size = 8
    while size < TOK:
        e = jnp.where((apart >= size) & (apart < 2 * size), a, 0.0).astype(BF16)
        tb = t.astype(BF16)
        t = t - mm(mm(tb, e).astype(BF16), tb)
        size *= 2
    guess = t.astype(BF16)
    high, low = parts(a, 2)
    rest = eye - guess.astype(F32) - mm(high, guess) - mm(low, guess)
    return guess.astype(F32) + mm(guess, rest.astype(BF16))


def pack_kernel(k_ref, v_ref, q_ref, out_ref):
    out_ref[:, 0:256] = k_ref[...]
    out_ref[:, 256:768] = v_ref[...]
    out_ref[:, 768:1024] = q_ref[...]


def half_kernel(weight_ref, after_ref, out_ref, sem):
    core = lax.axis_index("ctx") % CORES
    rows = weight_ref.shape[0] // CORES
    copy = pltpu.make_async_copy(weight_ref.at[pl.ds(core * rows, rows)], out_ref, sem)
    copy.start()
    copy.wait()


def early_kernel(
    k_hbm, v_hbm, decay_hbm, beta_hbm, doc_hbm, wk_hbm, wv_hbm,
    key_ref, value_ref, factor_ref, carry_ref, last_ref, start_ref, head_ref,
    k_ref, v_ref, decay_ref, beta_ref, doc_ref, wk_ref, wv_ref, ext_ref, sems,
):
    moves = (
        (doc_hbm, doc_ref), (decay_hbm, decay_ref), (beta_hbm, beta_ref), (k_hbm, k_ref),
        (wk_hbm, wk_ref), (v_hbm, v_ref), (wv_hbm, wv_ref),
    )
    copies = [pltpu.make_async_copy(a, b, sems.at[i]) for i, (a, b) in enumerate(moves)]
    for copy in copies:
        copy.start()
    row, col = rows_and_columns()
    lower = (col <= row).astype(BF16)
    eye = (col == row).astype(BF16)
    for copy in copies[:3]:
        copy.wait()
    start = spread([local_start(doc_ref)], eye, 1)[0]
    start_ref[...] = start[0:RIM]
    decay = decay_ref[...]
    beta = beta_ref[...]
    cum_row = sum(mm_t(piece, lower) for piece in parts(decay, 3))
    cum_col = spread([decay[h : h + 1] for h in range(HEADS)], lower, 3)
    beta_col = spread([beta[h : h + 1] for h in range(HEADS)], eye, 2)
    keep = linked_mask(start)
    for h in range(HEADS):
        fade = fading(cum_col[h], cum_row[h : h + 1], start, keep)
        beta_wide = jnp.concatenate([beta_col[h], beta_col[h]], axis=1)
        factor_ref[h] = jnp.where(col < row, beta_wide * fade, 0.0)
        carry_ref[h] = jnp.where(start < 0.0, jnp.exp(cum_col[h]), 0.0)
        last_ref[h : h + 1] = fade[TOK - 1 : TOK, :]
    for copy in copies[3:]:
        copy.wait()
    valid = tap_masks(start)
    key_conv = short_conv(ext_ref, k_ref, jnp.zeros((8, 256), F32), wk_ref, valid)
    for g, key in enumerate(unit_keys(key_conv)):
        key_ref[g] = key.astype(BF16)
    value_conv = short_conv(ext_ref, v_ref, jnp.zeros((8, 512), F32), wv_ref, valid)
    value_ref[...] = value_conv.astype(BF16)
    head_ref[:, 0:256] = k_ref[0:RIM, :]
    head_ref[:, 256:768] = v_ref[0:RIM, :]


def first_rows(rim, own, w_ref, start):
    width = own.shape[1]
    ext = jnp.concatenate([rim, own], axis=0)
    token = lax.broadcasted_iota(jnp.int32, (8, 128), 0).astype(F32)
    total = own * w_ref[0:1, :]
    for tap in range(1, TAPS):
        mask = jnp.concatenate([start <= token - tap] * (width // 128), axis=1)
        total = total + jnp.where(mask, ext[8 - tap : 16 - tap] * w_ref[tap : tap + 1, :], 0.0)
    return total * jax.nn.sigmoid(total)


def map_kernel(
    rim_ref, head_ref, start_ref, key_ref, value_ref, factor_ref, carry_ref, last_ref, beta_ref,
    wk_ref, wv_ref, wu_ref, kb_ref, own_ref, give_ref,
):
    row, col = rows_and_columns()
    rim = rim_ref[...].astype(F32)[8:16]
    head = head_ref[...].astype(F32)[0:8]
    start = start_ref[0:8]
    first_keys = unit_keys(first_rows(rim[:, 0:256], head[:, 0:256], wk_ref, start))
    first_values = first_rows(rim[:, 256:768], head[:, 256:768], wv_ref, start)

    def patched(first, whole):
        whole = whole.astype(F32)
        return jnp.concatenate([first, whole[8:]], axis=0)

    keys = [patched(first_keys[g], key_ref[g]).astype(BF16) for g in range(GROUPS)]
    values = patched(first_values, value_ref[...]).astype(BF16)
    beta = beta_ref[...]
    gram = [mm_t(k, k) for k in keys]
    flipped = [k.astype(F32).T for k in keys]
    core = lax.axis_index("ctx") % CORES
    for g in range(GROUPS):
        kb_ref[g] = keys[g]
    for h in range(HEADS):
        g = h // 2
        key = keys[g].astype(F32)
        t = unit_lower_inverse(factor_ref[h] * gram[g], row, col) * beta[h : h + 1]
        carry = carry_ref[h]
        right = jnp.concatenate([(carry * key).astype(BF16), values[:, h * DV : (h + 1) * DV]], axis=1)
        high, low = parts(t, 2)
        solved = (mm(high, right) + mm(low, right)).astype(BF16)
        wu_ref[h] = solved
        faded = (flipped[g] * last_ref[h : h + 1, :]).astype(BF16)
        both = mm(faded, solved)
        r, c = rows_and_columns((DK, DK))
        diagonal = jnp.where(r == c, jnp.broadcast_to(carry[TOK - 1 : TOK, :], (DK, DK)), 0.0)
        step = jnp.concatenate([diagonal - both[:, :DK], both[:, DK:]], axis=1).astype(BF16)

        @pl.when(core == h // 2)
        def _():
            own_ref[h % 2] = step

        @pl.when(core != h // 2)
        def _():
            give_ref[h % 2] = step


def output_kernel(
    q_ref, rim_ref, decay_ref, doc_ref, wq_ref, kb_ref, wu_ref, out_ref, reach_ref, ext_ref
):
    row, col = rows_and_columns()
    lower = (col <= row).astype(BF16)
    eye = (col == row).astype(BF16)
    rim = rim_ref[...].astype(F32)[8:16]
    start = spread([local_start(doc_ref)], eye, 1)[0]
    query_conv = short_conv(ext_ref, q_ref, rim[:, 768:1024], wq_ref, tap_masks(start))
    decay = decay_ref[...]
    cum_row = sum(mm_t(piece, lower) for piece in parts(decay, 3))
    cum_col = spread([decay[h : h + 1] for h in range(HEADS)], lower, 3)
    keep = linked_mask(start)
    scores = []
    for g in range(GROUPS):
        query = query_conv[:, g * DK : (g + 1) * DK].astype(BF16)
        scores.append(mm_t(query, kb_ref[g]))
    for h in range(HEADS):
        g = h // 2
        fade = fading(cum_col[h], cum_row[h : h + 1], start, keep)
        both = mm((fade * scores[g]).astype(BF16), wu_ref[h])
        carry = jnp.where(start < 0.0, jnp.exp(cum_col[h]), 0.0)
        reach = carry * query_conv[:, g * DK : (g + 1) * DK] - both[:, :DK]
        reach_ref[h] = reach.astype(BF16)
        out_ref[h] = both[:, DK:]


def joined(first, later):
    moved = mm(later[:, :DK], first)
    return jnp.concatenate([moved[:, :DK], moved[:, DK:] + later[:, DK:].astype(F32)], axis=1)


def pair_kernel(own_ref, got_ref, out_ref):
    core = lax.axis_index("ctx") % CORES
    for k in range(2):
        own = own_ref[k]
        got = got_ref[k]
        first = jnp.where(core == 0, own, got)
        later = jnp.where(core == 0, got, own)
        out_ref[k] = joined(first, later).astype(BF16)


def row_kernel(own_ref, one_ref, two_ref, three_ref, after_ref, before_ref, total_ref, slots):
    x = (lax.axis_index("ctx") // CORES) % CHIPS_X
    for step, ref in enumerate((own_ref, one_ref, two_ref, three_ref)):
        slots[(x + CHIPS_X - step) % CHIPS_X] = ref[...]
    r, c = rows_and_columns((DK, DK + DV))
    start = (r == c).astype(BF16)
    for k in range(2):
        run = slots[0, k]
        before_ref[k] = jnp.where(x == 0, start, run)
        for place in range(1, CHIPS_X):
            run = joined(run, slots[place, k]).astype(BF16)
            if place < CHIPS_X - 1:
                before_ref[k] = jnp.where(x == place + 1, run, before_ref[k])
        total_ref[k] = run


def state_kernel(
    own_ref, one_ref, two_ref, three_ref, before_ref, mine_ref, other_ref, keep_ref, give_ref, slots
):
    index = lax.axis_index("ctx")
    core = index % CORES
    y = index // (CORES * CHIPS_X)
    for step, ref in enumerate((own_ref, one_ref, two_ref, three_ref)):
        slots[(y + CHIPS_Y - step) % CHIPS_Y] = ref[...]
    for k in range(2):
        state = jnp.where(y > 0, slots[0, k][:, DK:].astype(F32), 0.0)
        for place in range(1, CHIPS_Y - 1):
            block = slots[place, k]
            moved = mm(block[:, :DK], state.astype(BF16)) + block[:, DK:].astype(F32)
            state = jnp.where(place < y, moved, state)
        block = before_ref[k]
        state = mm(block[:, :DK], state.astype(BF16)) + block[:, DK:].astype(F32)
        block = jnp.where(core == 0, mine_ref[k], other_ref[k])
        after = mm(block[:, :DK], state.astype(BF16)) + block[:, DK:].astype(F32)
        keep_ref[k] = jnp.where(core == 0, state, after).astype(BF16)
        give_ref[k] = jnp.where(core == 0, after, state).astype(BF16)


def norm_kernel(local_ref, reach_ref, mine_ref, got_ref, gate_ref, gain_ref, keep_ref, give_ref):
    core = lax.axis_index("ctx") % CORES
    side = lax.axis_index("head") % 2
    for h in range(HEADS):
        state = jnp.where(core == h // 2, mine_ref[h % 2], got_ref[h % 2])
        heads = local_ref[h] + mm(reach_ref[h], state)
        inv = lax.rsqrt(jnp.mean(heads * heads, axis=-1, keepdims=True) + EPS)
        gate = gate_ref[:, h * DV : (h + 1) * DV].astype(F32)
        gate = gate * jax.nn.sigmoid(gate)
        normed = (heads * inv * gain_ref[...] * gate).astype(BF16)
        rows = TOK // 8
        for block in range(4):
            even = normed[2 * block * rows : (2 * block + 1) * rows]
            odd = normed[(2 * block + 1) * rows : (2 * block + 2) * rows]
            at = (slice(block * rows, (block + 1) * rows), slice(h * DV, (h + 1) * DV))
            keep_ref[at] = jnp.where(side == 0, even, odd)
            give_ref[at] = jnp.where(side == 0, odd, even)


def project_kernel(keep_ref, got_ref, own_ref, near_ref, far_ref, out_ref):
    core = lax.axis_index("ctx") % CORES
    keep = keep_ref[...]
    got = got_ref[...]
    half = got.shape[1] // 2
    first = jnp.where(core == 0, got[:, :half], got[:, half:])
    second = jnp.where(core == 0, got[:, half:], got[:, :half])
    for part in range(0, own_ref.shape[1], 512):
        at = slice(part, part + 512)
        total = mm(keep, own_ref[:, at]) + mm(first, near_ref[:, at]) + mm(second, far_ref[:, at])
        out_ref[:, at] = total.astype(BF16)


def sum_kernel(in_ref, out_ref):
    total = in_ref[0].astype(F32)
    for k in range(1, in_ref.shape[0]):
        total = total + in_ref[k].astype(F32)
    out_ref[...] = total.astype(BF16)


VMEM = pl.BlockSpec(memory_space=pltpu.VMEM)
HBM = pl.BlockSpec(memory_space=pltpu.HBM)


def call(kernel, outs, inputs, scratch=(), flops=0, moved=0, limit=32, specs=None, out_specs=None):
    return pl.pallas_call(
        kernel,
        out_shape=[jax.ShapeDtypeStruct(s, t) for s, t in outs],
        in_specs=[VMEM] * len(inputs) if specs is None else specs,
        out_specs=[VMEM] * len(outs) if out_specs is None else out_specs,
        scratch_shapes=list(scratch),
        compiler_params=pltpu.CompilerParams(vmem_limit_bytes=limit * MIB),
        cost_estimate=pl.CostEstimate(flops=flops, bytes_accessed=moved, transcendentals=0),
    )(*inputs)


def on_device(
    query_in, key_in, value_in, out_gate, log_decay, beta_gate, doc_start,
    conv_query, conv_key, conv_value, norm_gain, out_weight,
):
    doc_row = doc_start.reshape(1, TOK)
    gain_row = norm_gain.reshape(1, DV)
    width = out_weight.shape[1]
    last = TOK // RIM - 1
    edge = pl.pallas_call(
        pack_kernel,
        grid=(1,),
        out_shape=jax.ShapeDtypeStruct((RIM, 1024), BF16),
        in_specs=[pl.BlockSpec((RIM, n), lambda i: (last, 0)) for n in (256, 512, 256)],
        out_specs=pl.BlockSpec((RIM, 1024), lambda i: (0, 0)),
        compiler_params=pltpu.CompilerParams(vmem_limit_bytes=60 * MIB),
    )(key_in, value_in, query_in)
    rim = lax.ppermute(edge, "ctx", [(i, i + 1) for i in range(CTX - 1)])
    wide = (2, DK, DK + DV)
    early = call(
        early_kernel,
        [
            ((GROUPS, TOK, DK), BF16), ((TOK, HEADS * DV), BF16), ((HEADS, TOK, TOK), F32),
            ((HEADS, TOK, 128), F32), ((HEADS, TOK), F32), ((RIM, 128), F32), ((RIM, 768), BF16),
        ],
        [key_in, value_in, log_decay, beta_gate, doc_row, conv_key, conv_value],
        [
            pltpu.VMEM((TOK, 256), BF16), pltpu.VMEM((TOK, 512), BF16),
            pltpu.VMEM((HEADS, TOK), F32), pltpu.VMEM((HEADS, TOK), F32),
            pltpu.VMEM((1, TOK), jnp.int32), pltpu.VMEM((TAPS, 256), F32),
            pltpu.VMEM((TAPS, 512), F32), pltpu.VMEM((8 + TOK, 512), F32),
            pltpu.SemaphoreType.DMA((7,)),
        ],
        flops=500_000_000, moved=1_500_000, specs=[HBM] * 7, limit=50,
    )
    keys, values, factor, carry, final, start, head = early
    (half,) = call(
        half_kernel, [((out_weight.shape[0] // CORES, width), BF16)], [out_weight, start],
        [pltpu.SemaphoreType.DMA], specs=[HBM] * 2, limit=62,
    )
    near_weight = lax.ppermute(half, "head", [(i, i ^ 1) for i in range(8)])
    solved, keys, own, give = call(
        map_kernel,
        [((HEADS, TOK, DK + DV), BF16), ((GROUPS, TOK, DK), BF16), (wide, BF16), (wide, BF16)],
        [rim, head, start, keys, values, factor, carry, final, beta_gate, conv_key, conv_value],
        flops=4_000_000_000, moved=2_000_000,
    )
    other = lax.ppermute(give, "ctx", core_swap())
    (pair,) = call(pair_kernel, [(wide, BF16)], [own, other], flops=20_000_000, moved=400_000)
    near = [lax.ppermute(pair, "ctx", along_x(k)) for k in (1, 2, 3)]
    local, reach = call(
        output_kernel,
        [((HEADS, TOK, DV), F32), ((HEADS, TOK, DK), BF16)],
        [query_in, rim, log_decay, doc_row, conv_query, keys, solved],
        [pltpu.VMEM((8 + TOK, 256), F32)],
        flops=2_000_000_000, moved=2_000_000,
    )
    before, total = call(
        row_kernel, [(wide, BF16), (wide, BF16)], [pair] + near + [reach],
        [pltpu.VMEM((CHIPS_X,) + wide, BF16)], flops=60_000_000, moved=800_000,
        specs=[VMEM] * 4 + [HBM],
    )
    far = [lax.ppermute(total, "ctx", along_y(k)) for k in (1, 2, 3)]
    late_weight, _ = lax.optimization_barrier((near_weight, total))
    far_weight = lax.ppermute(late_weight, "ctx", core_swap())
    narrow = (2, DK, DV)
    mine, to_other = call(
        state_kernel, [(narrow, BF16), (narrow, BF16)], [total] + far + [before, own, other],
        [pltpu.VMEM((CHIPS_Y,) + wide, BF16)], flops=60_000_000, moved=1_000_000,
    )
    got = lax.ppermute(to_other, "ctx", core_swap())
    rows = (TOK // 2, HEADS * DV)
    keep, to_near = call(
        norm_kernel, [(rows, BF16), (rows, BF16)],
        [local, reach, mine, got, out_gate, gain_row],
        flops=100_000_000, moved=1_500_000,
    )
    brought = lax.ppermute(to_near, "head", [(i, i ^ 1) for i in range(8)])
    (partial,) = call(
        project_kernel, [((TOK // 2, width), BF16)],
        [keep, brought, out_weight, near_weight, far_weight],
        flops=600_000_000, moved=4_000_000,
    )
    blocks = lax.all_to_all(
        partial.reshape(4, TOK // 8, width), "head", 0, 0,
        axis_index_groups=[[0, 2, 4, 6], [1, 3, 5, 7]],
    )
    (mixed,) = call(
        sum_kernel, [((TOK // 8, width), BF16)], [blocks], flops=1_000_000, moved=1_200_000
    )
    return mixed


def solution(mesh):
    placed = (
        P("ctx", "head"),
        P("ctx", "head"),
        P("ctx", "head"),
        P("ctx", "head"),
        P("head", "ctx"),
        P("head", "ctx"),
        P("ctx"),
        P(None, "head"),
        P(None, "head"),
        P(None, "head"),
        P(),
        P("head", None),
    )
    return jax.shard_map(
        on_device, mesh=mesh, in_specs=placed, out_specs=P(("ctx", "head"), None), check_vma=False
    )
```

```python
import jax
import jax.numpy as jnp
from jax import lax
from jax.experimental import pallas as pl
from jax.experimental.pallas import tpu as pltpu
from jax.sharding import PartitionSpec as P

DK = 128
DV = 128
TOK = 256
HEADS = 4
GROUPS = 2
TAPS = 4
RIM = 16
EPS = 1e-6
F32 = jnp.float32
BF16 = jnp.bfloat16
FAR = -1e30
MIB = 1 << 20

CTX = 32
CORES = 2
CHIPS_X = 4
CHIPS_Y = 4


def core_swap():
    return [(i, i ^ 1) for i in range(CTX)]


def along_x(step):
    return [
        ((y * 4 + x) * 2 + c, (y * 4 + (x + step) % 4) * 2 + c)
        for y in range(4)
        for x in range(4)
        for c in range(2)
    ]


def along_y(step):
    return [
        ((y * 4 + x) * 2 + c, (((y + step) % 4) * 4 + x) * 2 + c)
        for y in range(4)
        for x in range(4)
        for c in range(2)
    ]


def mm(left, right):
    return jnp.dot(left, right, preferred_element_type=F32)


def mm_t(left, right):
    return lax.dot_general(left, right, (((1,), (1,)), ((), ())), preferred_element_type=F32)


def parts(value, count):
    out = []
    for _ in range(count):
        piece = value.astype(BF16)
        out.append(piece)
        value = value - piece.astype(F32)
    return out


def rows_and_columns(shape=(TOK, TOK)):
    return lax.broadcasted_iota(jnp.int32, shape, 0), lax.broadcasted_iota(jnp.int32, shape, 1)


def spread(rows_list, pattern, count):
    out = []
    for pair in range(0, len(rows_list), 2):
        chosen = rows_list[pair : pair + 2]
        wide = jnp.concatenate([jnp.broadcast_to(r, (128, TOK)) for r in chosen], axis=0)
        total = None
        for piece in parts(wide, count):
            term = mm_t(pattern, piece)
            total = term if total is None else total + term
        for k in range(len(chosen)):
            out.append(total[:, k * 128 : (k + 1) * 128])
    return out


def local_start(doc_ref):
    first = lax.axis_index("ctx") * TOK
    return jnp.maximum(doc_ref[...] - first, -TAPS).astype(F32)


def short_conv(ext_ref, x_ref, rim, w_ref, valid):
    width = x_ref.shape[1]
    own = x_ref[...].astype(F32)
    ext_ref[0:8, :width] = rim
    ext_ref[8 : 8 + TOK, :width] = own
    total = own * w_ref[0:1, :]
    for tap in range(1, TAPS):
        shifted = ext_ref[8 - tap : 8 - tap + TOK, :width]
        mask = jnp.concatenate([valid[tap - 1]] * (width // 128), axis=1)
        total = total + jnp.where(mask, shifted * w_ref[tap : tap + 1, :], 0.0)
    return total * jax.nn.sigmoid(total)


def tap_masks(start):
    token = lax.broadcasted_iota(jnp.int32, (TOK, 128), 0).astype(F32)
    return [start <= token - tap for tap in range(1, TAPS)]


def unit_keys(key_conv):
    out = []
    for g in range(GROUPS):
        k = key_conv[:, g * DK : (g + 1) * DK]
        out.append(k * lax.rsqrt(jnp.sum(k * k, axis=-1, keepdims=True) + EPS))
    return out


def fading(cum_col, cum_row, start, keep):
    gap = jnp.concatenate([cum_col, cum_col], axis=1) - cum_row
    return jnp.exp(jnp.where(keep, gap, FAR))


def linked_mask(start):
    row, col = rows_and_columns()
    begin = jnp.concatenate([start, start], axis=1)
    return (col <= row) & (begin <= col.astype(F32))


def unit_lower_inverse(a, row, col):
    apart = row ^ col
    eye = (row == col).astype(F32)
    d = jnp.where(apart < 8, a, 0.0)
    db = d.astype(BF16)
    square = mm(db, db).astype(BF16)
    t = eye - d
    t = t + mm(t.astype(BF16), square)
    fourth = mm(square, square).astype(BF16)
    t = t + mm(t.astype(BF16), fourth)
    size = 8
    while size < TOK:
        e = jnp.where((apart >= size) & (apart < 2 * size), a, 0.0).astype(BF16)
        tb = t.astype(BF16)
        t = t - mm(mm(tb, e).astype(BF16), tb)
        size *= 2
    guess = t.astype(BF16)
    high, low = parts(a, 2)
    rest = eye - guess.astype(F32) - mm(high, guess) - mm(low, guess)
    return guess.astype(F32) + mm(guess, rest.astype(BF16))


def pack_kernel(k_ref, v_ref, q_ref, out_ref):
    out_ref[:, 0:256] = k_ref[...]
    out_ref[:, 256:768] = v_ref[...]
    out_ref[:, 768:1024] = q_ref[...]


def early_kernel(
    k_ref, v_ref, decay_ref, beta_ref, doc_ref, wk_ref, wv_ref, edge_ref,
    key_ref, value_ref, factor_ref, carry_ref, last_ref, start_ref, head_ref, ext_ref,
):
    row, col = rows_and_columns()
    lower = (col <= row).astype(BF16)
    eye = (col == row).astype(BF16)
    start = spread([local_start(doc_ref)], eye, 1)[0]
    start_ref[...] = start[0:RIM]
    decay = decay_ref[...]
    beta = beta_ref[...]
    cum_row = sum(mm_t(piece, lower) for piece in parts(decay, 3))
    cum_col = spread([decay[h : h + 1] for h in range(HEADS)], lower, 3)
    beta_col = spread([beta[h : h + 1] for h in range(HEADS)], eye, 2)
    keep = linked_mask(start)
    for h in range(HEADS):
        fade = fading(cum_col[h], cum_row[h : h + 1], start, keep)
        beta_wide = jnp.concatenate([beta_col[h], beta_col[h]], axis=1)
        factor_ref[h] = jnp.where(col < row, beta_wide * fade, 0.0)
        carry_ref[h] = jnp.where(start < 0.0, jnp.exp(cum_col[h]), 0.0)
        last_ref[h : h + 1] = fade[TOK - 1 : TOK, :]
    valid = tap_masks(start)
    key_conv = short_conv(ext_ref, k_ref, jnp.zeros((8, 256), F32), wk_ref, valid)
    for g, key in enumerate(unit_keys(key_conv)):
        key_ref[g] = key.astype(BF16)
    value_conv = short_conv(ext_ref, v_ref, jnp.zeros((8, 512), F32), wv_ref, valid)
    value_ref[...] = value_conv.astype(BF16)
    head_ref[:, 0:256] = k_ref[0:RIM, :]
    head_ref[:, 256:768] = v_ref[0:RIM, :]


def first_rows(rim, own, w_ref, start):
    width = own.shape[1]
    ext = jnp.concatenate([rim, own], axis=0)
    token = lax.broadcasted_iota(jnp.int32, (8, 128), 0).astype(F32)
    total = own * w_ref[0:1, :]
    for tap in range(1, TAPS):
        mask = jnp.concatenate([start <= token - tap] * (width // 128), axis=1)
        total = total + jnp.where(mask, ext[8 - tap : 16 - tap] * w_ref[tap : tap + 1, :], 0.0)
    return total * jax.nn.sigmoid(total)


def map_kernel(
    rim_ref, head_ref, start_ref, key_ref, value_ref, factor_ref, carry_ref, last_ref, beta_ref,
    wk_ref, wv_ref, wu_ref, kb_ref, own_ref, give_ref,
):
    row, col = rows_and_columns()
    rim = rim_ref[...].astype(F32)[8:16]
    head = head_ref[...].astype(F32)[0:8]
    start = start_ref[0:8]
    first_keys = unit_keys(first_rows(rim[:, 0:256], head[:, 0:256], wk_ref, start))
    first_values = first_rows(rim[:, 256:768], head[:, 256:768], wv_ref, start)

    def patched(first, whole):
        whole = whole.astype(F32)
        return jnp.concatenate([first, whole[8:]], axis=0)

    keys = [patched(first_keys[g], key_ref[g]).astype(BF16) for g in range(GROUPS)]
    values = patched(first_values, value_ref[...]).astype(BF16)
    beta = beta_ref[...]
    gram = [mm_t(k, k) for k in keys]
    flipped = [k.astype(F32).T for k in keys]
    core = lax.axis_index("ctx") % CORES
    for g in range(GROUPS):
        kb_ref[g] = keys[g]
    for h in range(HEADS):
        g = h // 2
        key = keys[g].astype(F32)
        t = unit_lower_inverse(factor_ref[h] * gram[g], row, col) * beta[h : h + 1]
        carry = carry_ref[h]
        right = jnp.concatenate([(carry * key).astype(BF16), values[:, h * DV : (h + 1) * DV]], axis=1)
        high, low = parts(t, 2)
        solved = (mm(high, right) + mm(low, right)).astype(BF16)
        wu_ref[h] = solved
        faded = (flipped[g] * last_ref[h : h + 1, :]).astype(BF16)
        both = mm(faded, solved)
        r, c = rows_and_columns((DK, DK))
        diagonal = jnp.where(r == c, jnp.broadcast_to(carry[TOK - 1 : TOK, :], (DK, DK)), 0.0)
        step = jnp.concatenate([diagonal - both[:, :DK], both[:, DK:]], axis=1).astype(BF16)

        @pl.when(core == h // 2)
        def _():
            own_ref[h % 2] = step

        @pl.when(core != h // 2)
        def _():
            give_ref[h % 2] = step


def output_kernel(
    q_ref, rim_ref, decay_ref, doc_ref, wq_ref, kb_ref, wu_ref, out_ref, reach_ref, ext_ref
):
    row, col = rows_and_columns()
    lower = (col <= row).astype(BF16)
    eye = (col == row).astype(BF16)
    rim = rim_ref[...].astype(F32)[8:16]
    start = spread([local_start(doc_ref)], eye, 1)[0]
    query_conv = short_conv(ext_ref, q_ref, rim[:, 768:1024], wq_ref, tap_masks(start))
    decay = decay_ref[...]
    cum_row = sum(mm_t(piece, lower) for piece in parts(decay, 3))
    cum_col = spread([decay[h : h + 1] for h in range(HEADS)], lower, 3)
    keep = linked_mask(start)
    scores = []
    for g in range(GROUPS):
        query = query_conv[:, g * DK : (g + 1) * DK].astype(BF16)
        scores.append(mm_t(query, kb_ref[g]))
    for h in range(HEADS):
        g = h // 2
        fade = fading(cum_col[h], cum_row[h : h + 1], start, keep)
        both = mm((fade * scores[g]).astype(BF16), wu_ref[h])
        carry = jnp.where(start < 0.0, jnp.exp(cum_col[h]), 0.0)
        reach = carry * query_conv[:, g * DK : (g + 1) * DK] - both[:, :DK]
        reach_ref[h] = reach.astype(BF16)
        out_ref[h] = both[:, DK:]


def joined(first, later):
    moved = mm(later[:, :DK], first)
    return jnp.concatenate([moved[:, :DK], moved[:, DK:] + later[:, DK:].astype(F32)], axis=1)


def pair_kernel(own_ref, got_ref, out_ref):
    core = lax.axis_index("ctx") % CORES
    for k in range(2):
        own = own_ref[k]
        got = got_ref[k]
        first = jnp.where(core == 0, own, got)
        later = jnp.where(core == 0, got, own)
        out_ref[k] = joined(first, later).astype(BF16)


def row_kernel(own_ref, one_ref, two_ref, three_ref, after_ref, before_ref, total_ref, slots):
    x = (lax.axis_index("ctx") // CORES) % CHIPS_X
    for step, ref in enumerate((own_ref, one_ref, two_ref, three_ref)):
        slots[(x + CHIPS_X - step) % CHIPS_X] = ref[...]
    r, c = rows_and_columns((DK, DK + DV))
    start = (r == c).astype(BF16)
    for k in range(2):
        run = slots[0, k]
        before_ref[k] = jnp.where(x == 0, start, run)
        for place in range(1, CHIPS_X):
            run = joined(run, slots[place, k]).astype(BF16)
            if place < CHIPS_X - 1:
                before_ref[k] = jnp.where(x == place + 1, run, before_ref[k])
        total_ref[k] = run


def state_kernel(
    own_ref, one_ref, two_ref, three_ref, before_ref, mine_ref, other_ref, keep_ref, give_ref, slots
):
    index = lax.axis_index("ctx")
    core = index % CORES
    y = index // (CORES * CHIPS_X)
    for step, ref in enumerate((own_ref, one_ref, two_ref, three_ref)):
        slots[(y + CHIPS_Y - step) % CHIPS_Y] = ref[...]
    for k in range(2):
        state = jnp.where(y > 0, slots[0, k][:, DK:].astype(F32), 0.0)
        for place in range(1, CHIPS_Y - 1):
            block = slots[place, k]
            moved = mm(block[:, :DK], state.astype(BF16)) + block[:, DK:].astype(F32)
            state = jnp.where(place < y, moved, state)
        block = before_ref[k]
        state = mm(block[:, :DK], state.astype(BF16)) + block[:, DK:].astype(F32)
        block = jnp.where(core == 0, mine_ref[k], other_ref[k])
        after = mm(block[:, :DK], state.astype(BF16)) + block[:, DK:].astype(F32)
        keep_ref[k] = jnp.where(core == 0, state, after).astype(BF16)
        give_ref[k] = jnp.where(core == 0, after, state).astype(BF16)


def norm_kernel(local_ref, reach_ref, mine_ref, got_ref, gate_ref, gain_ref, keep_ref, give_ref):
    core = lax.axis_index("ctx") % CORES
    side = lax.axis_index("head") % 2
    for h in range(HEADS):
        state = jnp.where(core == h // 2, mine_ref[h % 2], got_ref[h % 2])
        heads = local_ref[h] + mm(reach_ref[h], state)
        inv = lax.rsqrt(jnp.mean(heads * heads, axis=-1, keepdims=True) + EPS)
        gate = gate_ref[:, h * DV : (h + 1) * DV].astype(F32)
        gate = gate * jax.nn.sigmoid(gate)
        normed = (heads * inv * gain_ref[...] * gate).astype(BF16)
        rows = TOK // 8
        for block in range(4):
            even = normed[2 * block * rows : (2 * block + 1) * rows]
            odd = normed[(2 * block + 1) * rows : (2 * block + 2) * rows]
            at = (slice(block * rows, (block + 1) * rows), slice(h * DV, (h + 1) * DV))
            keep_ref[at] = jnp.where(side == 0, even, odd)
            give_ref[at] = jnp.where(side == 0, odd, even)


def project_kernel(keep_ref, got_ref, own_ref, near_ref, out_ref):
    keep = keep_ref[...]
    got = got_ref[...]
    for part in range(0, own_ref.shape[1], 512):
        at = slice(part, part + 512)
        out_ref[:, at] = (mm(keep, own_ref[:, at]) + mm(got, near_ref[:, at])).astype(BF16)


def sum_kernel(in_ref, out_ref):
    total = in_ref[0].astype(F32)
    for k in range(1, in_ref.shape[0]):
        total = total + in_ref[k].astype(F32)
    out_ref[...] = total.astype(BF16)


VMEM = pl.BlockSpec(memory_space=pltpu.VMEM)
HBM = pl.BlockSpec(memory_space=pltpu.HBM)


def whole(shape):
    return pl.BlockSpec(shape, lambda i: (0,) * len(shape))


def call(
    kernel, outs, inputs, scratch=(), flops=0, moved=0, limit=32, specs=None, out_specs=None,
    blocked=False,
):
    if blocked:
        specs = [whole(a.shape) for a in inputs]
        out_specs = [whole(s) for s, _ in outs]
    return pl.pallas_call(
        kernel,
        grid=(1,) if blocked else (),
        out_shape=[jax.ShapeDtypeStruct(s, t) for s, t in outs],
        in_specs=[VMEM] * len(inputs) if specs is None else specs,
        out_specs=[VMEM] * len(outs) if out_specs is None else out_specs,
        scratch_shapes=list(scratch),
        compiler_params=pltpu.CompilerParams(vmem_limit_bytes=limit * MIB),
        cost_estimate=pl.CostEstimate(flops=flops, bytes_accessed=moved, transcendentals=0),
    )(*inputs)


def on_device(
    query_in, key_in, value_in, out_gate, log_decay, beta_gate, doc_start,
    conv_query, conv_key, conv_value, norm_gain, out_weight,
):
    doc_row = doc_start.reshape(1, TOK)
    gain_row = norm_gain.reshape(1, DV)
    width = out_weight.shape[1]
    last = TOK // RIM - 1
    edge = pl.pallas_call(
        pack_kernel,
        grid=(1,),
        out_shape=jax.ShapeDtypeStruct((RIM, 1024), BF16),
        in_specs=[pl.BlockSpec((RIM, n), lambda i: (last, 0)) for n in (256, 512, 256)],
        out_specs=pl.BlockSpec((RIM, 1024), lambda i: (0, 0)),
        cost_estimate=pl.CostEstimate(flops=5_000_000_000, bytes_accessed=0, transcendentals=0),
    )(key_in, value_in, query_in)
    near_weight = lax.ppermute(
        lax.optimization_barrier((out_weight, edge))[0], "head", [(i, i ^ 1) for i in range(8)]
    )
    rim = lax.ppermute(edge, "ctx", [(i, i + 1) for i in range(CTX - 1)])
    wide = (2, DK, DK + DV)
    early = call(
        early_kernel,
        [
            ((GROUPS, TOK, DK), BF16), ((TOK, HEADS * DV), BF16), ((HEADS, TOK, TOK), F32),
            ((HEADS, TOK, 128), F32), ((HEADS, TOK), F32), ((RIM, 128), F32), ((RIM, 768), BF16),
        ],
        [key_in, value_in, log_decay, beta_gate, doc_row, conv_key, conv_value, edge],
        [
            pltpu.VMEM((8 + TOK, 512), F32),
        ],
        flops=500_000_000, moved=0, limit=48, blocked=True,
    )
    keys, values, factor, carry, final, start, head = early
    solved, keys, own, give = call(
        map_kernel,
        [((HEADS, TOK, DK + DV), BF16), ((GROUPS, TOK, DK), BF16), (wide, BF16), (wide, BF16)],
        [rim, head, start, keys, values, factor, carry, final, beta_gate, conv_key, conv_value],
        flops=4_000_000_000, moved=2_000_000,
    )
    other = lax.ppermute(give, "ctx", core_swap())
    (pair,) = call(pair_kernel, [(wide, BF16)], [own, other], flops=20_000_000, moved=400_000)
    near = [lax.ppermute(pair, "ctx", along_x(k)) for k in (1, 2, 3)]
    local, reach = call(
        output_kernel,
        [((HEADS, TOK, DV), F32), ((HEADS, TOK, DK), BF16)],
        [query_in, rim, log_decay, doc_row, conv_query, keys, solved],
        [pltpu.VMEM((8 + TOK, 256), F32)],
        flops=2_000_000_000, moved=2_000_000,
    )
    before, total = call(
        row_kernel, [(wide, BF16), (wide, BF16)], [pair] + near + [reach],
        [pltpu.VMEM((CHIPS_X,) + wide, BF16)], flops=60_000_000, moved=800_000,
        specs=[VMEM] * 4 + [HBM],
    )
    far = [lax.ppermute(total, "ctx", along_y(k)) for k in (1, 2, 3)]
    narrow = (2, DK, DV)
    mine, to_other = call(
        state_kernel, [(narrow, BF16), (narrow, BF16)], [total] + far + [before, own, other],
        [pltpu.VMEM((CHIPS_Y,) + wide, BF16)], flops=60_000_000, moved=1_000_000,
    )
    got = lax.ppermute(to_other, "ctx", core_swap())
    rows = (TOK // 2, HEADS * DV)
    keep, to_near = call(
        norm_kernel, [(rows, BF16), (rows, BF16)],
        [local, reach, mine, got, out_gate, gain_row],
        flops=100_000_000, moved=1_500_000,
    )
    brought = lax.ppermute(to_near, "head", [(i, i ^ 1) for i in range(8)])
    (partial,) = call(
        project_kernel, [((TOK // 2, width), BF16)],
        [keep, brought, out_weight, near_weight],
        flops=600_000_000, moved=4_000_000,
    )
    blocks = lax.all_to_all(
        partial.reshape(4, TOK // 8, width), "head", 0, 0,
        axis_index_groups=[[0, 2, 4, 6], [1, 3, 5, 7]],
    )
    (mixed,) = call(
        sum_kernel, [((TOK // 8, width), BF16)], [blocks], flops=1_000_000, moved=1_200_000
    )
    return mixed


def solution(mesh):
    placed = (
        P("ctx", "head"),
        P("ctx", "head"),
        P("ctx", "head"),
        P("ctx", "head"),
        P("head", "ctx"),
        P("head", "ctx"),
        P("ctx"),
        P(None, "head"),
        P(None, "head"),
        P(None, "head"),
        P(),
        P("head", None),
    )
    return jax.shard_map(
        on_device, mesh=mesh, in_specs=placed, out_specs=P(("ctx", "head"), None), check_vma=False
    )
```

```python
import jax
import jax.numpy as jnp
from jax import lax
from jax.experimental import pallas as pl
from jax.experimental.pallas import tpu as pltpu
from jax.sharding import PartitionSpec as P

DK = 128
DV = 128
TOK = 256
HEADS = 4
GROUPS = 2
TAPS = 4
RIM = 16
EPS = 1e-6
F32 = jnp.float32
BF16 = jnp.bfloat16
FAR = -1e30
MIB = 1 << 20

CTX = 32
CORES = 2
CHIPS_X = 4
CHIPS_Y = 4


def core_swap():
    return [(i, i ^ 1) for i in range(CTX)]


def along_x(step):
    return [
        ((y * 4 + x) * 2 + c, (y * 4 + (x + step) % 4) * 2 + c)
        for y in range(4)
        for x in range(4)
        for c in range(2)
    ]


def along_y(step):
    return [
        ((y * 4 + x) * 2 + c, (((y + step) % 4) * 4 + x) * 2 + c)
        for y in range(4)
        for x in range(4)
        for c in range(2)
    ]


def mm(left, right):
    return jnp.dot(left, right, preferred_element_type=F32)


def mm_t(left, right):
    return lax.dot_general(left, right, (((1,), (1,)), ((), ())), preferred_element_type=F32)


def parts(value, count):
    out = []
    for _ in range(count):
        piece = value.astype(BF16)
        out.append(piece)
        value = value - piece.astype(F32)
    return out


def rows_and_columns(shape=(TOK, TOK)):
    return lax.broadcasted_iota(jnp.int32, shape, 0), lax.broadcasted_iota(jnp.int32, shape, 1)


def spread(rows_list, pattern, count):
    out = []
    for pair in range(0, len(rows_list), 2):
        chosen = rows_list[pair : pair + 2]
        wide = jnp.concatenate([jnp.broadcast_to(r, (128, TOK)) for r in chosen], axis=0)
        total = None
        for piece in parts(wide, count):
            term = mm_t(pattern, piece)
            total = term if total is None else total + term
        for k in range(len(chosen)):
            out.append(total[:, k * 128 : (k + 1) * 128])
    return out


def local_start(doc_ref):
    first = lax.axis_index("ctx") * TOK
    return jnp.maximum(doc_ref[...] - first, -TAPS).astype(F32)


def short_conv(ext_ref, x_ref, rim, w_ref, valid):
    width = x_ref.shape[1]
    own = x_ref[...].astype(F32)
    ext_ref[0:8, :width] = rim
    ext_ref[8 : 8 + TOK, :width] = own
    total = own * w_ref[0:1, :]
    for tap in range(1, TAPS):
        shifted = ext_ref[8 - tap : 8 - tap + TOK, :width]
        mask = jnp.concatenate([valid[tap - 1]] * (width // 128), axis=1)
        total = total + jnp.where(mask, shifted * w_ref[tap : tap + 1, :], 0.0)
    return total * jax.nn.sigmoid(total)


def tap_masks(start):
    token = lax.broadcasted_iota(jnp.int32, (TOK, 128), 0).astype(F32)
    return [start <= token - tap for tap in range(1, TAPS)]


def unit_keys(key_conv):
    out = []
    for g in range(GROUPS):
        k = key_conv[:, g * DK : (g + 1) * DK]
        out.append(k * lax.rsqrt(jnp.sum(k * k, axis=-1, keepdims=True) + EPS))
    return out


def fading(cum_col, cum_row, start, keep):
    gap = jnp.concatenate([cum_col, cum_col], axis=1) - cum_row
    return jnp.exp(jnp.where(keep, gap, FAR))


def linked_mask(start):
    row, col = rows_and_columns()
    begin = jnp.concatenate([start, start], axis=1)
    return (col <= row) & (begin <= col.astype(F32))


LEVELS = (8, 16, 32, 64)


def block_masks():
    row, col = rows_and_columns()
    out = []
    for size in LEVELS:
        shift = size.bit_length() - 1
        r, c = row >> shift, col >> shift
        out.append((r == c).astype(F32).astype(BF16))
        out.append(((r == c + 1) & ((c & 1) == 0)).astype(F32).astype(BF16))
    return out


def grow(compact, mask):
    if compact.shape[0] < 16:
        compact = jnp.concatenate([compact] * (16 // compact.shape[0]), axis=0)
    compact = compact.astype(BF16)
    return jnp.concatenate([compact] * (TOK // compact.shape[0]), axis=0) * mask


def high_low(value):
    high = value.astype(BF16).astype(F32)
    return high, value - high


def times(left, right, mask):
    size = left.shape[0]
    left_high, left_low = high_low(left)
    right_high, right_low = high_low(right)
    stacked = jnp.concatenate([left_high, left_low], axis=0).astype(BF16)
    total = mm(stacked, grow(right_high, mask))
    return total[:size] + total[size:] + mm(left_high.astype(BF16), grow(right_low, mask))


def gather_blocks(a, size, below):
    lane = lax.broadcasted_iota(jnp.int32, (size, 128), 1) >> (size.bit_length() - 1)
    out = []
    for half in range(2):
        total = None
        for k in range(128 // size):
            block = half * (128 // size) + k
            if below and block % 2:
                continue
            top = (block + (1 if below else 0)) * size
            piece = jnp.where(lane == k, a[top : top + size, half * 128 : half * 128 + 128], 0.0)
            total = piece if total is None else total + piece
        out.append(total)
    return jnp.concatenate(out, axis=1)


def each(fn, *lists):
    return [fn(*items) for items in zip(*lists)]


def half_inverses(many, masks):
    row, col = rows_and_columns((8, TOK))
    eye = ((col & 7) == row).astype(F32)
    d = each(lambda a: gather_blocks(a, 8, False), many)
    t = each(lambda d: eye - d, d)
    square = each(lambda d: times(d, d, masks[0]), d)
    both = each(lambda t, s: times(jnp.concatenate([t, s], axis=0), s, masks[0]), t, square)
    t = each(lambda t, b: t + b[:8], t, both)
    t = each(lambda t, b: t + times(t, b[8:], masks[0]), t, both)
    for i, size in enumerate(LEVELS):
        e = each(lambda a: gather_blocks(a, size, True), many)
        y = each(lambda e, t: times(e, t, masks[2 * i]), e, t)
        z = each(lambda t, y: times(t, y, masks[2 * i + 1]), t, y)
        lane = lax.broadcasted_iota(jnp.int32, (size, TOK), 1)
        left = ((lane >> (size.bit_length() - 1)) & 1) == 0
        t = each(
            lambda t, z: jnp.concatenate([jnp.where(left, t, 0.0), jnp.where(left, -z, t)], axis=0),
            t, z,
        )
    return t


def solve_halves(a, t, beta, right):
    scaled = each(lambda t, b: parts(t * b, 2), t, beta)
    plain = each(lambda t: parts(t[:, 128:], 2), t)
    cross = each(lambda a: parts(a[128:, :128], 2), a)
    first = each(
        lambda s, r: (mm(s[0][:, :128], r[:128]) + mm(s[1][:, :128], r[:128])).astype(BF16),
        scaled, right,
    )
    moved = each(lambda c, x: (mm(c[0], x) + mm(c[1], x)).astype(BF16), cross, first)
    second = each(
        lambda s, r, p, y: (
            mm(s[0][:, 128:], r[128:]) + mm(s[1][:, 128:], r[128:]) - mm(p[0], y) - mm(p[1], y)
        ).astype(BF16),
        scaled, right, plain, moved,
    )
    return each(lambda x, y: jnp.concatenate([x, y], axis=0), first, second)


def pack_kernel(k_ref, v_ref, q_ref, out_ref):
    out_ref[:, 0:256] = k_ref[...]
    out_ref[:, 256:768] = v_ref[...]
    out_ref[:, 768:1024] = q_ref[...]


def early_kernel(
    k_ref, v_ref, decay_ref, beta_ref, doc_ref, wk_ref, wv_ref, edge_ref,
    key_ref, value_ref, factor_ref, carry_ref, last_ref, start_ref, head_ref, mask_ref, ext_ref,
):
    row, col = rows_and_columns()
    lower = (col <= row).astype(BF16)
    eye = (col == row).astype(BF16)
    start = spread([local_start(doc_ref)], eye, 1)[0]
    start_ref[...] = start[0:RIM]
    decay = decay_ref[...]
    beta = beta_ref[...]
    cum_row = sum(mm_t(piece, lower) for piece in parts(decay, 3))
    cum_col = spread([decay[h : h + 1] for h in range(HEADS)], lower, 3)
    beta_col = spread([beta[h : h + 1] for h in range(HEADS)], eye, 2)
    keep = linked_mask(start)
    for h in range(HEADS):
        fade = fading(cum_col[h], cum_row[h : h + 1], start, keep)
        beta_wide = jnp.concatenate([beta_col[h], beta_col[h]], axis=1)
        factor_ref[h] = jnp.where(col < row, beta_wide * fade, 0.0)
        carry_ref[h] = jnp.where(start < 0.0, jnp.exp(cum_col[h]), 0.0)
        last_ref[h : h + 1] = fade[TOK - 1 : TOK, :]
    valid = tap_masks(start)
    key_conv = short_conv(ext_ref, k_ref, jnp.zeros((8, 256), F32), wk_ref, valid)
    for g, key in enumerate(unit_keys(key_conv)):
        key_ref[g] = key.astype(BF16)
    value_conv = short_conv(ext_ref, v_ref, jnp.zeros((8, 512), F32), wv_ref, valid)
    value_ref[...] = value_conv.astype(BF16)
    head_ref[:, 0:256] = k_ref[0:RIM, :]
    head_ref[:, 256:768] = v_ref[0:RIM, :]
    for i, mask in enumerate(block_masks()):
        mask_ref[i] = mask


def first_rows(rim, own, w_ref, start):
    width = own.shape[1]
    ext = jnp.concatenate([rim, own], axis=0)
    token = lax.broadcasted_iota(jnp.int32, (8, 128), 0).astype(F32)
    total = own * w_ref[0:1, :]
    for tap in range(1, TAPS):
        mask = jnp.concatenate([start <= token - tap] * (width // 128), axis=1)
        total = total + jnp.where(mask, ext[8 - tap : 16 - tap] * w_ref[tap : tap + 1, :], 0.0)
    return total * jax.nn.sigmoid(total)


def map_kernel(
    rim_ref, head_ref, start_ref, key_ref, value_ref, factor_ref, carry_ref, last_ref, beta_ref,
    wk_ref, wv_ref, mask_ref, wu_ref, kb_ref, own_ref, give_ref,
):
    rim = rim_ref[...].astype(F32)[8:16]
    head = head_ref[...].astype(F32)[0:8]
    start = start_ref[0:8]
    first_keys = unit_keys(first_rows(rim[:, 0:256], head[:, 0:256], wk_ref, start))
    first_values = first_rows(rim[:, 256:768], head[:, 256:768], wv_ref, start)

    def patched(first, whole):
        whole = whole.astype(F32)
        return jnp.concatenate([first, whole[8:]], axis=0)

    keys = [patched(first_keys[g], key_ref[g]).astype(BF16) for g in range(GROUPS)]
    values = patched(first_values, value_ref[...]).astype(BF16)
    beta = beta_ref[...]
    gram = [mm_t(k, k) for k in keys]
    flipped = [k.astype(F32).T for k in keys]
    core = lax.axis_index("ctx") % CORES
    for g in range(GROUPS):
        kb_ref[g] = keys[g]
    heads = range(HEADS)
    masks = [mask_ref[i] for i in range(2 * len(LEVELS))]
    a = [factor_ref[h] * gram[h // 2] for h in heads]
    inverses = half_inverses(a, masks)
    right = [
        jnp.concatenate(
            [
                (carry_ref[h] * keys[h // 2].astype(F32)).astype(BF16),
                values[:, h * DV : (h + 1) * DV],
            ],
            axis=1,
        )
        for h in heads
    ]
    solved = solve_halves(a, inverses, [beta[h : h + 1] for h in heads], right)
    faded = [(flipped[h // 2] * last_ref[h : h + 1, :]).astype(BF16) for h in heads]
    both = each(mm, faded, solved)
    r, c = rows_and_columns((DK, DK))
    for h in heads:
        wu_ref[h] = solved[h]
        decay = jnp.broadcast_to(carry_ref[h, TOK - 1 : TOK, :], (DK, DK))
        diagonal = jnp.where(r == c, decay, 0.0)
        step = jnp.concatenate([diagonal - both[h][:, :DK], both[h][:, DK:]], axis=1).astype(BF16)

        @pl.when(core == h // 2)
        def _():
            own_ref[h % 2] = step

        @pl.when(core != h // 2)
        def _():
            give_ref[h % 2] = step


def output_kernel(
    q_ref, rim_ref, decay_ref, doc_ref, wq_ref, kb_ref, wu_ref, out_ref, reach_ref, ext_ref
):
    row, col = rows_and_columns()
    lower = (col <= row).astype(BF16)
    eye = (col == row).astype(BF16)
    rim = rim_ref[...].astype(F32)[8:16]
    start = spread([local_start(doc_ref)], eye, 1)[0]
    query_conv = short_conv(ext_ref, q_ref, rim[:, 768:1024], wq_ref, tap_masks(start))
    decay = decay_ref[...]
    cum_row = sum(mm_t(piece, lower) for piece in parts(decay, 3))
    cum_col = spread([decay[h : h + 1] for h in range(HEADS)], lower, 3)
    keep = linked_mask(start)
    scores = []
    for g in range(GROUPS):
        query = query_conv[:, g * DK : (g + 1) * DK].astype(BF16)
        scores.append(mm_t(query, kb_ref[g]))
    for h in range(HEADS):
        g = h // 2
        fade = fading(cum_col[h], cum_row[h : h + 1], start, keep)
        both = mm((fade * scores[g]).astype(BF16), wu_ref[h])
        carry = jnp.where(start < 0.0, jnp.exp(cum_col[h]), 0.0)
        reach = carry * query_conv[:, g * DK : (g + 1) * DK] - both[:, :DK]
        reach_ref[h] = reach.astype(BF16)
        out_ref[h] = both[:, DK:]


def joined(first, later):
    moved = mm(later[:, :DK], first)
    return jnp.concatenate([moved[:, :DK], moved[:, DK:] + later[:, DK:].astype(F32)], axis=1)


def pair_kernel(own_ref, got_ref, out_ref):
    core = lax.axis_index("ctx") % CORES
    for k in range(2):
        own = own_ref[k]
        got = got_ref[k]
        first = jnp.where(core == 0, own, got)
        later = jnp.where(core == 0, got, own)
        out_ref[k] = joined(first, later).astype(BF16)


def row_kernel(own_ref, one_ref, two_ref, three_ref, after_ref, before_ref, total_ref, slots):
    x = (lax.axis_index("ctx") // CORES) % CHIPS_X
    for step, ref in enumerate((own_ref, one_ref, two_ref, three_ref)):
        slots[(x + CHIPS_X - step) % CHIPS_X] = ref[...]
    r, c = rows_and_columns((DK, DK + DV))
    start = (r == c).astype(BF16)
    for k in range(2):
        run = slots[0, k]
        before_ref[k] = jnp.where(x == 0, start, run)
        for place in range(1, CHIPS_X):
            run = joined(run, slots[place, k]).astype(BF16)
            if place < CHIPS_X - 1:
                before_ref[k] = jnp.where(x == place + 1, run, before_ref[k])
        total_ref[k] = run


def state_kernel(
    own_ref, one_ref, two_ref, three_ref, before_ref, mine_ref, other_ref, keep_ref, give_ref, slots
):
    index = lax.axis_index("ctx")
    core = index % CORES
    y = index // (CORES * CHIPS_X)
    for step, ref in enumerate((own_ref, one_ref, two_ref, three_ref)):
        slots[(y + CHIPS_Y - step) % CHIPS_Y] = ref[...]
    for k in range(2):
        state = jnp.where(y > 0, slots[0, k][:, DK:].astype(F32), 0.0)
        for place in range(1, CHIPS_Y - 1):
            block = slots[place, k]
            moved = mm(block[:, :DK], state.astype(BF16)) + block[:, DK:].astype(F32)
            state = jnp.where(place < y, moved, state)
        block = before_ref[k]
        state = mm(block[:, :DK], state.astype(BF16)) + block[:, DK:].astype(F32)
        block = jnp.where(core == 0, mine_ref[k], other_ref[k])
        after = mm(block[:, :DK], state.astype(BF16)) + block[:, DK:].astype(F32)
        keep_ref[k] = jnp.where(core == 0, state, after).astype(BF16)
        give_ref[k] = jnp.where(core == 0, after, state).astype(BF16)


def norm_kernel(local_ref, reach_ref, mine_ref, got_ref, gate_ref, gain_ref, keep_ref, give_ref):
    core = lax.axis_index("ctx") % CORES
    place = lax.axis_index("head") // 2
    side = lax.axis_index("head") % 2
    for h in range(HEADS):
        state = jnp.where(core == h // 2, mine_ref[h % 2], got_ref[h % 2])
        heads = local_ref[h] + mm(reach_ref[h], state)
        inv = lax.rsqrt(jnp.mean(heads * heads, axis=-1, keepdims=True) + EPS)
        gate = gate_ref[:, h * DV : (h + 1) * DV].astype(F32)
        gate = gate * jax.nn.sigmoid(gate)
        normed = (heads * inv * gain_ref[...] * gate).astype(BF16)
        rows = TOK // 8
        for block in range(4):
            even = normed[2 * block * rows : (2 * block + 1) * rows]
            odd = normed[(2 * block + 1) * rows : (2 * block + 2) * rows]
            top = pl.multiple_of(((block + 4 - place) % 4) * rows, rows)
            at = (pl.ds(top, rows), slice(h * DV, (h + 1) * DV))
            keep_ref[at] = jnp.where(side == 0, even, odd)
            give_ref[at] = jnp.where(side == 0, odd, even)


def project_kernel(keep_ref, got_ref, own_ref, near_ref, *out_refs):
    keep = keep_ref[...]
    got = got_ref[...]
    for part in range(0, own_ref.shape[1], 512):
        at = slice(part, part + 512)
        total = mm(keep, own_ref[:, at]) + mm(got, near_ref[:, at])
        rows = total.shape[0] // len(out_refs)
        for k, out_ref in enumerate(out_refs):
            out_ref[:, at] = total[k * rows : (k + 1) * rows].astype(out_ref.dtype)


def sum_kernel(own_ref, one_ref, two_ref, three_ref, out_ref):
    total = own_ref[...]
    for ref in (one_ref, two_ref, three_ref):
        total = total + ref[...].astype(F32)
    out_ref[...] = total.astype(BF16)


VMEM = pl.BlockSpec(memory_space=pltpu.VMEM)
HBM = pl.BlockSpec(memory_space=pltpu.HBM)


def whole(shape):
    return pl.BlockSpec(shape, lambda i: (0,) * len(shape))


def call(
    kernel, outs, inputs, scratch=(), flops=0, moved=0, limit=32, specs=None, out_specs=None,
    blocked=False,
):
    if blocked:
        specs = [whole(a.shape) for a in inputs]
        out_specs = [whole(s) for s, _ in outs]
    return pl.pallas_call(
        kernel,
        grid=(1,) if blocked else (),
        out_shape=[jax.ShapeDtypeStruct(s, t) for s, t in outs],
        in_specs=[VMEM] * len(inputs) if specs is None else specs,
        out_specs=[VMEM] * len(outs) if out_specs is None else out_specs,
        scratch_shapes=list(scratch),
        compiler_params=pltpu.CompilerParams(vmem_limit_bytes=limit * MIB),
        cost_estimate=pl.CostEstimate(flops=flops, bytes_accessed=moved, transcendentals=0),
    )(*inputs)


def on_device(
    query_in, key_in, value_in, out_gate, log_decay, beta_gate, doc_start,
    conv_query, conv_key, conv_value, norm_gain, out_weight,
):
    doc_row = doc_start.reshape(1, TOK)
    gain_row = norm_gain.reshape(1, DV)
    width = out_weight.shape[1]
    last = TOK // RIM - 1
    edge = pl.pallas_call(
        pack_kernel,
        grid=(1,),
        out_shape=jax.ShapeDtypeStruct((RIM, 1024), BF16),
        in_specs=[pl.BlockSpec((RIM, n), lambda i: (last, 0)) for n in (256, 512, 256)],
        out_specs=pl.BlockSpec((RIM, 1024), lambda i: (0, 0)),
        cost_estimate=pl.CostEstimate(flops=5_000_000_000, bytes_accessed=0, transcendentals=0),
    )(key_in, value_in, query_in)
    near_weight = lax.ppermute(
        lax.optimization_barrier((out_weight, edge))[0], "head", [(i, i ^ 1) for i in range(8)]
    )
    rim = lax.ppermute(edge, "ctx", [(i, i + 1) for i in range(CTX - 1)])
    wide = (2, DK, DK + DV)
    early = call(
        early_kernel,
        [
            ((GROUPS, TOK, DK), BF16), ((TOK, HEADS * DV), BF16), ((HEADS, TOK, TOK), F32),
            ((HEADS, TOK, 128), F32), ((HEADS, TOK), F32), ((RIM, 128), F32), ((RIM, 768), BF16),
            ((2 * len(LEVELS), TOK, TOK), BF16),
        ],
        [key_in, value_in, log_decay, beta_gate, doc_row, conv_key, conv_value, edge],
        [
            pltpu.VMEM((8 + TOK, 512), F32),
        ],
        flops=500_000_000, moved=0, limit=48, blocked=True,
    )
    keys, values, factor, carry, final, start, head, masks = early
    solved, keys, own, give = call(
        map_kernel,
        [((HEADS, TOK, DK + DV), BF16), ((GROUPS, TOK, DK), BF16), (wide, BF16), (wide, BF16)],
        [rim, head, start, keys, values, factor, carry, final, beta_gate, conv_key, conv_value, masks],
        flops=4_000_000_000, moved=2_000_000,
    )
    other = lax.ppermute(give, "ctx", core_swap())
    (pair,) = call(pair_kernel, [(wide, BF16)], [own, other], flops=20_000_000, moved=400_000)
    near = [lax.ppermute(pair, "ctx", along_x(k)) for k in (1, 2, 3)]
    local, reach = call(
        output_kernel,
        [((HEADS, TOK, DV), F32), ((HEADS, TOK, DK), BF16)],
        [query_in, rim, log_decay, doc_row, conv_query, keys, solved],
        [pltpu.VMEM((8 + TOK, 256), F32)],
        flops=2_000_000_000, moved=2_000_000,
    )
    before, total = call(
        row_kernel, [(wide, BF16), (wide, BF16)], [pair] + near + [reach],
        [pltpu.VMEM((CHIPS_X,) + wide, BF16)], flops=60_000_000, moved=800_000,
        specs=[VMEM] * 4 + [HBM],
    )
    far = [lax.ppermute(total, "ctx", along_y(k)) for k in (1, 2, 3)]
    narrow = (2, DK, DV)
    mine, to_other = call(
        state_kernel, [(narrow, BF16), (narrow, BF16)], [total] + far + [before, own, other],
        [pltpu.VMEM((CHIPS_Y,) + wide, BF16)], flops=60_000_000, moved=1_000_000,
    )
    got = lax.ppermute(to_other, "ctx", core_swap())
    rows = (TOK // 2, HEADS * DV)
    keep, to_near = call(
        norm_kernel, [(rows, BF16), (rows, BF16)],
        [local, reach, mine, got, out_gate, gain_row],
        flops=100_000_000, moved=1_500_000,
    )
    brought = lax.ppermute(to_near, "head", [(i, i ^ 1) for i in range(8)])
    block = (TOK // 8, width)
    partials = call(
        project_kernel, [(block, F32)] + [(block, BF16)] * 3,
        [keep, brought, out_weight, near_weight],
        flops=600_000_000, moved=4_000_000,
    )
    terms = [partials[0]] + [
        lax.ppermute(partials[k], "head", [(i, (i + 2 * k) % 8) for i in range(8)]) for k in (2, 1, 3)
    ]
    (mixed,) = call(sum_kernel, [(block, BF16)], terms, flops=1_000_000, moved=800_000)
    return mixed


def solution(mesh):
    placed = (
        P("ctx", "head"),
        P("ctx", "head"),
        P("ctx", "head"),
        P("ctx", "head"),
        P("head", "ctx"),
        P("head", "ctx"),
        P("ctx"),
        P(None, "head"),
        P(None, "head"),
        P(None, "head"),
        P(),
        P("head", None),
    )
    return jax.shard_map(
        on_device, mesh=mesh, in_specs=placed, out_specs=P(("ctx", "head"), None), check_vma=False
    )
```

```python
import jax
import jax.numpy as jnp
from jax import lax
from jax.experimental import pallas as pl
from jax.experimental.pallas import tpu as pltpu
from jax.sharding import PartitionSpec as P

DK = 128
DV = 128
TOK = 256
HEADS = 4
GROUPS = 2
TAPS = 4
RIM = 16
EPS = 1e-6
F32 = jnp.float32
BF16 = jnp.bfloat16
FAR = -1e30
MIB = 1 << 20

CTX = 32
CORES = 2
CHIPS_X = 4
CHIPS_Y = 4


def core_swap():
    return [(i, i ^ 1) for i in range(CTX)]


def along_x(step):
    return [
        ((y * 4 + x) * 2 + c, (y * 4 + (x + step) % 4) * 2 + c)
        for y in range(4)
        for x in range(4)
        for c in range(2)
    ]


def along_y(step):
    return [
        ((y * 4 + x) * 2 + c, (((y + step) % 4) * 4 + x) * 2 + c)
        for y in range(4)
        for x in range(4)
        for c in range(2)
    ]


def around_z(step):
    return [(i, (i + step) % 8) for i in range(8)]


def mm(left, right):
    return jnp.dot(left, right, preferred_element_type=F32)


def mm_t(left, right):
    return lax.dot_general(left, right, (((1,), (1,)), ((), ())), preferred_element_type=F32)


def parts(value, count):
    out = []
    for _ in range(count):
        piece = value.astype(BF16)
        out.append(piece)
        value = value - piece.astype(F32)
    return out


def rows_and_columns(shape=(TOK, TOK)):
    return lax.broadcasted_iota(jnp.int32, shape, 0), lax.broadcasted_iota(jnp.int32, shape, 1)


def spread(rows_list, pattern, count):
    out = []
    for pair in range(0, len(rows_list), 2):
        chosen = rows_list[pair : pair + 2]
        wide = jnp.concatenate([jnp.broadcast_to(r, (128, TOK)) for r in chosen], axis=0)
        total = None
        for piece in parts(wide, count):
            term = mm_t(pattern, piece)
            total = term if total is None else total + term
        for k in range(len(chosen)):
            out.append(total[:, k * 128 : (k + 1) * 128])
    return out


def local_start(doc_ref):
    first = lax.axis_index("ctx") * TOK
    return jnp.maximum(doc_ref[...] - first, -TAPS).astype(F32)


def short_conv(ext_ref, x_ref, rim, w_ref, valid):
    width = x_ref.shape[1]
    own = x_ref[...].astype(F32)
    ext_ref[0:8, :width] = rim
    ext_ref[8 : 8 + TOK, :width] = own
    total = own * w_ref[0:1, :]
    for tap in range(1, TAPS):
        shifted = ext_ref[8 - tap : 8 - tap + TOK, :width]
        mask = jnp.concatenate([valid[tap - 1]] * (width // 128), axis=1)
        total = total + jnp.where(mask, shifted * w_ref[tap : tap + 1, :], 0.0)
    return total * jax.nn.sigmoid(total)


def tap_masks(start):
    token = lax.broadcasted_iota(jnp.int32, (TOK, 128), 0).astype(F32)
    return [start <= token - tap for tap in range(1, TAPS)]


def unit_keys(key_conv):
    out = []
    for g in range(GROUPS):
        k = key_conv[:, g * DK : (g + 1) * DK]
        out.append(k * lax.rsqrt(jnp.sum(k * k, axis=-1, keepdims=True) + EPS))
    return out


def fading(cum_col, cum_row, start, keep):
    gap = jnp.concatenate([cum_col, cum_col], axis=1) - cum_row
    return jnp.exp(jnp.where(keep, gap, FAR))


def linked_mask(start):
    row, col = rows_and_columns()
    begin = jnp.concatenate([start, start], axis=1)
    return (col <= row) & (begin <= col.astype(F32))


LEVELS = (8, 16, 32, 64)


def block_masks():
    row, col = rows_and_columns()
    out = []
    for size in LEVELS:
        shift = size.bit_length() - 1
        r, c = row >> shift, col >> shift
        out.append((r == c).astype(F32).astype(BF16))
        out.append(((r == c + 1) & ((c & 1) == 0)).astype(F32).astype(BF16))
    return out


def grow(compact, mask):
    if compact.shape[0] < 16:
        compact = jnp.concatenate([compact] * (16 // compact.shape[0]), axis=0)
    compact = compact.astype(BF16)
    return jnp.concatenate([compact] * (TOK // compact.shape[0]), axis=0) * mask


def high_low(value):
    high = value.astype(BF16).astype(F32)
    return high, value - high


def times(left, right, mask):
    size = left.shape[0]
    left_high, left_low = high_low(left)
    right_high, right_low = high_low(right)
    stacked = jnp.concatenate([left_high, left_low], axis=0).astype(BF16)
    total = mm(stacked, grow(right_high, mask))
    return total[:size] + total[size:] + mm(left_high.astype(BF16), grow(right_low, mask))


def gather_blocks(a, size, below):
    lane = lax.broadcasted_iota(jnp.int32, (size, 128), 1) >> (size.bit_length() - 1)
    out = []
    for half in range(2):
        total = None
        for k in range(128 // size):
            block = half * (128 // size) + k
            if below and block % 2:
                continue
            top = (block + (1 if below else 0)) * size
            piece = jnp.where(lane == k, a[top : top + size, half * 128 : half * 128 + 128], 0.0)
            total = piece if total is None else total + piece
        out.append(total)
    return jnp.concatenate(out, axis=1)


def each(fn, *lists):
    return [fn(*items) for items in zip(*lists)]


def half_inverses(many, masks):
    row, col = rows_and_columns((8, TOK))
    eye = ((col & 7) == row).astype(F32)
    d = each(lambda a: gather_blocks(a, 8, False), many)
    t = each(lambda d: eye - d, d)
    square = each(lambda d: times(d, d, masks[0]), d)
    both = each(lambda t, s: times(jnp.concatenate([t, s], axis=0), s, masks[0]), t, square)
    t = each(lambda t, b: t + b[:8], t, both)
    t = each(lambda t, b: t + times(t, b[8:], masks[0]), t, both)
    for i, size in enumerate(LEVELS):
        e = each(lambda a: gather_blocks(a, size, True), many)
        y = each(lambda e, t: times(e, t, masks[2 * i]), e, t)
        z = each(lambda t, y: times(t, y, masks[2 * i + 1]), t, y)
        lane = lax.broadcasted_iota(jnp.int32, (size, TOK), 1)
        left = ((lane >> (size.bit_length() - 1)) & 1) == 0
        t = each(
            lambda t, z: jnp.concatenate([jnp.where(left, t, 0.0), jnp.where(left, -z, t)], axis=0),
            t, z,
        )
    return t


def solve_halves(a, t, beta, right):
    scaled = each(lambda t, b: parts(t * b, 2), t, beta)
    plain = each(lambda t: parts(t[:, 128:], 2), t)
    cross = each(lambda a: parts(a[128:, :128], 2), a)
    first = each(
        lambda s, r: (mm(s[0][:, :128], r[:128]) + mm(s[1][:, :128], r[:128])).astype(BF16),
        scaled, right,
    )
    moved = each(lambda c, x: (mm(c[0], x) + mm(c[1], x)).astype(BF16), cross, first)
    second = each(
        lambda s, r, p, y: (
            mm(s[0][:, 128:], r[128:]) + mm(s[1][:, 128:], r[128:]) - mm(p[0], y) - mm(p[1], y)
        ).astype(BF16),
        scaled, right, plain, moved,
    )
    return each(lambda x, y: jnp.concatenate([x, y], axis=0), first, second)


def pack_kernel(k_ref, v_ref, q_ref, weight_ref, out_ref, half_ref, sem):
    core = lax.axis_index("ctx") % CORES
    rows = weight_ref.shape[0] // CORES
    copy = pltpu.make_async_copy(weight_ref.at[pl.ds(core * rows, rows)], half_ref, sem)
    copy.start()
    out_ref[:, 0:256] = k_ref[...]
    out_ref[:, 256:768] = v_ref[...]
    out_ref[:, 768:1024] = q_ref[...]
    copy.wait()


def early_kernel(
    k_ref, v_ref, decay_ref, beta_ref, doc_ref, wk_ref, wv_ref, edge_ref,
    key_ref, value_ref, factor_ref, carry_ref, last_ref, start_ref, head_ref, mask_ref, ext_ref,
):
    row, col = rows_and_columns()
    lower = (col <= row).astype(BF16)
    eye = (col == row).astype(BF16)
    start = spread([local_start(doc_ref)], eye, 1)[0]
    start_ref[...] = start[0:RIM]
    decay = decay_ref[...]
    beta = beta_ref[...]
    cum_row = sum(mm_t(piece, lower) for piece in parts(decay, 3))
    cum_col = spread([decay[h : h + 1] for h in range(HEADS)], lower, 3)
    beta_col = spread([beta[h : h + 1] for h in range(HEADS)], eye, 2)
    keep = linked_mask(start)
    for h in range(HEADS):
        fade = fading(cum_col[h], cum_row[h : h + 1], start, keep)
        beta_wide = jnp.concatenate([beta_col[h], beta_col[h]], axis=1)
        factor_ref[h] = jnp.where(col < row, beta_wide * fade, 0.0)
        carry_ref[h] = jnp.where(start < 0.0, jnp.exp(cum_col[h]), 0.0)
        last_ref[h : h + 1] = fade[TOK - 1 : TOK, :]
    valid = tap_masks(start)
    key_conv = short_conv(ext_ref, k_ref, jnp.zeros((8, 256), F32), wk_ref, valid)
    for g, key in enumerate(unit_keys(key_conv)):
        key_ref[g] = key.astype(BF16)
    value_conv = short_conv(ext_ref, v_ref, jnp.zeros((8, 512), F32), wv_ref, valid)
    value_ref[...] = value_conv.astype(BF16)
    head_ref[:, 0:256] = k_ref[0:RIM, :]
    head_ref[:, 256:768] = v_ref[0:RIM, :]
    for i, mask in enumerate(block_masks()):
        mask_ref[i] = mask


def first_rows(rim, own, w_ref, start):
    width = own.shape[1]
    ext = jnp.concatenate([rim, own], axis=0)
    token = lax.broadcasted_iota(jnp.int32, (8, 128), 0).astype(F32)
    total = own * w_ref[0:1, :]
    for tap in range(1, TAPS):
        mask = jnp.concatenate([start <= token - tap] * (width // 128), axis=1)
        total = total + jnp.where(mask, ext[8 - tap : 16 - tap] * w_ref[tap : tap + 1, :], 0.0)
    return total * jax.nn.sigmoid(total)


def map_kernel(
    rim_ref, head_ref, start_ref, key_ref, value_ref, factor_ref, carry_ref, last_ref, beta_ref,
    wk_ref, wv_ref, mask_ref, wu_ref, kb_ref, own_ref, give_ref,
):
    rim = rim_ref[...].astype(F32)[8:16]
    head = head_ref[...].astype(F32)[0:8]
    start = start_ref[0:8]
    first_keys = unit_keys(first_rows(rim[:, 0:256], head[:, 0:256], wk_ref, start))
    first_values = first_rows(rim[:, 256:768], head[:, 256:768], wv_ref, start)

    def patched(first, whole):
        whole = whole.astype(F32)
        return jnp.concatenate([first, whole[8:]], axis=0)

    keys = [patched(first_keys[g], key_ref[g]).astype(BF16) for g in range(GROUPS)]
    values = patched(first_values, value_ref[...]).astype(BF16)
    beta = beta_ref[...]
    gram = [mm_t(k, k) for k in keys]
    flipped = [k.astype(F32).T for k in keys]
    core = lax.axis_index("ctx") % CORES
    for g in range(GROUPS):
        kb_ref[g] = keys[g]
    heads = range(HEADS)
    masks = [mask_ref[i] for i in range(2 * len(LEVELS))]
    a = [factor_ref[h] * gram[h // 2] for h in heads]
    inverses = half_inverses(a, masks)
    right = [
        jnp.concatenate(
            [
                (carry_ref[h] * keys[h // 2].astype(F32)).astype(BF16),
                values[:, h * DV : (h + 1) * DV],
            ],
            axis=1,
        )
        for h in heads
    ]
    solved = solve_halves(a, inverses, [beta[h : h + 1] for h in heads], right)
    faded = [(flipped[h // 2] * last_ref[h : h + 1, :]).astype(BF16) for h in heads]
    both = each(mm, faded, solved)
    r, c = rows_and_columns((DK, DK))
    for h in heads:
        wu_ref[h] = solved[h]
        decay = jnp.broadcast_to(carry_ref[h, TOK - 1 : TOK, :], (DK, DK))
        diagonal = jnp.where(r == c, decay, 0.0)
        step = jnp.concatenate([diagonal - both[h][:, :DK], both[h][:, DK:]], axis=1).astype(BF16)

        @pl.when(core == h // 2)
        def _():
            own_ref[h % 2] = step

        @pl.when(core != h // 2)
        def _():
            give_ref[h % 2] = step


def output_kernel(
    q_ref, rim_ref, decay_ref, doc_ref, wq_ref, kb_ref, wu_ref, out_ref, reach_ref, ext_ref
):
    row, col = rows_and_columns()
    lower = (col <= row).astype(BF16)
    eye = (col == row).astype(BF16)
    rim = rim_ref[...].astype(F32)[8:16]
    start = spread([local_start(doc_ref)], eye, 1)[0]
    query_conv = short_conv(ext_ref, q_ref, rim[:, 768:1024], wq_ref, tap_masks(start))
    decay = decay_ref[...]
    cum_row = sum(mm_t(piece, lower) for piece in parts(decay, 3))
    cum_col = spread([decay[h : h + 1] for h in range(HEADS)], lower, 3)
    keep = linked_mask(start)
    scores = []
    for g in range(GROUPS):
        query = query_conv[:, g * DK : (g + 1) * DK].astype(BF16)
        scores.append(mm_t(query, kb_ref[g]))
    for h in range(HEADS):
        g = h // 2
        fade = fading(cum_col[h], cum_row[h : h + 1], start, keep)
        both = mm((fade * scores[g]).astype(BF16), wu_ref[h])
        carry = jnp.where(start < 0.0, jnp.exp(cum_col[h]), 0.0)
        reach = carry * query_conv[:, g * DK : (g + 1) * DK] - both[:, :DK]
        reach_ref[h] = reach.astype(BF16)
        out_ref[h] = both[:, DK:]


def joined(first, later):
    moved = mm(later[:, :DK], first)
    return jnp.concatenate([moved[:, :DK], moved[:, DK:] + later[:, DK:].astype(F32)], axis=1)


def pair_kernel(own_ref, got_ref, out_ref):
    core = lax.axis_index("ctx") % CORES
    for k in range(2):
        own = own_ref[k]
        got = got_ref[k]
        first = jnp.where(core == 0, own, got)
        later = jnp.where(core == 0, got, own)
        out_ref[k] = joined(first, later).astype(BF16)


def row_kernel(own_ref, one_ref, two_ref, three_ref, after_ref, before_ref, total_ref, slots):
    x = (lax.axis_index("ctx") // CORES) % CHIPS_X
    for step, ref in enumerate((own_ref, one_ref, two_ref, three_ref)):
        slots[(x + CHIPS_X - step) % CHIPS_X] = ref[...]
    r, c = rows_and_columns((DK, DK + DV))
    start = (r == c).astype(BF16)
    for k in range(2):
        run = slots[0, k]
        before_ref[k] = jnp.where(x == 0, start, run)
        for place in range(1, CHIPS_X):
            run = joined(run, slots[place, k]).astype(BF16)
            if place < CHIPS_X - 1:
                before_ref[k] = jnp.where(x == place + 1, run, before_ref[k])
        total_ref[k] = run


def state_kernel(
    own_ref, one_ref, two_ref, three_ref, before_ref, mine_ref, other_ref, keep_ref, give_ref, slots
):
    index = lax.axis_index("ctx")
    core = index % CORES
    y = index // (CORES * CHIPS_X)
    for step, ref in enumerate((own_ref, one_ref, two_ref, three_ref)):
        slots[(y + CHIPS_Y - step) % CHIPS_Y] = ref[...]
    for k in range(2):
        state = jnp.where(y > 0, slots[0, k][:, DK:].astype(F32), 0.0)
        for place in range(1, CHIPS_Y - 1):
            block = slots[place, k]
            moved = mm(block[:, :DK], state.astype(BF16)) + block[:, DK:].astype(F32)
            state = jnp.where(place < y, moved, state)
        block = before_ref[k]
        state = mm(block[:, :DK], state.astype(BF16)) + block[:, DK:].astype(F32)
        block = jnp.where(core == 0, mine_ref[k], other_ref[k])
        after = mm(block[:, :DK], state.astype(BF16)) + block[:, DK:].astype(F32)
        keep_ref[k] = jnp.where(core == 0, state, after).astype(BF16)
        give_ref[k] = jnp.where(core == 0, after, state).astype(BF16)


KEPT = (0, -3, 2)
TO_RIGHT = (1, -2, 3)
TO_LEFT = (-1, -4)


def norm_kernel(
    local_ref, reach_ref, mine_ref, got_ref, gate_ref, gain_ref, keep_ref, right_ref, left_ref, normed_ref
):
    core = lax.axis_index("ctx") % CORES
    place = lax.axis_index("head")
    for h in range(HEADS):
        state = jnp.where(core == h // 2, mine_ref[h % 2], got_ref[h % 2])
        heads = local_ref[h] + mm(reach_ref[h], state)
        inv = lax.rsqrt(jnp.mean(heads * heads, axis=-1, keepdims=True) + EPS)
        gate = gate_ref[:, h * DV : (h + 1) * DV].astype(F32)
        gate = gate * jax.nn.sigmoid(gate)
        normed_ref[:, h * DV : (h + 1) * DV] = (heads * inv * gain_ref[...] * gate).astype(BF16)
    rows = TOK // 8
    for steps, ref in ((KEPT, keep_ref), (TO_RIGHT, right_ref), (TO_LEFT, left_ref)):
        for k, step in enumerate(steps):
            top = pl.multiple_of(((place + step + 8) % 8) * rows, rows)
            ref[k * rows : (k + 1) * rows, :] = normed_ref[pl.ds(top, rows), :]


def project_kernel(
    keep_ref, left_ref, right_ref, own_ref, left_w_ref, left_w2_ref, right_w_ref, right_w2_ref,
    *out_refs,
):
    core = lax.axis_index("ctx") % CORES
    keep = keep_ref[...]

    def halves(rows):
        half = rows.shape[1] // 2
        first, second = rows[:, :half], rows[:, half:]
        return jnp.where(core == 0, first, second), jnp.where(core == 0, second, first)

    left, left2 = halves(left_ref[...])
    right, right2 = halves(right_ref[...])
    rows = TOK // 8
    for part in range(0, own_ref.shape[1], 512):
        at = slice(part, part + 512)
        total = mm(keep, own_ref[:, at]) + mm(left, left_w_ref[:, at]) + mm(left2, left_w2_ref[:, at])
        more = mm(right, right_w_ref[:, at]) + mm(right2, right_w2_ref[:, at])
        for k, out_ref in enumerate(out_refs):
            term = total[k * rows : (k + 1) * rows]
            if k < len(TO_LEFT):
                term = term + more[k * rows : (k + 1) * rows]
            out_ref[:, at] = term.astype(out_ref.dtype)


def sum_kernel(own_ref, one_ref, two_ref, out_ref):
    total = own_ref[...]
    for ref in (one_ref, two_ref):
        total = total + ref[...].astype(F32)
    out_ref[...] = total.astype(BF16)


VMEM = pl.BlockSpec(memory_space=pltpu.VMEM)
HBM = pl.BlockSpec(memory_space=pltpu.HBM)


def whole(shape):
    return pl.BlockSpec(shape, lambda i: (0,) * len(shape))


def call(
    kernel, outs, inputs, scratch=(), flops=0, moved=0, limit=32, specs=None, out_specs=None,
    blocked=False,
):
    if blocked:
        specs = [whole(a.shape) for a in inputs]
        out_specs = [whole(s) for s, _ in outs]
    return pl.pallas_call(
        kernel,
        grid=(1,) if blocked else (),
        out_shape=[jax.ShapeDtypeStruct(s, t) for s, t in outs],
        in_specs=[VMEM] * len(inputs) if specs is None else specs,
        out_specs=[VMEM] * len(outs) if out_specs is None else out_specs,
        scratch_shapes=list(scratch),
        compiler_params=pltpu.CompilerParams(vmem_limit_bytes=limit * MIB),
        cost_estimate=pl.CostEstimate(flops=flops, bytes_accessed=moved, transcendentals=0),
    )(*inputs)


def on_device(
    query_in, key_in, value_in, out_gate, log_decay, beta_gate, doc_start,
    conv_query, conv_key, conv_value, norm_gain, out_weight,
):
    doc_row = doc_start.reshape(1, TOK)
    gain_row = norm_gain.reshape(1, DV)
    width = out_weight.shape[1]
    last = TOK // RIM - 1
    edge, half = pl.pallas_call(
        pack_kernel,
        grid=(1,),
        out_shape=[
            jax.ShapeDtypeStruct((RIM, 1024), BF16),
            jax.ShapeDtypeStruct((out_weight.shape[0] // CORES, width), BF16),
        ],
        in_specs=[pl.BlockSpec((RIM, n), lambda i: (last, 0)) for n in (256, 512, 256)] + [HBM],
        out_specs=[pl.BlockSpec((RIM, 1024), lambda i: (0, 0)), VMEM],
        scratch_shapes=[pltpu.SemaphoreType.DMA],
        compiler_params=pltpu.CompilerParams(vmem_limit_bytes=54 * MIB),
        cost_estimate=pl.CostEstimate(flops=5_000_000_000, bytes_accessed=0, transcendentals=0),
    )(key_in, value_in, query_in, out_weight)
    left_half = lax.ppermute(half, "head", around_z(1))
    right_half = lax.ppermute(half, "head", around_z(-1))
    rim = lax.ppermute(edge, "ctx", [(i, i + 1) for i in range(CTX - 1)])
    wide = (2, DK, DK + DV)
    early = call(
        early_kernel,
        [
            ((GROUPS, TOK, DK), BF16), ((TOK, HEADS * DV), BF16), ((HEADS, TOK, TOK), F32),
            ((HEADS, TOK, 128), F32), ((HEADS, TOK), F32), ((RIM, 128), F32), ((RIM, 768), BF16),
            ((2 * len(LEVELS), TOK, TOK), BF16),
        ],
        [key_in, value_in, log_decay, beta_gate, doc_row, conv_key, conv_value, edge],
        [
            pltpu.VMEM((8 + TOK, 512), F32),
        ],
        flops=500_000_000, moved=0, limit=48, blocked=True,
    )
    keys, values, factor, carry, final, start, head, masks = early
    solved, keys, own, give = call(
        map_kernel,
        [((HEADS, TOK, DK + DV), BF16), ((GROUPS, TOK, DK), BF16), (wide, BF16), (wide, BF16)],
        [rim, head, start, keys, values, factor, carry, final, beta_gate, conv_key, conv_value, masks],
        flops=4_000_000_000, moved=2_000_000,
    )
    other = lax.ppermute(give, "ctx", core_swap())
    (pair,) = call(pair_kernel, [(wide, BF16)], [own, other], flops=20_000_000, moved=400_000)
    near = [lax.ppermute(pair, "ctx", along_x(k)) for k in (1, 2, 3)]
    local, reach = call(
        output_kernel,
        [((HEADS, TOK, DV), F32), ((HEADS, TOK, DK), BF16)],
        [query_in, rim, log_decay, doc_row, conv_query, keys, solved],
        [pltpu.VMEM((8 + TOK, 256), F32)],
        flops=2_000_000_000, moved=2_000_000,
    )
    before, total = call(
        row_kernel, [(wide, BF16), (wide, BF16)], [pair] + near + [reach],
        [pltpu.VMEM((CHIPS_X,) + wide, BF16)], flops=60_000_000, moved=800_000,
        specs=[VMEM] * 4 + [HBM],
    )
    far = [lax.ppermute(total, "ctx", along_y(k)) for k in (1, 2, 3)]
    narrow = (2, DK, DV)
    mine, to_other = call(
        state_kernel, [(narrow, BF16), (narrow, BF16)], [total] + far + [before, own, other],
        [pltpu.VMEM((CHIPS_Y,) + wide, BF16)], flops=60_000_000, moved=1_000_000,
    )
    got = lax.ppermute(to_other, "ctx", core_swap())
    left_late, right_late, _ = lax.optimization_barrier((left_half, right_half, got))
    left_half2 = lax.ppermute(left_late, "ctx", core_swap())
    right_half2 = lax.ppermute(right_late, "ctx", core_swap())
    block = TOK // 8

    def normed_rows(steps):
        return ((len(steps) * block, HEADS * DV), BF16)

    keep, to_right, to_left = call(
        norm_kernel, [normed_rows(KEPT), normed_rows(TO_RIGHT), normed_rows(TO_LEFT)],
        [local, reach, mine, got, out_gate, gain_row],
        [pltpu.VMEM((TOK, HEADS * DV), BF16)],
        flops=100_000_000, moved=1_500_000,
    )
    from_left = lax.ppermute(to_right, "head", around_z(1))
    from_right = lax.ppermute(to_left, "head", around_z(-1))
    own_part, back_part, ahead_part = call(
        project_kernel, [((block, width), F32)] + [((block, width), BF16)] * 2,
        [
            keep, from_left, from_right, out_weight, left_half, left_half2, right_half, right_half2
        ],
        flops=600_000_000, moved=6_000_000,
    )
    (mixed,) = call(
        sum_kernel, [((block, width), BF16)],
        [
            own_part,
            lax.ppermute(back_part, "head", around_z(-3)),
            lax.ppermute(ahead_part, "head", around_z(2)),
        ],
        flops=1_000_000, moved=800_000,
    )
    return mixed


def solution(mesh):
    placed = (
        P("ctx", "head"),
        P("ctx", "head"),
        P("ctx", "head"),
        P("ctx", "head"),
        P("head", "ctx"),
        P("head", "ctx"),
        P("ctx"),
        P(None, "head"),
        P(None, "head"),
        P(None, "head"),
        P(),
        P("head", None),
    )
    return jax.shard_map(
        on_device, mesh=mesh, in_specs=placed, out_specs=P(("ctx", "head"), None), check_vma=False
    )
```

```python
import jax
import jax.numpy as jnp
from jax import lax
from jax.experimental import pallas as pl
from jax.experimental.pallas import tpu as pltpu
from jax.sharding import PartitionSpec as P

DK = 128
DV = 128
TOK = 256
HEADS = 4
GROUPS = 2
TAPS = 4
RIM = 16
EPS = 1e-6
F32 = jnp.float32
BF16 = jnp.bfloat16
FAR = -1e30
MIB = 1 << 20

CTX = 32
CORES = 2
CHIPS_X = 4
CHIPS_Y = 4


def core_swap():
    return [(i, i ^ 1) for i in range(CTX)]


def along_x(step):
    return [
        ((y * 4 + x) * 2 + c, (y * 4 + (x + step) % 4) * 2 + c)
        for y in range(4)
        for x in range(4)
        for c in range(2)
    ]


def along_y(step):
    return [
        ((y * 4 + x) * 2 + c, (((y + step) % 4) * 4 + x) * 2 + c)
        for y in range(4)
        for x in range(4)
        for c in range(2)
    ]


def around_z(step):
    return [(i, (i + step) % 8) for i in range(8)]


def neighbours_by_core():
    return [
        (ctx * 8 + (z + (1 if ctx % CORES else -1)) % 8, ctx * 8 + z)
        for ctx in range(CTX)
        for z in range(8)
    ]


def mm(left, right):
    return jnp.dot(left, right, preferred_element_type=F32)


def mm_t(left, right):
    return lax.dot_general(left, right, (((1,), (1,)), ((), ())), preferred_element_type=F32)


def parts(value, count):
    out = []
    for _ in range(count):
        piece = value.astype(BF16)
        out.append(piece)
        value = value - piece.astype(F32)
    return out


def rows_and_columns(shape=(TOK, TOK)):
    return lax.broadcasted_iota(jnp.int32, shape, 0), lax.broadcasted_iota(jnp.int32, shape, 1)


def spread(rows_list, pattern, count):
    out = []
    for pair in range(0, len(rows_list), 2):
        chosen = rows_list[pair : pair + 2]
        wide = jnp.concatenate([jnp.broadcast_to(r, (128, TOK)) for r in chosen], axis=0)
        total = None
        for piece in parts(wide, count):
            term = mm_t(pattern, piece)
            total = term if total is None else total + term
        for k in range(len(chosen)):
            out.append(total[:, k * 128 : (k + 1) * 128])
    return out


def local_start(doc_ref):
    first = lax.axis_index("ctx") * TOK
    return jnp.maximum(doc_ref[...] - first, -TAPS).astype(F32)


def short_conv(ext_ref, x_ref, rim, w_ref, valid):
    width = x_ref.shape[1]
    own = x_ref[...].astype(F32)
    ext_ref[0:8, :width] = rim
    ext_ref[8 : 8 + TOK, :width] = own
    total = own * w_ref[0:1, :]
    for tap in range(1, TAPS):
        shifted = ext_ref[8 - tap : 8 - tap + TOK, :width]
        mask = jnp.concatenate([valid[tap - 1]] * (width // 128), axis=1)
        total = total + jnp.where(mask, shifted * w_ref[tap : tap + 1, :], 0.0)
    return total * jax.nn.sigmoid(total)


def tap_masks(start):
    token = lax.broadcasted_iota(jnp.int32, (TOK, 128), 0).astype(F32)
    return [start <= token - tap for tap in range(1, TAPS)]


def unit_keys(key_conv):
    out = []
    for g in range(GROUPS):
        k = key_conv[:, g * DK : (g + 1) * DK]
        out.append(k * lax.rsqrt(jnp.sum(k * k, axis=-1, keepdims=True) + EPS))
    return out


def fading(cum_col, cum_row, start, keep):
    gap = jnp.concatenate([cum_col, cum_col], axis=1) - cum_row
    return jnp.exp(jnp.where(keep, gap, FAR))


def linked_mask(start):
    row, col = rows_and_columns()
    begin = jnp.concatenate([start, start], axis=1)
    return (col <= row) & (begin <= col.astype(F32))


LEVELS = (8, 16, 32, 64)


def block_masks():
    row, col = rows_and_columns()
    out = []
    for size in LEVELS:
        shift = size.bit_length() - 1
        r, c = row >> shift, col >> shift
        out.append((r == c).astype(F32).astype(BF16))
        out.append(((r == c + 1) & ((c & 1) == 0)).astype(F32).astype(BF16))
    return out


def grow(compact, mask):
    if compact.shape[0] < 16:
        compact = jnp.concatenate([compact] * (16 // compact.shape[0]), axis=0)
    compact = compact.astype(BF16)
    return jnp.concatenate([compact] * (TOK // compact.shape[0]), axis=0) * mask


def high_low(value):
    high = value.astype(BF16).astype(F32)
    return high, value - high


def times(left, right, mask):
    size = left.shape[0]
    left_high, left_low = high_low(left)
    right_high, right_low = high_low(right)
    stacked = jnp.concatenate([left_high, left_low], axis=0).astype(BF16)
    total = mm(stacked, grow(right_high, mask))
    return total[:size] + total[size:] + mm(left_high.astype(BF16), grow(right_low, mask))


def gather_blocks(a, size, below):
    lane = lax.broadcasted_iota(jnp.int32, (size, 128), 1) >> (size.bit_length() - 1)
    out = []
    for half in range(2):
        total = None
        for k in range(128 // size):
            block = half * (128 // size) + k
            if below and block % 2:
                continue
            top = (block + (1 if below else 0)) * size
            piece = jnp.where(lane == k, a[top : top + size, half * 128 : half * 128 + 128], 0.0)
            total = piece if total is None else total + piece
        out.append(total)
    return jnp.concatenate(out, axis=1)


def each(fn, *lists):
    return [fn(*items) for items in zip(*lists)]


def half_inverses(many, masks):
    row, col = rows_and_columns((8, TOK))
    eye = ((col & 7) == row).astype(F32)
    d = each(lambda a: gather_blocks(a, 8, False), many)
    t = each(lambda d: eye - d, d)
    square = each(lambda d: times(d, d, masks[0]), d)
    both = each(lambda t, s: times(jnp.concatenate([t, s], axis=0), s, masks[0]), t, square)
    t = each(lambda t, b: t + b[:8], t, both)
    t = each(lambda t, b: t + times(t, b[8:], masks[0]), t, both)
    for i, size in enumerate(LEVELS):
        e = each(lambda a: gather_blocks(a, size, True), many)
        y = each(lambda e, t: times(e, t, masks[2 * i]), e, t)
        z = each(lambda t, y: times(t, y, masks[2 * i + 1]), t, y)
        lane = lax.broadcasted_iota(jnp.int32, (size, TOK), 1)
        left = ((lane >> (size.bit_length() - 1)) & 1) == 0
        t = each(
            lambda t, z: jnp.concatenate([jnp.where(left, t, 0.0), jnp.where(left, -z, t)], axis=0),
            t, z,
        )
    return t


def solve_halves(a, t, beta, right):
    scaled = each(lambda t, b: parts(t * b, 2), t, beta)
    plain = each(lambda t: parts(t[:, 128:], 2), t)
    cross = each(lambda a: parts(a[128:, :128], 2), a)
    first = each(
        lambda s, r: (mm(s[0][:, :128], r[:128]) + mm(s[1][:, :128], r[:128])).astype(BF16),
        scaled, right,
    )
    moved = each(lambda c, x: (mm(c[0], x) + mm(c[1], x)).astype(BF16), cross, first)
    second = each(
        lambda s, r, p, y: (
            mm(s[0][:, 128:], r[128:]) + mm(s[1][:, 128:], r[128:]) - mm(p[0], y) - mm(p[1], y)
        ).astype(BF16),
        scaled, right, plain, moved,
    )
    return each(lambda x, y: jnp.concatenate([x, y], axis=0), first, second)


def pack_kernel(k_ref, v_ref, q_ref, out_ref):
    out_ref[:, 0:256] = k_ref[...]
    out_ref[:, 256:768] = v_ref[...]
    out_ref[:, 768:1024] = q_ref[...]


def early_kernel(
    k_ref, v_ref, decay_ref, beta_ref, doc_ref, wk_ref, wv_ref,
    key_ref, value_ref, factor_ref, carry_ref, last_ref, start_ref, head_ref, mask_ref, ext_ref,
):
    row, col = rows_and_columns()
    lower = (col <= row).astype(BF16)
    eye = (col == row).astype(BF16)
    start = spread([local_start(doc_ref)], eye, 1)[0]
    start_ref[...] = start[0:RIM]
    decay = decay_ref[...]
    beta = beta_ref[...]
    cum_row = sum(mm_t(piece, lower) for piece in parts(decay, 3))
    cum_col = spread([decay[h : h + 1] for h in range(HEADS)], lower, 3)
    beta_col = spread([beta[h : h + 1] for h in range(HEADS)], eye, 2)
    keep = linked_mask(start)
    for h in range(HEADS):
        fade = fading(cum_col[h], cum_row[h : h + 1], start, keep)
        beta_wide = jnp.concatenate([beta_col[h], beta_col[h]], axis=1)
        factor_ref[h] = jnp.where(col < row, beta_wide * fade, 0.0)
        carry_ref[h] = jnp.where(start < 0.0, jnp.exp(cum_col[h]), 0.0)
        last_ref[h : h + 1] = fade[TOK - 1 : TOK, :]
    valid = tap_masks(start)
    key_conv = short_conv(ext_ref, k_ref, jnp.zeros((8, 256), F32), wk_ref, valid)
    for g, key in enumerate(unit_keys(key_conv)):
        key_ref[g] = key.astype(BF16)
    value_conv = short_conv(ext_ref, v_ref, jnp.zeros((8, 512), F32), wv_ref, valid)
    value_ref[...] = value_conv.astype(BF16)
    head_ref[:, 0:256] = k_ref[0:RIM, :]
    head_ref[:, 256:768] = v_ref[0:RIM, :]
    for i, mask in enumerate(block_masks()):
        mask_ref[i] = mask


def first_rows(rim, own, w_ref, start):
    width = own.shape[1]
    ext = jnp.concatenate([rim, own], axis=0)
    token = lax.broadcasted_iota(jnp.int32, (8, 128), 0).astype(F32)
    total = own * w_ref[0:1, :]
    for tap in range(1, TAPS):
        mask = jnp.concatenate([start <= token - tap] * (width // 128), axis=1)
        total = total + jnp.where(mask, ext[8 - tap : 16 - tap] * w_ref[tap : tap + 1, :], 0.0)
    return total * jax.nn.sigmoid(total)


def map_kernel(
    rim_ref, head_ref, start_ref, key_ref, value_ref, factor_ref, carry_ref, last_ref, beta_ref,
    wk_ref, wv_ref, mask_ref, wu_ref, kb_ref, own_ref, give_ref,
):
    rim = rim_ref[...].astype(F32)[8:16]
    head = head_ref[...].astype(F32)[0:8]
    start = start_ref[0:8]
    first_keys = unit_keys(first_rows(rim[:, 0:256], head[:, 0:256], wk_ref, start))
    first_values = first_rows(rim[:, 256:768], head[:, 256:768], wv_ref, start)

    def patched(first, whole):
        whole = whole.astype(F32)
        return jnp.concatenate([first, whole[8:]], axis=0)

    keys = [patched(first_keys[g], key_ref[g]).astype(BF16) for g in range(GROUPS)]
    values = patched(first_values, value_ref[...]).astype(BF16)
    beta = beta_ref[...]
    gram = [mm_t(k, k) for k in keys]
    flipped = [k.astype(F32).T for k in keys]
    core = lax.axis_index("ctx") % CORES
    for g in range(GROUPS):
        kb_ref[g] = keys[g]
    heads = range(HEADS)
    masks = [mask_ref[i] for i in range(2 * len(LEVELS))]
    a = [factor_ref[h] * gram[h // 2] for h in heads]
    inverses = half_inverses(a, masks)
    right = [
        jnp.concatenate(
            [
                (carry_ref[h] * keys[h // 2].astype(F32)).astype(BF16),
                values[:, h * DV : (h + 1) * DV],
            ],
            axis=1,
        )
        for h in heads
    ]
    solved = solve_halves(a, inverses, [beta[h : h + 1] for h in heads], right)
    faded = [(flipped[h // 2] * last_ref[h : h + 1, :]).astype(BF16) for h in heads]
    both = each(mm, faded, solved)
    r, c = rows_and_columns((DK, DK))
    for h in heads:
        wu_ref[h] = solved[h]
        decay = jnp.broadcast_to(carry_ref[h, TOK - 1 : TOK, :], (DK, DK))
        diagonal = jnp.where(r == c, decay, 0.0)
        step = jnp.concatenate([diagonal - both[h][:, :DK], both[h][:, DK:]], axis=1).astype(BF16)

        @pl.when(core == h // 2)
        def _():
            own_ref[h % 2] = step

        @pl.when(core != h // 2)
        def _():
            give_ref[h % 2] = step


def output_kernel(
    q_ref, rim_ref, decay_ref, doc_ref, wq_ref, kb_ref, wu_ref, out_ref, reach_ref, ext_ref
):
    row, col = rows_and_columns()
    lower = (col <= row).astype(BF16)
    eye = (col == row).astype(BF16)
    rim = rim_ref[...].astype(F32)[8:16]
    start = spread([local_start(doc_ref)], eye, 1)[0]
    query_conv = short_conv(ext_ref, q_ref, rim[:, 768:1024], wq_ref, tap_masks(start))
    decay = decay_ref[...]
    cum_row = sum(mm_t(piece, lower) for piece in parts(decay, 3))
    cum_col = spread([decay[h : h + 1] for h in range(HEADS)], lower, 3)
    keep = linked_mask(start)
    scores = []
    for g in range(GROUPS):
        query = query_conv[:, g * DK : (g + 1) * DK].astype(BF16)
        scores.append(mm_t(query, kb_ref[g]))
    for h in range(HEADS):
        g = h // 2
        fade = fading(cum_col[h], cum_row[h : h + 1], start, keep)
        both = mm((fade * scores[g]).astype(BF16), wu_ref[h])
        carry = jnp.where(start < 0.0, jnp.exp(cum_col[h]), 0.0)
        reach = carry * query_conv[:, g * DK : (g + 1) * DK] - both[:, :DK]
        reach_ref[h] = reach.astype(BF16)
        out_ref[h] = both[:, DK:]


def joined(first, later):
    moved = mm(later[:, :DK], first)
    return jnp.concatenate([moved[:, :DK], moved[:, DK:] + later[:, DK:].astype(F32)], axis=1)


def pair_kernel(own_ref, got_ref, out_ref):
    core = lax.axis_index("ctx") % CORES
    for k in range(2):
        own = own_ref[k]
        got = got_ref[k]
        first = jnp.where(core == 0, own, got)
        later = jnp.where(core == 0, got, own)
        out_ref[k] = joined(first, later).astype(BF16)


def row_kernel(own_ref, one_ref, two_ref, three_ref, after_ref, before_ref, total_ref, slots):
    x = (lax.axis_index("ctx") // CORES) % CHIPS_X
    for step, ref in enumerate((own_ref, one_ref, two_ref, three_ref)):
        slots[(x + CHIPS_X - step) % CHIPS_X] = ref[...]
    r, c = rows_and_columns((DK, DK + DV))
    start = (r == c).astype(BF16)
    for k in range(2):
        run = slots[0, k]
        before_ref[k] = jnp.where(x == 0, start, run)
        for place in range(1, CHIPS_X):
            run = joined(run, slots[place, k]).astype(BF16)
            if place < CHIPS_X - 1:
                before_ref[k] = jnp.where(x == place + 1, run, before_ref[k])
        total_ref[k] = run


def state_kernel(
    own_ref, one_ref, two_ref, three_ref, before_ref, mine_ref, other_ref, keep_ref, give_ref, slots
):
    index = lax.axis_index("ctx")
    core = index % CORES
    y = index // (CORES * CHIPS_X)
    for step, ref in enumerate((own_ref, one_ref, two_ref, three_ref)):
        slots[(y + CHIPS_Y - step) % CHIPS_Y] = ref[...]
    for k in range(2):
        state = jnp.where(y > 0, slots[0, k][:, DK:].astype(F32), 0.0)
        for place in range(1, CHIPS_Y - 1):
            block = slots[place, k]
            moved = mm(block[:, :DK], state.astype(BF16)) + block[:, DK:].astype(F32)
            state = jnp.where(place < y, moved, state)
        block = before_ref[k]
        state = mm(block[:, :DK], state.astype(BF16)) + block[:, DK:].astype(F32)
        block = jnp.where(core == 0, mine_ref[k], other_ref[k])
        after = mm(block[:, :DK], state.astype(BF16)) + block[:, DK:].astype(F32)
        keep_ref[k] = jnp.where(core == 0, state, after).astype(BF16)
        give_ref[k] = jnp.where(core == 0, after, state).astype(BF16)


KEPT = (0, -3, 2)
TO_RIGHT = (1, -2, 3)
TO_LEFT = (-1, -4)


def norm_kernel(
    local_ref, reach_ref, mine_ref, got_ref, gate_ref, gain_ref, keep_ref, right_ref, left_ref, normed_ref
):
    core = lax.axis_index("ctx") % CORES
    place = lax.axis_index("head")
    for h in range(HEADS):
        state = jnp.where(core == h // 2, mine_ref[h % 2], got_ref[h % 2])
        heads = local_ref[h] + mm(reach_ref[h], state)
        inv = lax.rsqrt(jnp.mean(heads * heads, axis=-1, keepdims=True) + EPS)
        gate = gate_ref[:, h * DV : (h + 1) * DV].astype(F32)
        gate = gate * jax.nn.sigmoid(gate)
        normed_ref[:, h * DV : (h + 1) * DV] = (heads * inv * gain_ref[...] * gate).astype(BF16)
    rows = TOK // 8
    for steps, ref in ((KEPT, keep_ref), (TO_RIGHT, right_ref), (TO_LEFT, left_ref)):
        for k, step in enumerate(steps):
            top = pl.multiple_of(((place + step + 8) % 8) * rows, rows)
            ref[k * rows : (k + 1) * rows, :] = normed_ref[pl.ds(top, rows), :]


def project_kernel(keep_ref, left_ref, right_ref, own_ref, near_ref, far_ref, *out_refs):
    core = lax.axis_index("ctx") % CORES
    keep = keep_ref[...]
    left = left_ref[...]
    right = right_ref[...]
    none = jnp.zeros((left.shape[0] - right.shape[0], right.shape[1]), BF16)
    right = jnp.concatenate([right, none], axis=0)
    near = jnp.where(core == 0, left, right)
    far = jnp.where(core == 0, right, left)
    rows = TOK // 8
    for part in range(0, own_ref.shape[1], 512):
        at = slice(part, part + 512)
        total = mm(keep, own_ref[:, at]) + mm(near, near_ref[:, at]) + mm(far, far_ref[:, at])
        for k, out_ref in enumerate(out_refs):
            out_ref[:, at] = total[k * rows : (k + 1) * rows].astype(out_ref.dtype)


def sum_kernel(own_ref, one_ref, two_ref, out_ref):
    total = own_ref[...]
    for ref in (one_ref, two_ref):
        total = total + ref[...].astype(F32)
    out_ref[...] = total.astype(BF16)


VMEM = pl.BlockSpec(memory_space=pltpu.VMEM)
HBM = pl.BlockSpec(memory_space=pltpu.HBM)


def whole(shape):
    return pl.BlockSpec(shape, lambda i: (0,) * len(shape))


def call(
    kernel, outs, inputs, scratch=(), flops=0, moved=0, limit=32, specs=None, out_specs=None,
    blocked=False,
):
    if blocked:
        specs = [whole(a.shape) for a in inputs]
        out_specs = [whole(s) for s, _ in outs]
    return pl.pallas_call(
        kernel,
        grid=(1,) if blocked else (),
        out_shape=[jax.ShapeDtypeStruct(s, t) for s, t in outs],
        in_specs=[VMEM] * len(inputs) if specs is None else specs,
        out_specs=[VMEM] * len(outs) if out_specs is None else out_specs,
        scratch_shapes=list(scratch),
        compiler_params=pltpu.CompilerParams(vmem_limit_bytes=limit * MIB),
        cost_estimate=pl.CostEstimate(flops=flops, bytes_accessed=moved, transcendentals=0),
    )(*inputs)


def on_device(
    query_in, key_in, value_in, out_gate, log_decay, beta_gate, doc_start,
    conv_query, conv_key, conv_value, norm_gain, out_weight,
):
    doc_row = doc_start.reshape(1, TOK)
    gain_row = norm_gain.reshape(1, DV)
    width = out_weight.shape[1]
    last = TOK // RIM - 1
    edge = pl.pallas_call(
        pack_kernel,
        grid=(1,),
        out_shape=jax.ShapeDtypeStruct((RIM, 1024), BF16),
        in_specs=[pl.BlockSpec((RIM, n), lambda i: (last, 0)) for n in (256, 512, 256)],
        out_specs=pl.BlockSpec((RIM, 1024), lambda i: (0, 0)),
        cost_estimate=pl.CostEstimate(flops=5_000_000_000, bytes_accessed=0, transcendentals=0),
    )(key_in, value_in, query_in)
    near_weight = lax.ppermute(
        lax.optimization_barrier((out_weight, edge))[0], ("ctx", "head"), neighbours_by_core()
    )
    rim = lax.ppermute(edge, "ctx", [(i, (i + 1) % CTX) for i in range(CTX)])
    wide = (2, DK, DK + DV)
    early = call(
        early_kernel,
        [
            ((GROUPS, TOK, DK), BF16), ((TOK, HEADS * DV), BF16), ((HEADS, TOK, TOK), F32),
            ((HEADS, TOK, 128), F32), ((HEADS, TOK), F32), ((RIM, 128), F32), ((RIM, 768), BF16),
            ((2 * len(LEVELS), TOK, TOK), BF16),
        ],
        [key_in, value_in, log_decay, beta_gate, doc_row, conv_key, conv_value],
        [
            pltpu.VMEM((8 + TOK, 512), F32),
        ],
        flops=500_000_000, moved=0, limit=48, blocked=True,
    )
    keys, values, factor, carry, final, start, head, masks = early
    solved, keys, own, give = call(
        map_kernel,
        [((HEADS, TOK, DK + DV), BF16), ((GROUPS, TOK, DK), BF16), (wide, BF16), (wide, BF16)],
        [rim, head, start, keys, values, factor, carry, final, beta_gate, conv_key, conv_value, masks],
        flops=4_000_000_000, moved=2_000_000,
    )
    other = lax.ppermute(give, "ctx", core_swap())
    (pair,) = call(pair_kernel, [(wide, BF16)], [own, other], flops=20_000_000, moved=400_000)
    near = [lax.ppermute(pair, "ctx", along_x(k)) for k in (1, 2, 3)]
    local, reach = call(
        output_kernel,
        [((HEADS, TOK, DV), F32), ((HEADS, TOK, DK), BF16)],
        [query_in, rim, log_decay, doc_row, conv_query, keys, solved],
        [pltpu.VMEM((8 + TOK, 256), F32)],
        flops=2_000_000_000, moved=2_000_000,
    )
    before, total = call(
        row_kernel, [(wide, BF16), (wide, BF16)], [pair] + near + [reach],
        [pltpu.VMEM((CHIPS_X,) + wide, BF16)], flops=60_000_000, moved=800_000,
        specs=[VMEM] * 4 + [HBM],
    )
    far = [lax.ppermute(total, "ctx", along_y(k)) for k in (1, 2, 3)]
    narrow = (2, DK, DV)
    mine, to_other = call(
        state_kernel, [(narrow, BF16), (narrow, BF16)], [total] + far + [before, own, other],
        [pltpu.VMEM((CHIPS_Y,) + wide, BF16)], flops=60_000_000, moved=1_000_000,
    )
    got = lax.ppermute(to_other, "ctx", core_swap())
    late_weight, _ = lax.optimization_barrier((near_weight, got))
    far_weight = lax.ppermute(late_weight, "ctx", core_swap())
    block = TOK // 8

    def normed_rows(steps):
        return ((len(steps) * block, HEADS * DV), BF16)

    keep, to_right, to_left = call(
        norm_kernel, [normed_rows(KEPT), normed_rows(TO_RIGHT), normed_rows(TO_LEFT)],
        [local, reach, mine, got, out_gate, gain_row],
        [pltpu.VMEM((TOK, HEADS * DV), BF16)],
        flops=100_000_000, moved=1_500_000,
    )
    from_left = lax.ppermute(to_right, "head", around_z(1))
    from_right = lax.ppermute(to_left, "head", around_z(-1))
    own_part, back_part, ahead_part = call(
        project_kernel, [((block, width), F32)] + [((block, width), BF16)] * 2,
        [
            keep, from_left, from_right, out_weight, near_weight, far_weight
        ],
        flops=600_000_000, moved=6_000_000,
    )
    (mixed,) = call(
        sum_kernel, [((block, width), BF16)],
        [
            own_part,
            lax.ppermute(back_part, "head", around_z(-3)),
            lax.ppermute(ahead_part, "head", around_z(2)),
        ],
        flops=1_000_000, moved=800_000,
    )
    return mixed


def solution(mesh):
    placed = (
        P("ctx", "head"),
        P("ctx", "head"),
        P("ctx", "head"),
        P("ctx", "head"),
        P("head", "ctx"),
        P("head", "ctx"),
        P("ctx"),
        P(None, "head"),
        P(None, "head"),
        P(None, "head"),
        P(),
        P("head", None),
    )
    return jax.shard_map(
        on_device, mesh=mesh, in_specs=placed, out_specs=P(("ctx", "head"), None), check_vma=False
    )
```

```python
import jax
import jax.numpy as jnp
from jax import lax
from jax.experimental import pallas as pl
from jax.experimental.pallas import tpu as pltpu
from jax.sharding import PartitionSpec as P

DK = 128
DV = 128
TOK = 256
HEADS = 4
GROUPS = 2
TAPS = 4
RIM = 16
EPS = 1e-6
F32 = jnp.float32
BF16 = jnp.bfloat16
FAR = -1e30
MIB = 1 << 20

CTX = 32
CORES = 2
CHIPS_X = 4
CHIPS_Y = 4


def core_swap():
    return [(i, i ^ 1) for i in range(CTX)]


def along_x(step):
    return [
        ((y * 4 + x) * 2 + c, (y * 4 + (x + step) % 4) * 2 + c)
        for y in range(4)
        for x in range(4)
        for c in range(2)
    ]


def along_y(step):
    return [
        ((y * 4 + x) * 2 + c, (((y + step) % 4) * 4 + x) * 2 + c)
        for y in range(4)
        for x in range(4)
        for c in range(2)
    ]


def mm(left, right):
    return jnp.dot(left, right, preferred_element_type=F32)


def mm_t(left, right):
    return lax.dot_general(left, right, (((1,), (1,)), ((), ())), preferred_element_type=F32)


def parts(value, count):
    out = []
    for _ in range(count):
        piece = value.astype(BF16)
        out.append(piece)
        value = value - piece.astype(F32)
    return out


def rows_and_columns(shape=(TOK, TOK)):
    return lax.broadcasted_iota(jnp.int32, shape, 0), lax.broadcasted_iota(jnp.int32, shape, 1)


def spread(rows_list, pattern, count):
    out = []
    for pair in range(0, len(rows_list), 2):
        chosen = rows_list[pair : pair + 2]
        wide = jnp.concatenate([jnp.broadcast_to(r, (128, TOK)) for r in chosen], axis=0)
        total = None
        for piece in parts(wide, count):
            term = mm_t(pattern, piece)
            total = term if total is None else total + term
        for k in range(len(chosen)):
            out.append(total[:, k * 128 : (k + 1) * 128])
    return out


def local_start(doc_ref):
    first = lax.axis_index("ctx") * TOK
    return jnp.maximum(doc_ref[...] - first, -TAPS).astype(F32)


def short_conv(ext_ref, x_ref, rim, w_ref, valid):
    width = x_ref.shape[1]
    own = x_ref[...].astype(F32)
    ext_ref[0:8, :width] = rim
    ext_ref[8 : 8 + TOK, :width] = own
    total = own * w_ref[0:1, :]
    for tap in range(1, TAPS):
        shifted = ext_ref[8 - tap : 8 - tap + TOK, :width]
        mask = jnp.concatenate([valid[tap - 1]] * (width // 128), axis=1)
        total = total + jnp.where(mask, shifted * w_ref[tap : tap + 1, :], 0.0)
    return total * jax.nn.sigmoid(total)


def tap_masks(start):
    token = lax.broadcasted_iota(jnp.int32, (TOK, 128), 0).astype(F32)
    return [start <= token - tap for tap in range(1, TAPS)]


def unit_keys(key_conv):
    out = []
    for g in range(GROUPS):
        k = key_conv[:, g * DK : (g + 1) * DK]
        out.append(k * lax.rsqrt(jnp.sum(k * k, axis=-1, keepdims=True) + EPS))
    return out


def fading(cum_col, cum_row, start, keep):
    gap = jnp.concatenate([cum_col, cum_col], axis=1) - cum_row
    return jnp.exp(jnp.where(keep, gap, FAR))


def linked_mask(start):
    row, col = rows_and_columns()
    begin = jnp.concatenate([start, start], axis=1)
    return (col <= row) & (begin <= col.astype(F32))


LEVELS = (8, 16, 32, 64)


def block_masks():
    row, col = rows_and_columns()
    out = []
    for size in LEVELS:
        shift = size.bit_length() - 1
        r, c = row >> shift, col >> shift
        out.append((r == c).astype(F32).astype(BF16))
        out.append(((r == c + 1) & ((c & 1) == 0)).astype(F32).astype(BF16))
    return out


def grow(compact, mask):
    if compact.shape[0] < 16:
        compact = jnp.concatenate([compact] * (16 // compact.shape[0]), axis=0)
    compact = compact.astype(BF16)
    return jnp.concatenate([compact] * (TOK // compact.shape[0]), axis=0) * mask


def high_low(value):
    high = value.astype(BF16).astype(F32)
    return high, value - high


def times(left, right, mask):
    size = left.shape[0]
    left_high, left_low = high_low(left)
    right_high, right_low = high_low(right)
    stacked = jnp.concatenate([left_high, left_low], axis=0).astype(BF16)
    total = mm(stacked, grow(right_high, mask))
    return total[:size] + total[size:] + mm(left_high.astype(BF16), grow(right_low, mask))


def gather_blocks(a, size, below):
    lane = lax.broadcasted_iota(jnp.int32, (size, 128), 1) >> (size.bit_length() - 1)
    out = []
    for half in range(2):
        total = None
        for k in range(128 // size):
            block = half * (128 // size) + k
            if below and block % 2:
                continue
            top = (block + (1 if below else 0)) * size
            piece = jnp.where(lane == k, a[top : top + size, half * 128 : half * 128 + 128], 0.0)
            total = piece if total is None else total + piece
        out.append(total)
    return jnp.concatenate(out, axis=1)


def each(fn, *lists):
    return [fn(*items) for items in zip(*lists)]


def half_inverses(many, masks):
    row, col = rows_and_columns((8, TOK))
    eye = ((col & 7) == row).astype(F32)
    d = each(lambda a: gather_blocks(a, 8, False), many)
    t = each(lambda d: eye - d, d)
    square = each(lambda d: times(d, d, masks[0]), d)
    both = each(lambda t, s: times(jnp.concatenate([t, s], axis=0), s, masks[0]), t, square)
    t = each(lambda t, b: t + b[:8], t, both)
    t = each(lambda t, b: t + times(t, b[8:], masks[0]), t, both)
    for i, size in enumerate(LEVELS):
        e = each(lambda a: gather_blocks(a, size, True), many)
        y = each(lambda e, t: times(e, t, masks[2 * i]), e, t)
        z = each(lambda t, y: times(t, y, masks[2 * i + 1]), t, y)
        lane = lax.broadcasted_iota(jnp.int32, (size, TOK), 1)
        left = ((lane >> (size.bit_length() - 1)) & 1) == 0
        t = each(
            lambda t, z: jnp.concatenate([jnp.where(left, t, 0.0), jnp.where(left, -z, t)], axis=0),
            t, z,
        )
    return t


def solve_halves(a, t, beta, right):
    scaled = each(lambda t, b: parts(t * b, 2), t, beta)
    plain = each(lambda t: parts(t[:, 128:], 2), t)
    cross = each(lambda a: parts(a[128:, :128], 2), a)
    first = each(
        lambda s, r: (mm(s[0][:, :128], r[:128]) + mm(s[1][:, :128], r[:128])).astype(BF16),
        scaled, right,
    )
    moved = each(lambda c, x: (mm(c[0], x) + mm(c[1], x)).astype(BF16), cross, first)
    second = each(
        lambda s, r, p, y: (
            mm(s[0][:, 128:], r[128:]) + mm(s[1][:, 128:], r[128:]) - mm(p[0], y) - mm(p[1], y)
        ).astype(BF16),
        scaled, right, plain, moved,
    )
    return each(lambda x, y: jnp.concatenate([x, y], axis=0), first, second)


def pack_kernel(k_ref, v_ref, q_ref, out_ref):
    out_ref[:, 0:256] = k_ref[...]
    out_ref[:, 256:768] = v_ref[...]
    out_ref[:, 768:1024] = q_ref[...]


def early_kernel(
    k_ref, v_ref, decay_ref, beta_ref, doc_ref, wk_ref, wv_ref,
    key_ref, value_ref, factor_ref, carry_ref, last_ref, start_ref, head_ref, mask_ref, ext_ref,
):
    row, col = rows_and_columns()
    lower = (col <= row).astype(BF16)
    eye = (col == row).astype(BF16)
    start = spread([local_start(doc_ref)], eye, 1)[0]
    start_ref[...] = start[0:RIM]
    decay = decay_ref[...]
    beta = beta_ref[...]
    cum_row = sum(mm_t(piece, lower) for piece in parts(decay, 3))
    cum_col = spread([decay[h : h + 1] for h in range(HEADS)], lower, 3)
    beta_col = spread([beta[h : h + 1] for h in range(HEADS)], eye, 2)
    keep = linked_mask(start)
    for h in range(HEADS):
        fade = fading(cum_col[h], cum_row[h : h + 1], start, keep)
        beta_wide = jnp.concatenate([beta_col[h], beta_col[h]], axis=1)
        factor_ref[h] = jnp.where(col < row, beta_wide * fade, 0.0)
        carry_ref[h] = jnp.where(start < 0.0, jnp.exp(cum_col[h]), 0.0)
        last_ref[h : h + 1] = fade[TOK - 1 : TOK, :]
    valid = tap_masks(start)
    key_conv = short_conv(ext_ref, k_ref, jnp.zeros((8, 256), F32), wk_ref, valid)
    for g, key in enumerate(unit_keys(key_conv)):
        key_ref[g] = key.astype(BF16)
    value_conv = short_conv(ext_ref, v_ref, jnp.zeros((8, 512), F32), wv_ref, valid)
    value_ref[...] = value_conv.astype(BF16)
    head_ref[:, 0:256] = k_ref[0:RIM, :]
    head_ref[:, 256:768] = v_ref[0:RIM, :]
    for i, mask in enumerate(block_masks()):
        mask_ref[i] = mask


def first_rows(rim, own, w_ref, start):
    width = own.shape[1]
    ext = jnp.concatenate([rim, own], axis=0)
    token = lax.broadcasted_iota(jnp.int32, (8, 128), 0).astype(F32)
    total = own * w_ref[0:1, :]
    for tap in range(1, TAPS):
        mask = jnp.concatenate([start <= token - tap] * (width // 128), axis=1)
        total = total + jnp.where(mask, ext[8 - tap : 16 - tap] * w_ref[tap : tap + 1, :], 0.0)
    return total * jax.nn.sigmoid(total)


def map_kernel(
    rim_ref, head_ref, start_ref, key_ref, value_ref, factor_ref, carry_ref, last_ref, beta_ref,
    wk_ref, wv_ref, mask_ref, wu_ref, kb_ref, own_ref, give_ref,
):
    rim = rim_ref[...].astype(F32)[8:16]
    head = head_ref[...].astype(F32)[0:8]
    start = start_ref[0:8]
    first_keys = unit_keys(first_rows(rim[:, 0:256], head[:, 0:256], wk_ref, start))
    first_values = first_rows(rim[:, 256:768], head[:, 256:768], wv_ref, start)

    def patched(first, whole):
        whole = whole.astype(F32)
        return jnp.concatenate([first, whole[8:]], axis=0)

    keys = [patched(first_keys[g], key_ref[g]).astype(BF16) for g in range(GROUPS)]
    values = patched(first_values, value_ref[...]).astype(BF16)
    beta = beta_ref[...]
    gram = [mm_t(k, k) for k in keys]
    flipped = [k.astype(F32).T for k in keys]
    core = lax.axis_index("ctx") % CORES
    for g in range(GROUPS):
        kb_ref[g] = keys[g]
    heads = range(HEADS)
    masks = [mask_ref[i] for i in range(2 * len(LEVELS))]
    a = [factor_ref[h] * gram[h // 2] for h in heads]
    inverses = half_inverses(a, masks)
    right = [
        jnp.concatenate(
            [
                (carry_ref[h] * keys[h // 2].astype(F32)).astype(BF16),
                values[:, h * DV : (h + 1) * DV],
            ],
            axis=1,
        )
        for h in heads
    ]
    solved = solve_halves(a, inverses, [beta[h : h + 1] for h in heads], right)
    faded = [(flipped[h // 2] * last_ref[h : h + 1, :]).astype(BF16) for h in heads]
    both = each(mm, faded, solved)
    r, c = rows_and_columns((DK, DK))
    for h in heads:
        wu_ref[h] = solved[h]
        decay = jnp.broadcast_to(carry_ref[h, TOK - 1 : TOK, :], (DK, DK))
        diagonal = jnp.where(r == c, decay, 0.0)
        step = jnp.concatenate([diagonal - both[h][:, :DK], both[h][:, DK:]], axis=1).astype(BF16)

        @pl.when(core == h // 2)
        def _():
            own_ref[h % 2] = step

        @pl.when(core != h // 2)
        def _():
            give_ref[h % 2] = step


def output_kernel(
    q_ref, rim_ref, decay_ref, doc_ref, wq_ref, kb_ref, wu_ref, out_ref, reach_ref, ext_ref
):
    row, col = rows_and_columns()
    lower = (col <= row).astype(BF16)
    eye = (col == row).astype(BF16)
    rim = rim_ref[...].astype(F32)[8:16]
    start = spread([local_start(doc_ref)], eye, 1)[0]
    query_conv = short_conv(ext_ref, q_ref, rim[:, 768:1024], wq_ref, tap_masks(start))
    decay = decay_ref[...]
    cum_row = sum(mm_t(piece, lower) for piece in parts(decay, 3))
    cum_col = spread([decay[h : h + 1] for h in range(HEADS)], lower, 3)
    keep = linked_mask(start)
    scores = []
    for g in range(GROUPS):
        query = query_conv[:, g * DK : (g + 1) * DK].astype(BF16)
        scores.append(mm_t(query, kb_ref[g]))
    for h in range(HEADS):
        g = h // 2
        fade = fading(cum_col[h], cum_row[h : h + 1], start, keep)
        both = mm((fade * scores[g]).astype(BF16), wu_ref[h])
        carry = jnp.where(start < 0.0, jnp.exp(cum_col[h]), 0.0)
        reach = carry * query_conv[:, g * DK : (g + 1) * DK] - both[:, :DK]
        reach_ref[h] = reach.astype(BF16)
        out_ref[h] = both[:, DK:]


def joined(first, later):
    moved = mm(later[:, :DK], first)
    return jnp.concatenate([moved[:, :DK], moved[:, DK:] + later[:, DK:].astype(F32)], axis=1)


def pair_kernel(own_ref, got_ref, out_ref):
    core = lax.axis_index("ctx") % CORES
    for k in range(2):
        own = own_ref[k]
        got = got_ref[k]
        first = jnp.where(core == 0, own, got)
        later = jnp.where(core == 0, got, own)
        out_ref[k] = joined(first, later).astype(BF16)


def row_kernel(own_ref, one_ref, two_ref, three_ref, after_ref, before_ref, total_ref, slots):
    x = (lax.axis_index("ctx") // CORES) % CHIPS_X
    for step, ref in enumerate((own_ref, one_ref, two_ref, three_ref)):
        slots[(x + CHIPS_X - step) % CHIPS_X] = ref[...]
    r, c = rows_and_columns((DK, DK + DV))
    start = (r == c).astype(BF16)
    run = [slots[0, k] for k in range(2)]
    before = [jnp.where(x == 0, start, first) for first in run]
    for place in range(1, CHIPS_X):
        run = [joined(run[k], slots[place, k]).astype(BF16) for k in range(2)]
        if place < CHIPS_X - 1:
            before = [jnp.where(x == place + 1, run[k], before[k]) for k in range(2)]
    for k in range(2):
        total_ref[k] = run[k]
        before_ref[k] = before[k]


def state_kernel(
    own_ref, one_ref, two_ref, three_ref, before_ref, mine_ref, other_ref, keep_ref, give_ref, slots
):
    index = lax.axis_index("ctx")
    core = index % CORES
    y = index // (CORES * CHIPS_X)
    for step, ref in enumerate((own_ref, one_ref, two_ref, three_ref)):
        slots[(y + CHIPS_Y - step) % CHIPS_Y] = ref[...]

    def passed(block, state):
        return mm(block[:, :DK], state.astype(BF16)) + block[:, DK:].astype(F32)

    states = [jnp.where(y > 0, slots[0, k][:, DK:].astype(F32), 0.0) for k in range(2)]
    for place in range(1, CHIPS_Y - 1):
        moved = [passed(slots[place, k], states[k]) for k in range(2)]
        states = [jnp.where(place < y, moved[k], states[k]) for k in range(2)]
    states = [passed(before_ref[k], states[k]) for k in range(2)]
    blocks = [jnp.where(core == 0, mine_ref[k], other_ref[k]) for k in range(2)]
    after = [passed(blocks[k], states[k]) for k in range(2)]
    for k in range(2):
        keep_ref[k] = jnp.where(core == 0, states[k], after[k]).astype(BF16)
        give_ref[k] = jnp.where(core == 0, after[k], states[k]).astype(BF16)


KEPT = (0, -3, 2)
TO_AHEAD = (1, -2, 3)
TO_BEHIND = (-1, -4)


def mirrored(step):
    return [
        (ctx * 8 + z, ctx * 8 + (z + (-step if ctx % CORES else step)) % 8)
        for ctx in range(CTX)
        for z in range(8)
    ]


def norm_kernel(
    local_ref, reach_ref, mine_ref, got_ref, gate_ref, gain_ref, keep_ref, ahead_ref, behind_ref, normed_ref
):
    core = lax.axis_index("ctx") % CORES
    place = lax.axis_index("head")
    for h in range(HEADS):
        state = jnp.where(core == h // 2, mine_ref[h % 2], got_ref[h % 2])
        heads = local_ref[h] + mm(reach_ref[h], state)
        inv = lax.rsqrt(jnp.mean(heads * heads, axis=-1, keepdims=True) + EPS)
        gate = gate_ref[:, h * DV : (h + 1) * DV].astype(F32)
        gate = gate * jax.nn.sigmoid(gate)
        normed_ref[:, h * DV : (h + 1) * DV] = (heads * inv * gain_ref[...] * gate).astype(BF16)
    rows = TOK // 8
    sign = 1 - 2 * core
    for steps, ref in ((KEPT, keep_ref), (TO_AHEAD, ahead_ref), (TO_BEHIND, behind_ref)):
        for k, step in enumerate(steps):
            top = pl.multiple_of(((place + sign * step + 8) % 8) * rows, rows)
            ref[k * rows : (k + 1) * rows, :] = normed_ref[pl.ds(top, rows), :]


def project_kernel(keep_ref, behind_ref, ahead_ref, own_ref, behind_w_ref, ahead_w_ref, *out_refs):
    keep = keep_ref[...]
    behind = behind_ref[...]
    ahead = ahead_ref[...]
    none = jnp.zeros((behind.shape[0] - ahead.shape[0], ahead.shape[1]), BF16)
    ahead = jnp.concatenate([ahead, none], axis=0)
    rows = TOK // 8
    for part in range(0, own_ref.shape[1], 512):
        at = slice(part, part + 512)
        total = (
            mm(keep, own_ref[:, at]) + mm(behind, behind_w_ref[:, at]) + mm(ahead, ahead_w_ref[:, at])
        )
        for k, out_ref in enumerate(out_refs):
            out_ref[:, at] = total[k * rows : (k + 1) * rows].astype(out_ref.dtype)


def sum_kernel(own_ref, one_ref, two_ref, out_ref):
    total = own_ref[...]
    for ref in (one_ref, two_ref):
        total = total + ref[...].astype(F32)
    out_ref[...] = total.astype(BF16)


VMEM = pl.BlockSpec(memory_space=pltpu.VMEM)
HBM = pl.BlockSpec(memory_space=pltpu.HBM)


def whole(shape):
    return pl.BlockSpec(shape, lambda i: (0,) * len(shape))


def call(
    kernel, outs, inputs, scratch=(), flops=0, moved=0, limit=32, specs=None, out_specs=None,
    blocked=False,
):
    if blocked:
        specs = [whole(a.shape) for a in inputs]
        out_specs = [whole(s) for s, _ in outs]
    return pl.pallas_call(
        kernel,
        grid=(1,) if blocked else (),
        out_shape=[jax.ShapeDtypeStruct(s, t) for s, t in outs],
        in_specs=[VMEM] * len(inputs) if specs is None else specs,
        out_specs=[VMEM] * len(outs) if out_specs is None else out_specs,
        scratch_shapes=list(scratch),
        compiler_params=pltpu.CompilerParams(vmem_limit_bytes=limit * MIB),
        cost_estimate=pl.CostEstimate(flops=flops, bytes_accessed=moved, transcendentals=0),
    )(*inputs)


def on_device(
    query_in, key_in, value_in, out_gate, log_decay, beta_gate, doc_start,
    conv_query, conv_key, conv_value, norm_gain, out_weight,
):
    doc_row = doc_start.reshape(1, TOK)
    gain_row = norm_gain.reshape(1, DV)
    width = out_weight.shape[1]
    last = TOK // RIM - 1
    edge = pl.pallas_call(
        pack_kernel,
        grid=(1,),
        out_shape=jax.ShapeDtypeStruct((RIM, 1024), BF16),
        in_specs=[pl.BlockSpec((RIM, n), lambda i: (last, 0)) for n in (256, 512, 256)],
        out_specs=pl.BlockSpec((RIM, 1024), lambda i: (0, 0)),
        cost_estimate=pl.CostEstimate(flops=5_000_000_000, bytes_accessed=0, transcendentals=0),
    )(key_in, value_in, query_in)
    near_weight = lax.ppermute(
        lax.optimization_barrier((out_weight, edge))[0], ("ctx", "head"), mirrored(1)
    )
    rim = lax.ppermute(edge, "ctx", [(i, (i + 1) % CTX) for i in range(CTX)])
    wide = (2, DK, DK + DV)
    early = call(
        early_kernel,
        [
            ((GROUPS, TOK, DK), BF16), ((TOK, HEADS * DV), BF16), ((HEADS, TOK, TOK), F32),
            ((HEADS, TOK, 128), F32), ((HEADS, TOK), F32), ((RIM, 128), F32), ((RIM, 768), BF16),
            ((2 * len(LEVELS), TOK, TOK), BF16),
        ],
        [key_in, value_in, log_decay, beta_gate, doc_row, conv_key, conv_value],
        [
            pltpu.VMEM((8 + TOK, 512), F32),
        ],
        flops=500_000_000, moved=0, limit=48, blocked=True,
    )
    keys, values, factor, carry, final, start, head, masks = early
    solved, keys, own, give = call(
        map_kernel,
        [((HEADS, TOK, DK + DV), BF16), ((GROUPS, TOK, DK), BF16), (wide, BF16), (wide, BF16)],
        [rim, head, start, keys, values, factor, carry, final, beta_gate, conv_key, conv_value, masks],
        flops=4_000_000_000, moved=2_000_000,
    )
    other = lax.ppermute(give, "ctx", core_swap())
    (pair,) = call(pair_kernel, [(wide, BF16)], [own, other], flops=20_000_000, moved=400_000)
    near = [lax.ppermute(pair, "ctx", along_x(k)) for k in (1, 2, 3)]
    local, reach = call(
        output_kernel,
        [((HEADS, TOK, DV), F32), ((HEADS, TOK, DK), BF16)],
        [query_in, rim, log_decay, doc_row, conv_query, keys, solved],
        [pltpu.VMEM((8 + TOK, 256), F32)],
        flops=2_000_000_000, moved=2_000_000,
    )
    before, total = call(
        row_kernel, [(wide, BF16), (wide, BF16)], [pair] + near + [reach],
        [pltpu.VMEM((CHIPS_X,) + wide, BF16)], flops=60_000_000, moved=800_000,
        specs=[VMEM] * 4 + [HBM],
    )
    far = [lax.ppermute(total, "ctx", along_y(k)) for k in (1, 2, 3)]
    narrow = (2, DK, DV)
    mine, to_other = call(
        state_kernel, [(narrow, BF16), (narrow, BF16)], [total] + far + [before, own, other],
        [pltpu.VMEM((CHIPS_Y,) + wide, BF16)], flops=60_000_000, moved=1_000_000,
    )
    got = lax.ppermute(to_other, "ctx", core_swap())
    late_weight, _ = lax.optimization_barrier((near_weight, got))
    far_weight = lax.ppermute(late_weight, "ctx", core_swap())
    block = TOK // 8

    def normed_rows(steps):
        return ((len(steps) * block, HEADS * DV), BF16)

    keep, to_ahead, to_behind = call(
        norm_kernel, [normed_rows(KEPT), normed_rows(TO_AHEAD), normed_rows(TO_BEHIND)],
        [local, reach, mine, got, out_gate, gain_row],
        [pltpu.VMEM((TOK, HEADS * DV), BF16)],
        flops=100_000_000, moved=1_500_000,
    )
    from_behind = lax.ppermute(to_ahead, ("ctx", "head"), mirrored(1))
    from_ahead = lax.ppermute(to_behind, ("ctx", "head"), mirrored(-1))
    own_part, far_part, near_part = call(
        project_kernel, [((block, width), F32)] + [((block, width), BF16)] * 2,
        [keep, from_behind, from_ahead, out_weight, near_weight, far_weight],
        flops=600_000_000, moved=6_000_000,
    )
    far_part = lax.ppermute(far_part, ("ctx", "head"), mirrored(-3))
    near_part = lax.ppermute(near_part, ("ctx", "head"), mirrored(2))
    (mixed,) = call(
        sum_kernel, [((block, width), BF16)], [own_part, far_part, near_part],
        flops=1_000_000, moved=800_000,
    )
    return mixed


def solution(mesh):
    placed = (
        P("ctx", "head"),
        P("ctx", "head"),
        P("ctx", "head"),
        P("ctx", "head"),
        P("head", "ctx"),
        P("head", "ctx"),
        P("ctx"),
        P(None, "head"),
        P(None, "head"),
        P(None, "head"),
        P(),
        P("head", None),
    )
    return jax.shard_map(
        on_device, mesh=mesh, in_specs=placed, out_specs=P(("ctx", "head"), None), check_vma=False
    )
```

```python
import jax
import jax.numpy as jnp
from jax import lax
from jax.experimental import pallas as pl
from jax.experimental.pallas import tpu as pltpu
from jax.sharding import PartitionSpec as P

DK = 128
DV = 128
TOK = 256
HEADS = 4
GROUPS = 2
TAPS = 4
RIM = 16
EPS = 1e-6
F32 = jnp.float32
BF16 = jnp.bfloat16
FAR = -1e30
MIB = 1 << 20

CTX = 32
CORES = 2
CHIPS_X = 4
CHIPS_Y = 4


def core_swap():
    return [(i, i ^ 1) for i in range(CTX)]


def along_x(step):
    return [
        ((y * 4 + x) * 2 + c, (y * 4 + (x + step) % 4) * 2 + c)
        for y in range(4)
        for x in range(4)
        for c in range(2)
    ]


def along_y(step):
    return [
        ((y * 4 + x) * 2 + c, (((y + step) % 4) * 4 + x) * 2 + c)
        for y in range(4)
        for x in range(4)
        for c in range(2)
    ]


def mm(left, right):
    return jnp.dot(left, right, preferred_element_type=F32)


def mm_t(left, right):
    return lax.dot_general(left, right, (((1,), (1,)), ((), ())), preferred_element_type=F32)


def parts(value, count):
    out = []
    for _ in range(count):
        piece = value.astype(BF16)
        out.append(piece)
        value = value - piece.astype(F32)
    return out


def rows_and_columns(shape=(TOK, TOK)):
    return lax.broadcasted_iota(jnp.int32, shape, 0), lax.broadcasted_iota(jnp.int32, shape, 1)


def spread(rows_list, pattern, count):
    out = []
    for pair in range(0, len(rows_list), 2):
        chosen = rows_list[pair : pair + 2]
        wide = jnp.concatenate([jnp.broadcast_to(r, (128, TOK)) for r in chosen], axis=0)
        total = None
        for piece in parts(wide, count):
            term = mm_t(pattern, piece)
            total = term if total is None else total + term
        for k in range(len(chosen)):
            out.append(total[:, k * 128 : (k + 1) * 128])
    return out


def local_start(doc_ref):
    first = lax.axis_index("ctx") * TOK
    return jnp.maximum(doc_ref[...] - first, -TAPS).astype(F32)


def short_conv(ext_ref, x_ref, rim, w_ref, valid):
    width = x_ref.shape[1]
    own = x_ref[...].astype(F32)
    ext_ref[0:8, :width] = rim
    ext_ref[8 : 8 + TOK, :width] = own
    total = own * w_ref[0:1, :]
    for tap in range(1, TAPS):
        shifted = ext_ref[8 - tap : 8 - tap + TOK, :width]
        mask = jnp.concatenate([valid[tap - 1]] * (width // 128), axis=1)
        total = total + jnp.where(mask, shifted * w_ref[tap : tap + 1, :], 0.0)
    return total * jax.nn.sigmoid(total)


def tap_masks(start):
    token = lax.broadcasted_iota(jnp.int32, (TOK, 128), 0).astype(F32)
    return [start <= token - tap for tap in range(1, TAPS)]


def unit_keys(key_conv):
    out = []
    for g in range(GROUPS):
        k = key_conv[:, g * DK : (g + 1) * DK]
        out.append(k * lax.rsqrt(jnp.sum(k * k, axis=-1, keepdims=True) + EPS))
    return out


def fading(cum_col, cum_row, start, keep):
    gap = jnp.concatenate([cum_col, cum_col], axis=1) - cum_row
    return jnp.exp(jnp.where(keep, gap, FAR))


def linked_mask(start):
    row, col = rows_and_columns()
    begin = jnp.concatenate([start, start], axis=1)
    return (col <= row) & (begin <= col.astype(F32))


LEVELS = (8, 16, 32, 64)


def block_masks():
    row, col = rows_and_columns()
    out = []
    for size in LEVELS:
        shift = size.bit_length() - 1
        r, c = row >> shift, col >> shift
        out.append((r == c).astype(F32).astype(BF16))
        out.append(((r == c + 1) & ((c & 1) == 0)).astype(F32).astype(BF16))
    return out


def grow(compact, mask):
    if compact.shape[0] < 16:
        compact = jnp.concatenate([compact] * (16 // compact.shape[0]), axis=0)
    compact = compact.astype(BF16)
    return jnp.concatenate([compact] * (TOK // compact.shape[0]), axis=0) * mask


def high_low(value):
    high = value.astype(BF16).astype(F32)
    return high, value - high


def times(left, right, mask):
    size = left.shape[0]
    left_high, left_low = high_low(left)
    right_high, right_low = high_low(right)
    stacked = jnp.concatenate([left_high, left_low], axis=0).astype(BF16)
    total = mm(stacked, grow(right_high, mask))
    return total[:size] + total[size:] + mm(left_high.astype(BF16), grow(right_low, mask))


def gather_blocks(a, size, below):
    lane = lax.broadcasted_iota(jnp.int32, (size, 128), 1) >> (size.bit_length() - 1)
    out = []
    for half in range(2):
        total = None
        for k in range(128 // size):
            block = half * (128 // size) + k
            if below and block % 2:
                continue
            top = (block + (1 if below else 0)) * size
            piece = jnp.where(lane == k, a[top : top + size, half * 128 : half * 128 + 128], 0.0)
            total = piece if total is None else total + piece
        out.append(total)
    return jnp.concatenate(out, axis=1)


def each(fn, *lists):
    return [fn(*items) for items in zip(*lists)]


def half_inverses(many, masks):
    row, col = rows_and_columns((8, TOK))
    eye = ((col & 7) == row).astype(F32)
    d = each(lambda a: gather_blocks(a, 8, False), many)
    t = each(lambda d: eye - d, d)
    square = each(lambda d: times(d, d, masks[0]), d)
    both = each(lambda t, s: times(jnp.concatenate([t, s], axis=0), s, masks[0]), t, square)
    t = each(lambda t, b: t + b[:8], t, both)
    t = each(lambda t, b: t + times(t, b[8:], masks[0]), t, both)
    for i, size in enumerate(LEVELS):
        e = each(lambda a: gather_blocks(a, size, True), many)
        y = each(lambda e, t: times(e, t, masks[2 * i]), e, t)
        z = each(lambda t, y: times(t, y, masks[2 * i + 1]), t, y)
        lane = lax.broadcasted_iota(jnp.int32, (size, TOK), 1)
        left = ((lane >> (size.bit_length() - 1)) & 1) == 0
        t = each(
            lambda t, z: jnp.concatenate([jnp.where(left, t, 0.0), jnp.where(left, -z, t)], axis=0),
            t, z,
        )
    return t


def solve_halves(a, t, beta, right):
    scaled = each(lambda t, b: parts(t * b, 2), t, beta)
    plain = each(lambda t: parts(t[:, 128:], 2), t)
    cross = each(lambda a: parts(a[128:, :128], 2), a)
    first = each(
        lambda s, r: (mm(s[0][:, :128], r[:128]) + mm(s[1][:, :128], r[:128])).astype(BF16),
        scaled, right,
    )
    moved = each(lambda c, x: (mm(c[0], x) + mm(c[1], x)).astype(BF16), cross, first)
    second = each(
        lambda s, r, p, y: (
            mm(s[0][:, 128:], r[128:]) + mm(s[1][:, 128:], r[128:]) - mm(p[0], y) - mm(p[1], y)
        ).astype(BF16),
        scaled, right, plain, moved,
    )
    return each(lambda x, y: jnp.concatenate([x, y], axis=0), first, second)


def pack_kernel(k_ref, v_ref, q_ref, out_ref):
    out_ref[:, 0:256] = k_ref[...]
    out_ref[:, 256:768] = v_ref[...]
    out_ref[:, 768:1024] = q_ref[...]


def early_kernel(
    k_ref, v_ref, decay_ref, beta_ref, doc_ref, wk_ref, wv_ref,
    key_ref, value_ref, factor_ref, carry_ref, last_ref, start_ref, head_ref, mask_ref, ext_ref,
):
    row, col = rows_and_columns()
    lower = (col <= row).astype(BF16)
    eye = (col == row).astype(BF16)
    start = spread([local_start(doc_ref)], eye, 1)[0]
    start_ref[...] = start[0:RIM]
    decay = decay_ref[...]
    beta = beta_ref[...]
    cum_row = sum(mm_t(piece, lower) for piece in parts(decay, 3))
    cum_col = spread([decay[h : h + 1] for h in range(HEADS)], lower, 3)
    beta_col = spread([beta[h : h + 1] for h in range(HEADS)], eye, 2)
    keep = linked_mask(start)
    for h in range(HEADS):
        fade = fading(cum_col[h], cum_row[h : h + 1], start, keep)
        beta_wide = jnp.concatenate([beta_col[h], beta_col[h]], axis=1)
        factor_ref[h] = jnp.where(col < row, beta_wide * fade, 0.0)
        carry_ref[h] = jnp.where(start < 0.0, jnp.exp(cum_col[h]), 0.0)
        last_ref[h : h + 1] = fade[TOK - 1 : TOK, :]
    valid = tap_masks(start)
    key_conv = short_conv(ext_ref, k_ref, jnp.zeros((8, 256), F32), wk_ref, valid)
    for g, key in enumerate(unit_keys(key_conv)):
        key_ref[g] = key.astype(BF16)
    value_conv = short_conv(ext_ref, v_ref, jnp.zeros((8, 512), F32), wv_ref, valid)
    value_ref[...] = value_conv.astype(BF16)
    head_ref[:, 0:256] = k_ref[0:RIM, :]
    head_ref[:, 256:768] = v_ref[0:RIM, :]
    for i, mask in enumerate(block_masks()):
        mask_ref[i] = mask


def first_rows(rim, own, w_ref, start):
    width = own.shape[1]
    ext = jnp.concatenate([rim, own], axis=0)
    token = lax.broadcasted_iota(jnp.int32, (8, 128), 0).astype(F32)
    total = own * w_ref[0:1, :]
    for tap in range(1, TAPS):
        mask = jnp.concatenate([start <= token - tap] * (width // 128), axis=1)
        total = total + jnp.where(mask, ext[8 - tap : 16 - tap] * w_ref[tap : tap + 1, :], 0.0)
    return total * jax.nn.sigmoid(total)


def map_kernel(
    rim_ref, head_ref, start_ref, key_ref, value_ref, factor_ref, carry_ref, last_ref, beta_ref,
    wk_ref, wv_ref, mask_ref, wu_ref, kb_ref, own_ref, give_ref,
):
    rim = rim_ref[...].astype(F32)[8:16]
    head = head_ref[...].astype(F32)[0:8]
    start = start_ref[0:8]
    first_keys = unit_keys(first_rows(rim[:, 0:256], head[:, 0:256], wk_ref, start))
    first_values = first_rows(rim[:, 256:768], head[:, 256:768], wv_ref, start)

    def patched(first, whole):
        whole = whole.astype(F32)
        return jnp.concatenate([first, whole[8:]], axis=0)

    keys = [patched(first_keys[g], key_ref[g]).astype(BF16) for g in range(GROUPS)]
    values = patched(first_values, value_ref[...]).astype(BF16)
    beta = beta_ref[...]
    gram = [mm_t(k, k) for k in keys]
    flipped = [k.astype(F32).T for k in keys]
    core = lax.axis_index("ctx") % CORES
    for g in range(GROUPS):
        kb_ref[g] = keys[g]
    heads = range(HEADS)
    masks = [mask_ref[i] for i in range(2 * len(LEVELS))]
    a = [factor_ref[h] * gram[h // 2] for h in heads]
    inverses = half_inverses(a, masks)
    right = [
        jnp.concatenate(
            [
                (carry_ref[h] * keys[h // 2].astype(F32)).astype(BF16),
                values[:, h * DV : (h + 1) * DV],
            ],
            axis=1,
        )
        for h in heads
    ]
    solved = solve_halves(a, inverses, [beta[h : h + 1] for h in heads], right)
    faded = [(flipped[h // 2] * last_ref[h : h + 1, :]).astype(BF16) for h in heads]
    both = each(mm, faded, solved)
    r, c = rows_and_columns((DK, DK))
    for h in heads:
        wu_ref[h] = solved[h]
        decay = jnp.broadcast_to(carry_ref[h, TOK - 1 : TOK, :], (DK, DK))
        diagonal = jnp.where(r == c, decay, 0.0)
        step = jnp.concatenate([diagonal - both[h][:, :DK], both[h][:, DK:]], axis=1).astype(BF16)

        @pl.when(core == h // 2)
        def _():
            own_ref[h % 2] = step

        @pl.when(core != h // 2)
        def _():
            give_ref[h % 2] = step


def output_kernel(
    q_ref, rim_ref, decay_ref, doc_ref, wq_ref, kb_ref, wu_ref, out_ref, reach_ref, ext_ref
):
    row, col = rows_and_columns()
    lower = (col <= row).astype(BF16)
    eye = (col == row).astype(BF16)
    rim = rim_ref[...].astype(F32)[8:16]
    start = spread([local_start(doc_ref)], eye, 1)[0]
    query_conv = short_conv(ext_ref, q_ref, rim[:, 768:1024], wq_ref, tap_masks(start))
    decay = decay_ref[...]
    cum_row = sum(mm_t(piece, lower) for piece in parts(decay, 3))
    cum_col = spread([decay[h : h + 1] for h in range(HEADS)], lower, 3)
    keep = linked_mask(start)
    scores = []
    for g in range(GROUPS):
        query = query_conv[:, g * DK : (g + 1) * DK].astype(BF16)
        scores.append(mm_t(query, kb_ref[g]))
    for h in range(HEADS):
        g = h // 2
        fade = fading(cum_col[h], cum_row[h : h + 1], start, keep)
        both = mm((fade * scores[g]).astype(BF16), wu_ref[h])
        carry = jnp.where(start < 0.0, jnp.exp(cum_col[h]), 0.0)
        reach = carry * query_conv[:, g * DK : (g + 1) * DK] - both[:, :DK]
        reach_ref[h] = reach.astype(BF16)
        out_ref[h] = both[:, DK:]


def joined(first, later):
    moved = mm(later[:, :DK], first)
    return jnp.concatenate([moved[:, :DK], moved[:, DK:] + later[:, DK:].astype(F32)], axis=1)


def pair_kernel(own_ref, got_ref, out_ref):
    core = lax.axis_index("ctx") % CORES
    for k in range(2):
        own = own_ref[k]
        got = got_ref[k]
        first = jnp.where(core == 0, own, got)
        later = jnp.where(core == 0, got, own)
        out_ref[k] = joined(first, later).astype(BF16)


def row_kernel(own_ref, one_ref, two_ref, three_ref, after_ref, before_ref, total_ref, alone_ref, slots):
    x = (lax.axis_index("ctx") // CORES) % CHIPS_X
    for step, ref in enumerate((own_ref, one_ref, two_ref, three_ref)):
        slots[(x + CHIPS_X - step) % CHIPS_X] = ref[...]
    r, c = rows_and_columns((DK, DK + DV))
    start = (r == c).astype(BF16)
    run = [slots[0, k] for k in range(2)]
    before = [jnp.where(x == 0, start, first) for first in run]
    for place in range(1, CHIPS_X):
        run = [joined(run[k], slots[place, k]).astype(BF16) for k in range(2)]
        if place < CHIPS_X - 1:
            before = [jnp.where(x == place + 1, run[k], before[k]) for k in range(2)]
    for k in range(2):
        total_ref[k] = run[k]
        alone_ref[k] = run[k][:, DK:]
        before_ref[k] = before[k]


def state_kernel(
    own_ref, one_ref, two_ref, three_ref, before_ref, mine_ref, other_ref, keep_ref, give_ref, slots
):
    index = lax.axis_index("ctx")
    core = index % CORES
    y = index // (CORES * CHIPS_X)
    for step, ref in enumerate((own_ref, one_ref, two_ref)):
        slots[(y + CHIPS_Y - step) % CHIPS_Y] = ref[...]
    slots[(y + 1) % CHIPS_Y, :, :, DK:] = three_ref[...]

    def passed(block, state):
        return mm(block[:, :DK], state.astype(BF16)) + block[:, DK:].astype(F32)

    states = [jnp.where(y > 0, slots[0, k][:, DK:].astype(F32), 0.0) for k in range(2)]
    for place in range(1, CHIPS_Y - 1):
        moved = [passed(slots[place, k], states[k]) for k in range(2)]
        states = [jnp.where(place < y, moved[k], states[k]) for k in range(2)]
    states = [passed(before_ref[k], states[k]) for k in range(2)]
    blocks = [jnp.where(core == 0, mine_ref[k], other_ref[k]) for k in range(2)]
    after = [passed(blocks[k], states[k]) for k in range(2)]
    for k in range(2):
        keep_ref[k] = jnp.where(core == 0, states[k], after[k]).astype(BF16)
        give_ref[k] = jnp.where(core == 0, after[k], states[k]).astype(BF16)


KEPT = (0, -3, 2)
TO_AHEAD = (1, -2, 3)
TO_BEHIND = (-1, -4)


def mirrored(step):
    return [
        (ctx * 8 + z, ctx * 8 + (z + (-step if ctx % CORES else step)) % 8)
        for ctx in range(CTX)
        for z in range(8)
    ]


def norm_kernel(
    local_ref, reach_ref, mine_ref, got_ref, gate_ref, gain_ref, keep_ref, ahead_ref, behind_ref, normed_ref
):
    core = lax.axis_index("ctx") % CORES
    place = lax.axis_index("head")
    for h in range(HEADS):
        state = jnp.where(core == h // 2, mine_ref[h % 2], got_ref[h % 2])
        heads = local_ref[h] + mm(reach_ref[h], state)
        inv = lax.rsqrt(jnp.mean(heads * heads, axis=-1, keepdims=True) + EPS)
        gate = gate_ref[:, h * DV : (h + 1) * DV].astype(F32)
        gate = gate * jax.nn.sigmoid(gate)
        normed_ref[:, h * DV : (h + 1) * DV] = (heads * inv * gain_ref[...] * gate).astype(BF16)
    rows = TOK // 8
    sign = 1 - 2 * core
    for steps, ref in ((KEPT, keep_ref), (TO_AHEAD, ahead_ref), (TO_BEHIND, behind_ref)):
        for k, step in enumerate(steps):
            top = pl.multiple_of(((place + sign * step + 8) % 8) * rows, rows)
            ref[k * rows : (k + 1) * rows, :] = normed_ref[pl.ds(top, rows), :]


def keep_kernel(keep_ref, weight_ref, out_ref):
    keep = keep_ref[...]
    for part in range(0, weight_ref.shape[1], 512):
        out_ref[:, part : part + 512] = mm(keep, weight_ref[:, part : part + 512])


def remote_kernel(kept_ref, behind_ref, ahead_ref, behind_w_ref, ahead_w_ref, far_ref, near_ref):
    rows = TOK // 8
    behind = behind_ref[rows:, :]
    ahead = ahead_ref[rows:, :]
    for part in range(0, kept_ref.shape[1], 512):
        at = slice(part, part + 512)
        total = kept_ref[rows:, at] + mm(behind, behind_w_ref[:, at])
        far_ref[:, at] = (total[:rows] + mm(ahead, ahead_w_ref[:, at])).astype(BF16)
        near_ref[:, at] = total[rows:].astype(BF16)


def own_kernel(kept_ref, behind_ref, ahead_ref, behind_w_ref, ahead_w_ref, out_ref):
    rows = TOK // 8
    behind = behind_ref[:rows, :]
    ahead = ahead_ref[:rows, :]
    for part in range(0, kept_ref.shape[1], 512):
        at = slice(part, part + 512)
        total = kept_ref[:rows, at] + mm(behind, behind_w_ref[:, at])
        out_ref[:, at] = total + mm(ahead, ahead_w_ref[:, at])


def sum_kernel(own_ref, one_ref, two_ref, out_ref):
    total = own_ref[...]
    for ref in (one_ref, two_ref):
        total = total + ref[...].astype(F32)
    out_ref[...] = total.astype(BF16)


VMEM = pl.BlockSpec(memory_space=pltpu.VMEM)
HBM = pl.BlockSpec(memory_space=pltpu.HBM)


def whole(shape):
    return pl.BlockSpec(shape, lambda i: (0,) * len(shape))


def call(
    kernel, outs, inputs, scratch=(), flops=0, moved=0, limit=32, specs=None, out_specs=None,
    blocked=False,
):
    if blocked:
        specs = [whole(a.shape) for a in inputs]
        out_specs = [whole(s) for s, _ in outs]
    return pl.pallas_call(
        kernel,
        grid=(1,) if blocked else (),
        out_shape=[jax.ShapeDtypeStruct(s, t) for s, t in outs],
        in_specs=[VMEM] * len(inputs) if specs is None else specs,
        out_specs=[VMEM] * len(outs) if out_specs is None else out_specs,
        scratch_shapes=list(scratch),
        compiler_params=pltpu.CompilerParams(vmem_limit_bytes=limit * MIB),
        cost_estimate=pl.CostEstimate(flops=flops, bytes_accessed=moved, transcendentals=0),
    )(*inputs)


def on_device(
    query_in, key_in, value_in, out_gate, log_decay, beta_gate, doc_start,
    conv_query, conv_key, conv_value, norm_gain, out_weight,
):
    doc_row = doc_start.reshape(1, TOK)
    gain_row = norm_gain.reshape(1, DV)
    width = out_weight.shape[1]
    last = TOK // RIM - 1
    edge = pl.pallas_call(
        pack_kernel,
        grid=(1,),
        out_shape=jax.ShapeDtypeStruct((RIM, 1024), BF16),
        in_specs=[pl.BlockSpec((RIM, n), lambda i: (last, 0)) for n in (256, 512, 256)],
        out_specs=pl.BlockSpec((RIM, 1024), lambda i: (0, 0)),
        cost_estimate=pl.CostEstimate(flops=5_000_000_000, bytes_accessed=0, transcendentals=0),
    )(key_in, value_in, query_in)
    near_weight = lax.ppermute(
        lax.optimization_barrier((out_weight, edge))[0], ("ctx", "head"), mirrored(1)
    )
    rim = lax.ppermute(edge, "ctx", [(i, (i + 1) % CTX) for i in range(CTX)])
    wide = (2, DK, DK + DV)
    early = call(
        early_kernel,
        [
            ((GROUPS, TOK, DK), BF16), ((TOK, HEADS * DV), BF16), ((HEADS, TOK, TOK), F32),
            ((HEADS, TOK, 128), F32), ((HEADS, TOK), F32), ((RIM, 128), F32), ((RIM, 768), BF16),
            ((2 * len(LEVELS), TOK, TOK), BF16),
        ],
        [key_in, value_in, log_decay, beta_gate, doc_row, conv_key, conv_value],
        [
            pltpu.VMEM((8 + TOK, 512), F32),
        ],
        flops=500_000_000, moved=0, limit=48, blocked=True,
    )
    keys, values, factor, carry, final, start, head, masks = early
    solved, keys, own, give = call(
        map_kernel,
        [((HEADS, TOK, DK + DV), BF16), ((GROUPS, TOK, DK), BF16), (wide, BF16), (wide, BF16)],
        [rim, head, start, keys, values, factor, carry, final, beta_gate, conv_key, conv_value, masks],
        flops=4_000_000_000, moved=2_000_000,
    )
    other = lax.ppermute(give, "ctx", core_swap())
    (pair,) = call(pair_kernel, [(wide, BF16)], [own, other], flops=20_000_000, moved=400_000)
    near = [lax.ppermute(pair, "ctx", along_x(k)) for k in (1, 2, 3)]
    local, reach = call(
        output_kernel,
        [((HEADS, TOK, DV), F32), ((HEADS, TOK, DK), BF16)],
        [query_in, rim, log_decay, doc_row, conv_query, keys, solved],
        [pltpu.VMEM((8 + TOK, 256), F32)],
        flops=2_000_000_000, moved=2_000_000,
    )
    narrow = (2, DK, DV)
    before, total, alone = call(
        row_kernel, [(wide, BF16), (wide, BF16), (narrow, BF16)], [pair] + near + [reach],
        [pltpu.VMEM((CHIPS_X,) + wide, BF16)], flops=60_000_000, moved=800_000,
        specs=[VMEM] * 4 + [HBM],
    )
    far = [
        lax.ppermute(total, "ctx", along_y(1)),
        lax.ppermute(total, "ctx", along_y(2)),
        lax.ppermute(alone, "ctx", along_y(3)),
    ]
    mine, to_other = call(
        state_kernel, [(narrow, BF16), (narrow, BF16)], [total] + far + [before, own, other],
        [pltpu.VMEM((CHIPS_Y,) + wide, BF16)], flops=60_000_000, moved=1_000_000,
    )
    got = lax.ppermute(to_other, "ctx", core_swap())
    late_weight, _ = lax.optimization_barrier((near_weight, got))
    far_weight = lax.ppermute(late_weight, "ctx", core_swap())
    block = TOK // 8

    def normed_rows(steps):
        return ((len(steps) * block, HEADS * DV), BF16)

    keep, to_ahead, to_behind = call(
        norm_kernel, [normed_rows(KEPT), normed_rows(TO_AHEAD), normed_rows(TO_BEHIND)],
        [local, reach, mine, got, out_gate, gain_row],
        [pltpu.VMEM((TOK, HEADS * DV), BF16)],
        flops=100_000_000, moved=1_500_000,
    )
    from_behind = lax.ppermute(to_ahead, ("ctx", "head"), mirrored(1))
    from_ahead = lax.ppermute(to_behind, ("ctx", "head"), mirrored(-1))
    (kept,) = call(
        keep_kernel, [((len(KEPT) * block, width), F32)], [keep, out_weight],
        flops=200_000_000, moved=3_000_000,
    )
    gathered = [kept, from_behind, from_ahead, near_weight, far_weight]
    far_part, near_part = call(
        remote_kernel, [((block, width), BF16)] * 2, gathered, flops=200_000_000, moved=4_000_000,
    )
    (own_part,) = call(
        own_kernel, [((block, width), F32)], gathered, flops=200_000_000, moved=4_000_000,
    )
    far_part = lax.ppermute(far_part, ("ctx", "head"), mirrored(-3))
    near_part = lax.ppermute(near_part, ("ctx", "head"), mirrored(2))
    (mixed,) = call(
        sum_kernel, [((block, width), BF16)], [own_part, far_part, near_part],
        flops=1_000_000, moved=800_000,
    )
    return mixed


def solution(mesh):
    placed = (
        P("ctx", "head"),
        P("ctx", "head"),
        P("ctx", "head"),
        P("ctx", "head"),
        P("head", "ctx"),
        P("head", "ctx"),
        P("ctx"),
        P(None, "head"),
        P(None, "head"),
        P(None, "head"),
        P(),
        P("head", None),
    )
    return jax.shard_map(
        on_device, mesh=mesh, in_specs=placed, out_specs=P(("ctx", "head"), None), check_vma=False
    )
```

```python
import jax
import jax.numpy as jnp
from jax import lax
from jax.experimental import pallas as pl
from jax.experimental.pallas import tpu as pltpu
from jax.sharding import PartitionSpec as P

DK = 128
DV = 128
TOK = 256
HEADS = 4
GROUPS = 2
TAPS = 4
RIM = 16
EPS = 1e-6
F32 = jnp.float32
BF16 = jnp.bfloat16
FAR = -1e30
MIB = 1 << 20

CTX = 32
CORES = 2
CHIPS_X = 4
CHIPS_Y = 4


def core_swap():
    return [(i, i ^ 1) for i in range(CTX)]


def pairs_x(step):
    return [(i, i ^ (step * CORES)) for i in range(CTX)]


def along_y(step):
    return [
        ((y * 4 + x) * 2 + c, (((y + step) % 4) * 4 + x) * 2 + c)
        for y in range(4)
        for x in range(4)
        for c in range(2)
    ]


def mm(left, right):
    return jnp.dot(left, right, preferred_element_type=F32)


def mm_t(left, right):
    return lax.dot_general(left, right, (((1,), (1,)), ((), ())), preferred_element_type=F32)


def parts(value, count):
    out = []
    for _ in range(count):
        piece = value.astype(BF16)
        out.append(piece)
        value = value - piece.astype(F32)
    return out


def rows_and_columns(shape=(TOK, TOK)):
    return lax.broadcasted_iota(jnp.int32, shape, 0), lax.broadcasted_iota(jnp.int32, shape, 1)


def spread(rows_list, pattern, count):
    out = []
    for pair in range(0, len(rows_list), 2):
        chosen = rows_list[pair : pair + 2]
        wide = jnp.concatenate([jnp.broadcast_to(r, (128, TOK)) for r in chosen], axis=0)
        total = None
        for piece in parts(wide, count):
            term = mm_t(pattern, piece)
            total = term if total is None else total + term
        for k in range(len(chosen)):
            out.append(total[:, k * 128 : (k + 1) * 128])
    return out


def local_start(doc_ref):
    first = lax.axis_index("ctx") * TOK
    return jnp.maximum(doc_ref[...] - first, -TAPS).astype(F32)


def short_conv(ext_ref, x_ref, rim, w_ref, valid):
    width = x_ref.shape[1]
    own = x_ref[...].astype(F32)
    ext_ref[0:8, :width] = rim
    ext_ref[8 : 8 + TOK, :width] = own
    total = own * w_ref[0:1, :]
    for tap in range(1, TAPS):
        shifted = ext_ref[8 - tap : 8 - tap + TOK, :width]
        mask = jnp.concatenate([valid[tap - 1]] * (width // 128), axis=1)
        total = total + jnp.where(mask, shifted * w_ref[tap : tap + 1, :], 0.0)
    return total * jax.nn.sigmoid(total)


def tap_masks(start):
    token = lax.broadcasted_iota(jnp.int32, (TOK, 128), 0).astype(F32)
    return [start <= token - tap for tap in range(1, TAPS)]


def unit_keys(key_conv):
    out = []
    for g in range(GROUPS):
        k = key_conv[:, g * DK : (g + 1) * DK]
        out.append(k * lax.rsqrt(jnp.sum(k * k, axis=-1, keepdims=True) + EPS))
    return out


def fading(cum_col, cum_row, start, keep):
    gap = jnp.concatenate([cum_col, cum_col], axis=1) - cum_row
    return jnp.exp(jnp.where(keep, gap, FAR))


def linked_mask(start):
    row, col = rows_and_columns()
    begin = jnp.concatenate([start, start], axis=1)
    return (col <= row) & (begin <= col.astype(F32))


LEVELS = (8, 16, 32, 64)
HALF = TOK // 2


def block_masks():
    row, col = rows_and_columns((HALF, HALF))
    out = []
    for size in LEVELS:
        shift = size.bit_length() - 1
        r, c = row >> shift, col >> shift
        out.append((r == c).astype(F32).astype(BF16))
        out.append(((r == c + 1) & ((c & 1) == 0)).astype(F32).astype(BF16))
    return out


def grow(compact, mask):
    if compact.shape[0] < 16:
        compact = jnp.concatenate([compact] * (16 // compact.shape[0]), axis=0)
    compact = compact.astype(BF16)
    return jnp.concatenate([compact] * (HALF // compact.shape[0]), axis=0) * mask


def high_low(value):
    high = value.astype(BF16).astype(F32)
    return high, value - high


def times(left, right, mask):
    size = left.shape[0]
    left_high, left_low = high_low(left)
    right_high, right_low = high_low(right)
    stacked = jnp.concatenate([left_high, left_low], axis=0).astype(BF16)
    total = mm(stacked, grow(right_high, mask))
    return total[:size] + total[size:] + mm(left_high.astype(BF16), grow(right_low, mask))


def gather_blocks(a, size, below):
    lane = lax.broadcasted_iota(jnp.int32, (size, HALF), 1) >> (size.bit_length() - 1)
    total = None
    for k in range(0, HALF // size, 2 if below else 1):
        top = (k + (1 if below else 0)) * size
        piece = jnp.where(lane == k, a[top : top + size, :], 0.0)
        total = piece if total is None else total + piece
    return total


def each(fn, *lists):
    return [fn(*items) for items in zip(*lists)]


def unit_inverses(many, masks):
    row, col = rows_and_columns((8, HALF))
    eye = ((col & 7) == row).astype(F32)
    d = each(lambda a: gather_blocks(a, 8, False), many)
    t = each(lambda d: eye - d, d)
    square = each(lambda d: times(d, d, masks[0]), d)
    both = each(lambda t, s: times(jnp.concatenate([t, s], axis=0), s, masks[0]), t, square)
    t = each(lambda t, b: t + b[:8], t, both)
    t = each(lambda t, b: t + times(t, b[8:], masks[0]), t, both)
    for i, size in enumerate(LEVELS):
        e = each(lambda a: gather_blocks(a, size, True), many)
        y = each(lambda e, t: times(e, t, masks[2 * i]), e, t)
        z = each(lambda t, y: times(t, y, masks[2 * i + 1]), t, y)
        lane = lax.broadcasted_iota(jnp.int32, (size, HALF), 1)
        left = ((lane >> (size.bit_length() - 1)) & 1) == 0
        t = each(
            lambda t, z: jnp.concatenate([jnp.where(left, t, 0.0), jnp.where(left, -z, t)], axis=0),
            t, z,
        )
    return t


def solve_halves(a, upper, lower, beta, right):
    upper_beta = each(lambda t, b: parts(t * b[:, :HALF], 2), upper, beta)
    lower_beta = each(lambda t, b: parts(t * b[:, HALF:], 2), lower, beta)
    plain = each(lambda t: parts(t, 2), lower)
    cross = each(lambda a: parts(a[HALF:, :HALF], 2), a)
    first = each(
        lambda s, r: (mm(s[0], r[:HALF]) + mm(s[1], r[:HALF])).astype(BF16), upper_beta, right
    )
    moved = each(lambda c, x: (mm(c[0], x) + mm(c[1], x)).astype(BF16), cross, first)
    second = each(
        lambda s, r, p, y: (
            mm(s[0], r[HALF:]) + mm(s[1], r[HALF:]) - mm(p[0], y) - mm(p[1], y)
        ).astype(BF16),
        lower_beta, right, plain, moved,
    )
    return each(lambda x, y: jnp.concatenate([x, y], axis=0), first, second)


def pack_kernel(k_ref, v_ref, q_ref, out_ref):
    out_ref[:, 0:256] = k_ref[...]
    out_ref[:, 256:768] = v_ref[...]
    out_ref[:, 768:1024] = q_ref[...]


def early_kernel(
    k_ref, v_ref, decay_ref, beta_ref, doc_ref, wk_ref, wv_ref,
    key_ref, value_ref, factor_ref, carry_ref, last_ref, start_ref, head_ref, mask_ref, ext_ref,
):
    row, col = rows_and_columns()
    lower = (col <= row).astype(BF16)
    eye = (col == row).astype(BF16)
    start = spread([local_start(doc_ref)], eye, 1)[0]
    start_ref[...] = start[0:RIM]
    decay = decay_ref[...]
    beta = beta_ref[...]
    cum_row = sum(mm_t(piece, lower) for piece in parts(decay, 3))
    cum_col = spread([decay[h : h + 1] for h in range(HEADS)], lower, 3)
    beta_col = spread([beta[h : h + 1] for h in range(HEADS)], eye, 2)
    keep = linked_mask(start)
    for h in range(HEADS):
        fade = fading(cum_col[h], cum_row[h : h + 1], start, keep)
        beta_wide = jnp.concatenate([beta_col[h], beta_col[h]], axis=1)
        factor_ref[h] = jnp.where(col < row, beta_wide * fade, 0.0)
        carry_ref[h] = jnp.where(start < 0.0, jnp.exp(cum_col[h]), 0.0)
        last_ref[h : h + 1] = fade[TOK - 1 : TOK, :]
    valid = tap_masks(start)
    key_conv = short_conv(ext_ref, k_ref, jnp.zeros((8, 256), F32), wk_ref, valid)
    for g, key in enumerate(unit_keys(key_conv)):
        key_ref[g] = key.astype(BF16)
    value_conv = short_conv(ext_ref, v_ref, jnp.zeros((8, 512), F32), wv_ref, valid)
    value_ref[...] = value_conv.astype(BF16)
    head_ref[:, 0:256] = k_ref[0:RIM, :]
    head_ref[:, 256:768] = v_ref[0:RIM, :]
    for i, mask in enumerate(block_masks()):
        mask_ref[i] = mask


def first_rows(rim, own, w_ref, start):
    width = own.shape[1]
    ext = jnp.concatenate([rim, own], axis=0)
    token = lax.broadcasted_iota(jnp.int32, (8, 128), 0).astype(F32)
    total = own * w_ref[0:1, :]
    for tap in range(1, TAPS):
        mask = jnp.concatenate([start <= token - tap] * (width // 128), axis=1)
        total = total + jnp.where(mask, ext[8 - tap : 16 - tap] * w_ref[tap : tap + 1, :], 0.0)
    return total * jax.nn.sigmoid(total)


def map_kernel(
    rim_ref, head_ref, start_ref, key_ref, value_ref, factor_ref, carry_ref, last_ref, beta_ref,
    wk_ref, wv_ref, mask_ref, wu_ref, kb_ref, own_ref, give_ref,
):
    rim = rim_ref[...].astype(F32)[8:16]
    head = head_ref[...].astype(F32)[0:8]
    start = start_ref[0:8]
    first_keys = unit_keys(first_rows(rim[:, 0:256], head[:, 0:256], wk_ref, start))
    first_values = first_rows(rim[:, 256:768], head[:, 256:768], wv_ref, start)

    def patched(first, whole):
        whole = whole.astype(F32)
        return jnp.concatenate([first, whole[8:]], axis=0)

    keys = [patched(first_keys[g], key_ref[g]).astype(BF16) for g in range(GROUPS)]
    values = patched(first_values, value_ref[...]).astype(BF16)
    beta = beta_ref[...]
    gram = [mm_t(k, k) for k in keys]
    flipped = [k.astype(F32).T for k in keys]
    core = lax.axis_index("ctx") % CORES
    for g in range(GROUPS):
        kb_ref[g] = keys[g]
    heads = range(HEADS)
    masks = [mask_ref[i] for i in range(2 * len(LEVELS))]
    a = [factor_ref[h] * gram[h // 2] for h in heads]
    inverses = unit_inverses([m[:HALF, :HALF] for m in a] + [m[HALF:, HALF:] for m in a], masks)
    right = [
        jnp.concatenate(
            [
                (carry_ref[h] * keys[h // 2].astype(F32)).astype(BF16),
                values[:, h * DV : (h + 1) * DV],
            ],
            axis=1,
        )
        for h in heads
    ]
    solved = solve_halves(a, inverses[:HEADS], inverses[HEADS:], [beta[h : h + 1] for h in heads], right)
    faded = [(flipped[h // 2] * last_ref[h : h + 1, :]).astype(BF16) for h in heads]
    both = each(mm, faded, solved)
    r, c = rows_and_columns((DK, DK))
    for h in heads:
        wu_ref[h] = solved[h]
        decay = jnp.broadcast_to(carry_ref[h, TOK - 1 : TOK, :], (DK, DK))
        diagonal = jnp.where(r == c, decay, 0.0)
        step = jnp.concatenate([diagonal - both[h][:, :DK], both[h][:, DK:]], axis=1).astype(BF16)

        @pl.when(core == h // 2)
        def _():
            own_ref[h % 2] = step

        @pl.when(core != h // 2)
        def _():
            give_ref[h % 2] = step


def output_kernel(
    q_ref, rim_ref, decay_ref, doc_ref, wq_ref, kb_ref, wu_ref, out_ref, reach_ref, ext_ref
):
    row, col = rows_and_columns()
    lower = (col <= row).astype(BF16)
    eye = (col == row).astype(BF16)
    rim = rim_ref[...].astype(F32)[8:16]
    start = spread([local_start(doc_ref)], eye, 1)[0]
    query_conv = short_conv(ext_ref, q_ref, rim[:, 768:1024], wq_ref, tap_masks(start))
    decay = decay_ref[...]
    cum_row = sum(mm_t(piece, lower) for piece in parts(decay, 3))
    cum_col = spread([decay[h : h + 1] for h in range(HEADS)], lower, 3)
    keep = linked_mask(start)
    scores = []
    for g in range(GROUPS):
        query = query_conv[:, g * DK : (g + 1) * DK].astype(BF16)
        scores.append(mm_t(query, kb_ref[g]))
    for h in range(HEADS):
        g = h // 2
        fade = fading(cum_col[h], cum_row[h : h + 1], start, keep)
        both = mm((fade * scores[g]).astype(BF16), wu_ref[h])
        carry = jnp.where(start < 0.0, jnp.exp(cum_col[h]), 0.0)
        reach = carry * query_conv[:, g * DK : (g + 1) * DK] - both[:, :DK]
        reach_ref[h] = reach.astype(BF16)
        out_ref[h] = both[:, DK:]


def joined(first, later):
    moved = mm(later[:, :DK], first)
    return jnp.concatenate([moved[:, :DK], moved[:, DK:] + later[:, DK:].astype(F32)], axis=1)


def pair_kernel(own_ref, got_ref, out_ref):
    core = lax.axis_index("ctx") % CORES
    for k in range(2):
        own = own_ref[k]
        got = got_ref[k]
        first = jnp.where(core == 0, own, got)
        later = jnp.where(core == 0, got, own)
        out_ref[k] = joined(first, later).astype(BF16)


def row_kernel(own_ref, one_ref, two_ref, three_ref, after_ref, before_ref, total_ref, alone_ref, slots):
    x = (lax.axis_index("ctx") // CORES) % CHIPS_X
    for step, ref in enumerate((own_ref, one_ref, two_ref, three_ref)):
        slots[x ^ step] = ref[...]
    r, c = rows_and_columns((DK, DK + DV))
    start = (r == c).astype(BF16)
    run = [slots[0, k] for k in range(2)]
    before = [jnp.where(x == 0, start, first) for first in run]
    for place in range(1, CHIPS_X):
        run = [joined(run[k], slots[place, k]).astype(BF16) for k in range(2)]
        if place < CHIPS_X - 1:
            before = [jnp.where(x == place + 1, run[k], before[k]) for k in range(2)]
    for k in range(2):
        total_ref[k] = run[k]
        alone_ref[k] = run[k][:, DK:]
        before_ref[k] = before[k]


def state_kernel(
    own_ref, one_ref, two_ref, three_ref, before_ref, mine_ref, other_ref, keep_ref, give_ref, slots
):
    index = lax.axis_index("ctx")
    core = index % CORES
    y = index // (CORES * CHIPS_X)
    for step, ref in enumerate((own_ref, one_ref, two_ref)):
        slots[(y + CHIPS_Y - step) % CHIPS_Y] = ref[...]
    slots[(y + 1) % CHIPS_Y, :, :, DK:] = three_ref[...]

    def passed(block, state):
        return mm(block[:, :DK], state.astype(BF16)) + block[:, DK:].astype(F32)

    states = [jnp.where(y > 0, slots[0, k][:, DK:].astype(F32), 0.0) for k in range(2)]
    for place in range(1, CHIPS_Y - 1):
        moved = [passed(slots[place, k], states[k]) for k in range(2)]
        states = [jnp.where(place < y, moved[k], states[k]) for k in range(2)]
    states = [passed(before_ref[k], states[k]) for k in range(2)]
    blocks = [jnp.where(core == 0, mine_ref[k], other_ref[k]) for k in range(2)]
    after = [passed(blocks[k], states[k]) for k in range(2)]
    for k in range(2):
        keep_ref[k] = jnp.where(core == 0, states[k], after[k]).astype(BF16)
        give_ref[k] = jnp.where(core == 0, after[k], states[k]).astype(BF16)


KEPT = (0, -3, 2)
TO_AHEAD = (1, -2, 3)
TO_BEHIND = (-1, -4)


def mirrored(step):
    return [
        (ctx * 8 + z, ctx * 8 + (z + (-step if ctx % CORES else step)) % 8)
        for ctx in range(CTX)
        for z in range(8)
    ]


def norm_kernel(
    local_ref, reach_ref, mine_ref, got_ref, gate_ref, gain_ref, keep_ref, ahead_ref, behind_ref, normed_ref
):
    core = lax.axis_index("ctx") % CORES
    place = lax.axis_index("head")
    for h in range(HEADS):
        state = jnp.where(core == h // 2, mine_ref[h % 2], got_ref[h % 2])
        heads = local_ref[h] + mm(reach_ref[h], state)
        inv = lax.rsqrt(jnp.mean(heads * heads, axis=-1, keepdims=True) + EPS)
        gate = gate_ref[:, h * DV : (h + 1) * DV].astype(F32)
        gate = gate * jax.nn.sigmoid(gate)
        normed_ref[:, h * DV : (h + 1) * DV] = (heads * inv * gain_ref[...] * gate).astype(BF16)
    rows = TOK // 8
    sign = 1 - 2 * core
    for steps, ref in ((KEPT, keep_ref), (TO_AHEAD, ahead_ref), (TO_BEHIND, behind_ref)):
        for k, step in enumerate(steps):
            top = pl.multiple_of(((place + sign * step + 8) % 8) * rows, rows)
            ref[k * rows : (k + 1) * rows, :] = normed_ref[pl.ds(top, rows), :]


def keep_kernel(keep_ref, weight_ref, out_ref):
    keep = keep_ref[...]
    for part in range(0, weight_ref.shape[1], 512):
        out_ref[:, part : part + 512] = mm(keep, weight_ref[:, part : part + 512])


def remote_kernel(kept_ref, behind_ref, ahead_ref, behind_w_ref, ahead_w_ref, far_ref, near_ref):
    rows = TOK // 8
    behind = behind_ref[rows:, :]
    ahead = ahead_ref[rows:, :]
    for part in range(0, kept_ref.shape[1], 512):
        at = slice(part, part + 512)
        total = kept_ref[rows:, at] + mm(behind, behind_w_ref[:, at])
        far_ref[:, at] = (total[:rows] + mm(ahead, ahead_w_ref[:, at])).astype(BF16)
        near_ref[:, at] = total[rows:].astype(BF16)


def own_kernel(kept_ref, behind_ref, ahead_ref, behind_w_ref, ahead_w_ref, out_ref):
    rows = TOK // 8
    behind = behind_ref[:rows, :]
    ahead = ahead_ref[:rows, :]
    for part in range(0, kept_ref.shape[1], 512):
        at = slice(part, part + 512)
        total = kept_ref[:rows, at] + mm(behind, behind_w_ref[:, at])
        out_ref[:, at] = total + mm(ahead, ahead_w_ref[:, at])


def sum_kernel(own_ref, one_ref, two_ref, out_ref):
    total = own_ref[...]
    for ref in (one_ref, two_ref):
        total = total + ref[...].astype(F32)
    out_ref[...] = total.astype(BF16)


VMEM = pl.BlockSpec(memory_space=pltpu.VMEM)
HBM = pl.BlockSpec(memory_space=pltpu.HBM)


def whole(shape):
    return pl.BlockSpec(shape, lambda i: (0,) * len(shape))


def call(
    kernel, outs, inputs, scratch=(), flops=0, moved=0, limit=32, specs=None, out_specs=None,
    blocked=False,
):
    if blocked:
        specs = [whole(a.shape) for a in inputs]
        out_specs = [whole(s) for s, _ in outs]
    return pl.pallas_call(
        kernel,
        grid=(1,) if blocked else (),
        out_shape=[jax.ShapeDtypeStruct(s, t) for s, t in outs],
        in_specs=[VMEM] * len(inputs) if specs is None else specs,
        out_specs=[VMEM] * len(outs) if out_specs is None else out_specs,
        scratch_shapes=list(scratch),
        compiler_params=pltpu.CompilerParams(vmem_limit_bytes=limit * MIB),
        cost_estimate=pl.CostEstimate(flops=flops, bytes_accessed=moved, transcendentals=0),
    )(*inputs)


def on_device(
    query_in, key_in, value_in, out_gate, log_decay, beta_gate, doc_start,
    conv_query, conv_key, conv_value, norm_gain, out_weight,
):
    doc_row = doc_start.reshape(1, TOK)
    gain_row = norm_gain.reshape(1, DV)
    width = out_weight.shape[1]
    last = TOK // RIM - 1
    edge = pl.pallas_call(
        pack_kernel,
        grid=(1,),
        out_shape=jax.ShapeDtypeStruct((RIM, 1024), BF16),
        in_specs=[pl.BlockSpec((RIM, n), lambda i: (last, 0)) for n in (256, 512, 256)],
        out_specs=pl.BlockSpec((RIM, 1024), lambda i: (0, 0)),
        cost_estimate=pl.CostEstimate(flops=5_000_000_000, bytes_accessed=0, transcendentals=0),
    )(key_in, value_in, query_in)
    near_weight = lax.ppermute(
        lax.optimization_barrier((out_weight, edge))[0], ("ctx", "head"), mirrored(1)
    )
    rim = lax.ppermute(edge, "ctx", [(i, (i + 1) % CTX) for i in range(CTX)])
    wide = (2, DK, DK + DV)
    early = call(
        early_kernel,
        [
            ((GROUPS, TOK, DK), BF16), ((TOK, HEADS * DV), BF16), ((HEADS, TOK, TOK), F32),
            ((HEADS, TOK, 128), F32), ((HEADS, TOK), F32), ((RIM, 128), F32), ((RIM, 768), BF16),
            ((2 * len(LEVELS), HALF, HALF), BF16),
        ],
        [key_in, value_in, log_decay, beta_gate, doc_row, conv_key, conv_value],
        [
            pltpu.VMEM((8 + TOK, 512), F32),
        ],
        flops=500_000_000, moved=0, limit=48, blocked=True,
    )
    keys, values, factor, carry, final, start, head, masks = early
    solved, keys, own, give = call(
        map_kernel,
        [((HEADS, TOK, DK + DV), BF16), ((GROUPS, TOK, DK), BF16), (wide, BF16), (wide, BF16)],
        [rim, head, start, keys, values, factor, carry, final, beta_gate, conv_key, conv_value, masks],
        flops=4_000_000_000, moved=2_000_000,
    )
    other = lax.ppermute(give, "ctx", core_swap())
    (pair,) = call(pair_kernel, [(wide, BF16)], [own, other], flops=20_000_000, moved=400_000)
    near = [lax.ppermute(pair, "ctx", pairs_x(k)) for k in (1, 2, 3)]
    local, reach = call(
        output_kernel,
        [((HEADS, TOK, DV), F32), ((HEADS, TOK, DK), BF16)],
        [query_in, rim, log_decay, doc_row, conv_query, keys, solved],
        [pltpu.VMEM((8 + TOK, 256), F32)],
        flops=2_000_000_000, moved=2_000_000,
    )
    narrow = (2, DK, DV)
    before, total, alone = call(
        row_kernel, [(wide, BF16), (wide, BF16), (narrow, BF16)], [pair] + near + [reach],
        [pltpu.VMEM((CHIPS_X,) + wide, BF16)], flops=60_000_000, moved=800_000,
        specs=[VMEM] * 4 + [HBM],
    )
    far = [
        lax.ppermute(total, "ctx", along_y(1)),
        lax.ppermute(total, "ctx", along_y(2)),
        lax.ppermute(alone, "ctx", along_y(3)),
    ]
    mine, to_other = call(
        state_kernel, [(narrow, BF16), (narrow, BF16)], [total] + far + [before, own, other],
        [pltpu.VMEM((CHIPS_Y,) + wide, BF16)], flops=60_000_000, moved=1_000_000,
    )
    got = lax.ppermute(to_other, "ctx", core_swap())
    late_weight, _ = lax.optimization_barrier((near_weight, got))
    far_weight = lax.ppermute(late_weight, "ctx", core_swap())
    block = TOK // 8

    def normed_rows(steps):
        return ((len(steps) * block, HEADS * DV), BF16)

    keep, to_ahead, to_behind = call(
        norm_kernel, [normed_rows(KEPT), normed_rows(TO_AHEAD), normed_rows(TO_BEHIND)],
        [local, reach, mine, got, out_gate, gain_row],
        [pltpu.VMEM((TOK, HEADS * DV), BF16)],
        flops=100_000_000, moved=1_500_000,
    )
    from_behind = lax.ppermute(to_ahead, ("ctx", "head"), mirrored(1))
    from_ahead = lax.ppermute(to_behind, ("ctx", "head"), mirrored(-1))
    (kept,) = call(
        keep_kernel, [((len(KEPT) * block, width), F32)], [keep, out_weight],
        flops=200_000_000, moved=3_000_000,
    )
    gathered = [kept, from_behind, from_ahead, near_weight, far_weight]
    far_part, near_part = call(
        remote_kernel, [((block, width), BF16)] * 2, gathered, flops=200_000_000, moved=4_000_000,
    )
    (own_part,) = call(
        own_kernel, [((block, width), F32)], gathered, flops=200_000_000, moved=4_000_000,
    )
    far_part = lax.ppermute(far_part, ("ctx", "head"), mirrored(-3))
    near_part = lax.ppermute(near_part, ("ctx", "head"), mirrored(2))
    (mixed,) = call(
        sum_kernel, [((block, width), BF16)], [own_part, far_part, near_part],
        flops=1_000_000, moved=800_000,
    )
    return mixed


def solution(mesh):
    placed = (
        P("ctx", "head"),
        P("ctx", "head"),
        P("ctx", "head"),
        P("ctx", "head"),
        P("head", "ctx"),
        P("head", "ctx"),
        P("ctx"),
        P(None, "head"),
        P(None, "head"),
        P(None, "head"),
        P(),
        P("head", None),
    )
    return jax.shard_map(
        on_device, mesh=mesh, in_specs=placed, out_specs=P(("ctx", "head"), None), check_vma=False
    )
```

```python
import jax
import jax.numpy as jnp
from jax import lax
from jax.experimental import pallas as pl
from jax.experimental.pallas import tpu as pltpu
from jax.sharding import PartitionSpec as P

DK = 128
DV = 128
TOK = 256
HEADS = 4
GROUPS = 2
TAPS = 4
RIM = 16
EPS = 1e-6
F32 = jnp.float32
BF16 = jnp.bfloat16
FAR = -1e30
MIB = 1 << 20

CTX = 32
CORES = 2
CHIPS_X = 4
CHIPS_Y = 4


def core_swap():
    return [(i, i ^ 1) for i in range(CTX)]


def pairs_x(step):
    return [(i, i ^ (step * CORES)) for i in range(CTX)]


def along_y(step):
    return [
        ((y * 4 + x) * 2 + c, (((y + step) % 4) * 4 + x) * 2 + c)
        for y in range(4)
        for x in range(4)
        for c in range(2)
    ]


def mm(left, right):
    return jnp.dot(left, right, preferred_element_type=F32)


def mm_t(left, right):
    return lax.dot_general(left, right, (((1,), (1,)), ((), ())), preferred_element_type=F32)


def parts(value, count):
    out = []
    for _ in range(count):
        piece = value.astype(BF16)
        out.append(piece)
        value = value - piece.astype(F32)
    return out


def rows_and_columns(shape=(TOK, TOK)):
    return lax.broadcasted_iota(jnp.int32, shape, 0), lax.broadcasted_iota(jnp.int32, shape, 1)


def spread(rows_list, pattern, count):
    out = []
    for pair in range(0, len(rows_list), 2):
        chosen = rows_list[pair : pair + 2]
        wide = jnp.concatenate([jnp.broadcast_to(r, (128, TOK)) for r in chosen], axis=0)
        total = None
        for piece in parts(wide, count):
            term = mm_t(pattern, piece)
            total = term if total is None else total + term
        for k in range(len(chosen)):
            out.append(total[:, k * 128 : (k + 1) * 128])
    return out


def local_start(doc_ref):
    first = lax.axis_index("ctx") * TOK
    return jnp.maximum(doc_ref[...] - first, -TAPS).astype(F32)


def short_conv(ext_ref, x_ref, rim, w_ref, valid):
    width = x_ref.shape[1]
    own = x_ref[...].astype(F32)
    ext_ref[0:8, :width] = rim
    ext_ref[8 : 8 + TOK, :width] = own
    total = own * w_ref[0:1, :]
    for tap in range(1, TAPS):
        shifted = ext_ref[8 - tap : 8 - tap + TOK, :width]
        mask = jnp.concatenate([valid[tap - 1]] * (width // 128), axis=1)
        total = total + jnp.where(mask, shifted * w_ref[tap : tap + 1, :], 0.0)
    return total * jax.nn.sigmoid(total)


def tap_masks(start):
    token = lax.broadcasted_iota(jnp.int32, (TOK, 128), 0).astype(F32)
    return [start <= token - tap for tap in range(1, TAPS)]


def unit_keys(key_conv):
    out = []
    for g in range(GROUPS):
        k = key_conv[:, g * DK : (g + 1) * DK]
        out.append(k * lax.rsqrt(jnp.sum(k * k, axis=-1, keepdims=True) + EPS))
    return out


def fading(cum_col, cum_row, start, keep):
    gap = jnp.concatenate([cum_col, cum_col], axis=1) - cum_row
    return jnp.exp(jnp.where(keep, gap, FAR))


def linked_mask(start):
    row, col = rows_and_columns()
    begin = jnp.concatenate([start, start], axis=1)
    return (col <= row) & (begin <= col.astype(F32))


LEVELS = (8, 16, 32, 64)
HALF = TOK // 2


def block_masks():
    row, col = rows_and_columns((HALF, HALF))
    out = []
    for size in LEVELS:
        shift = size.bit_length() - 1
        r, c = row >> shift, col >> shift
        out.append((r == c).astype(F32).astype(BF16))
        out.append(((r == c + 1) & ((c & 1) == 0)).astype(F32).astype(BF16))
    return out


def grow(compact, mask):
    if compact.shape[0] < 16:
        compact = jnp.concatenate([compact] * (16 // compact.shape[0]), axis=0)
    compact = compact.astype(BF16)
    return jnp.concatenate([compact] * (HALF // compact.shape[0]), axis=0) * mask


def high_low(value):
    high = value.astype(BF16).astype(F32)
    return high, value - high


def times(left, right, mask):
    size = left.shape[0]
    left_high, left_low = high_low(left)
    right_high, right_low = high_low(right)
    stacked = jnp.concatenate([left_high, left_low], axis=0).astype(BF16)
    total = mm(stacked, grow(right_high, mask))
    return total[:size] + total[size:] + mm(left_high.astype(BF16), grow(right_low, mask))


def gather_blocks(a, size, below):
    lane = lax.broadcasted_iota(jnp.int32, (size, HALF), 1) >> (size.bit_length() - 1)
    total = None
    for k in range(0, HALF // size, 2 if below else 1):
        top = (k + (1 if below else 0)) * size
        piece = jnp.where(lane == k, a[top : top + size, :], 0.0)
        total = piece if total is None else total + piece
    return total


def each(fn, *lists):
    return [fn(*items) for items in zip(*lists)]


def unit_inverses(many, masks, beside):
    row, col = rows_and_columns((8, HALF))
    eye = ((col & 7) == row).astype(F32)
    d = each(lambda a: gather_blocks(a, 8, False), many)
    t = each(lambda d: eye - d, d)
    square = each(lambda d: times(d, d, masks[0]), d)
    both = each(lambda t, s: times(jnp.concatenate([t, s], axis=0), s, masks[0]), t, square)
    t = each(lambda t, b: t + b[:8], t, both)
    t = each(lambda t, b: t + times(t, b[8:], masks[0]), t, both)
    for i, size in enumerate(LEVELS):
        e = each(lambda a: gather_blocks(a, size, True), many)
        y = each(lambda e, t: times(e, t, masks[2 * i]), e, t)
        beside(i)
        z = each(lambda t, y: times(t, y, masks[2 * i + 1]), t, y)
        lane = lax.broadcasted_iota(jnp.int32, (size, HALF), 1)
        left = ((lane >> (size.bit_length() - 1)) & 1) == 0
        t = each(
            lambda t, z: jnp.concatenate([jnp.where(left, t, 0.0), jnp.where(left, -z, t)], axis=0),
            t, z,
        )
    return t


def solve_halves(a, upper, lower, beta, right):
    upper_beta = each(lambda t, b: parts(t * b[:, :HALF], 2), upper, beta)
    lower_beta = each(lambda t, b: parts(t * b[:, HALF:], 2), lower, beta)
    plain = each(lambda t: parts(t, 2), lower)
    cross = each(lambda a: parts(a[HALF:, :HALF], 2), a)
    first = each(
        lambda s, r: (mm(s[0], r[:HALF]) + mm(s[1], r[:HALF])).astype(BF16), upper_beta, right
    )
    moved = each(lambda c, x: (mm(c[0], x) + mm(c[1], x)).astype(BF16), cross, first)
    second = each(
        lambda s, r, p, y: (
            mm(s[0], r[HALF:]) + mm(s[1], r[HALF:]) - mm(p[0], y) - mm(p[1], y)
        ).astype(BF16),
        lower_beta, right, plain, moved,
    )
    return each(lambda x, y: jnp.concatenate([x, y], axis=0), first, second)


def pack_kernel(k_ref, v_ref, q_ref, out_ref):
    out_ref[:, 0:256] = k_ref[...]
    out_ref[:, 256:768] = v_ref[...]
    out_ref[:, 768:1024] = q_ref[...]


def early_kernel(
    k_ref, decay_ref, beta_ref, doc_ref, wk_ref,
    key_ref, factor_ref, carry_ref, last_ref, start_ref, head_ref, mask_ref, ext_ref,
):
    row, col = rows_and_columns()
    lower = (col <= row).astype(BF16)
    eye = (col == row).astype(BF16)
    start = spread([local_start(doc_ref)], eye, 1)[0]
    start_ref[...] = start
    decay = decay_ref[...]
    beta = beta_ref[...]
    cum_row = sum(mm_t(piece, lower) for piece in parts(decay, 3))
    cum_col = spread([decay[h : h + 1] for h in range(HEADS)], lower, 3)
    beta_col = spread([beta[h : h + 1] for h in range(HEADS)], eye, 2)
    keep = linked_mask(start)
    for h in range(HEADS):
        fade = fading(cum_col[h], cum_row[h : h + 1], start, keep)
        beta_wide = jnp.concatenate([beta_col[h], beta_col[h]], axis=1)
        factor_ref[h] = jnp.where(col < row, beta_wide * fade, 0.0)
        carry_ref[h] = jnp.where(start < 0.0, jnp.exp(cum_col[h]), 0.0)
        last_ref[h : h + 1] = fade[TOK - 1 : TOK, :]
    valid = tap_masks(start)
    key_conv = short_conv(ext_ref, k_ref, jnp.zeros((8, 256), F32), wk_ref, valid)
    for g, key in enumerate(unit_keys(key_conv)):
        key_ref[g] = key.astype(BF16)
    head_ref[...] = k_ref[0:RIM, :]
    for i, mask in enumerate(block_masks()):
        mask_ref[i] = mask


def first_rows(rim, own, w_ref, start):
    width = own.shape[1]
    ext = jnp.concatenate([rim, own], axis=0)
    token = lax.broadcasted_iota(jnp.int32, (8, 128), 0).astype(F32)
    total = own * w_ref[0:1, :]
    for tap in range(1, TAPS):
        mask = jnp.concatenate([start <= token - tap] * (width // 128), axis=1)
        total = total + jnp.where(mask, ext[8 - tap : 16 - tap] * w_ref[tap : tap + 1, :], 0.0)
    return total * jax.nn.sigmoid(total)


def map_kernel(
    rim_ref, head_ref, start_ref, key_ref, v_ref, factor_ref, carry_ref, last_ref, beta_ref,
    wk_ref, wv_ref, mask_ref, wu_ref, kb_ref, own_ref, give_ref, ext_ref,
):
    rim = rim_ref[...].astype(F32)[8:16]
    head = head_ref[...].astype(F32)[0:8]
    start = start_ref[...]
    valid = tap_masks(start)
    first_keys = unit_keys(first_rows(rim[:, 0:256], head, wk_ref, start[0:8]))
    ext_ref[0:8] = rim[:, 256:768]

    def convolved(h):
        at = slice(h * DV, (h + 1) * DV)
        own = v_ref[:, at].astype(F32)
        ext_ref[8 : 8 + TOK, at] = own
        total = own * wv_ref[0:1, at]
        for tap in range(1, TAPS):
            shifted = ext_ref[8 - tap : 8 - tap + TOK, at]
            total = total + jnp.where(valid[tap - 1], shifted * wv_ref[tap : tap + 1, at], 0.0)
        return (total * jax.nn.sigmoid(total)).astype(BF16)

    def patched(first, whole):
        whole = whole.astype(F32)
        return jnp.concatenate([first, whole[8:]], axis=0)

    keys = [patched(first_keys[g], key_ref[g]).astype(BF16) for g in range(GROUPS)]
    beta = beta_ref[...]
    gram = [mm_t(k, k) for k in keys]
    flipped = [k.astype(F32).T for k in keys]
    core = lax.axis_index("ctx") % CORES
    for g in range(GROUPS):
        kb_ref[g] = keys[g]
    heads = range(HEADS)
    masks = [mask_ref[i] for i in range(2 * len(LEVELS))]
    a = [factor_ref[h] * gram[h // 2] for h in heads]
    values = []
    inverses = unit_inverses(
        [m[:HALF, :HALF] for m in a] + [m[HALF:, HALF:] for m in a],
        masks,
        lambda level: values.append(convolved(level)),
    )
    right = [
        jnp.concatenate(
            [
                (carry_ref[h] * keys[h // 2].astype(F32)).astype(BF16),
                values[h],
            ],
            axis=1,
        )
        for h in heads
    ]
    solved = solve_halves(a, inverses[:HEADS], inverses[HEADS:], [beta[h : h + 1] for h in heads], right)
    faded = [(flipped[h // 2] * last_ref[h : h + 1, :]).astype(BF16) for h in heads]
    both = each(mm, faded, solved)
    r, c = rows_and_columns((DK, DK))
    for h in heads:
        wu_ref[h] = solved[h]
        decay = jnp.broadcast_to(carry_ref[h, TOK - 1 : TOK, :], (DK, DK))
        diagonal = jnp.where(r == c, decay, 0.0)
        step = jnp.concatenate([diagonal - both[h][:, :DK], both[h][:, DK:]], axis=1).astype(BF16)

        @pl.when(core == h // 2)
        def _():
            own_ref[h % 2] = step

        @pl.when(core != h // 2)
        def _():
            give_ref[h % 2] = step


def output_kernel(
    q_ref, rim_ref, decay_ref, doc_ref, wq_ref, kb_ref, wu_ref, gate_ref, gain_ref,
    out_ref, reach_ref, factor_ref, ext_ref,
):
    row, col = rows_and_columns()
    lower = (col <= row).astype(BF16)
    eye = (col == row).astype(BF16)
    rim = rim_ref[...].astype(F32)[8:16]
    start = spread([local_start(doc_ref)], eye, 1)[0]
    query_conv = short_conv(ext_ref, q_ref, rim[:, 768:1024], wq_ref, tap_masks(start))
    decay = decay_ref[...]
    cum_row = sum(mm_t(piece, lower) for piece in parts(decay, 3))
    cum_col = spread([decay[h : h + 1] for h in range(HEADS)], lower, 3)
    keep = linked_mask(start)
    scores = []
    for g in range(GROUPS):
        query = query_conv[:, g * DK : (g + 1) * DK].astype(BF16)
        scores.append(mm_t(query, kb_ref[g]))
    for h in range(HEADS):
        g = h // 2
        fade = fading(cum_col[h], cum_row[h : h + 1], start, keep)
        both = mm((fade * scores[g]).astype(BF16), wu_ref[h])
        carry = jnp.where(start < 0.0, jnp.exp(cum_col[h]), 0.0)
        reach = carry * query_conv[:, g * DK : (g + 1) * DK] - both[:, :DK]
        reach_ref[h] = reach.astype(BF16)
        out_ref[h] = both[:, DK:]
        gate = gate_ref[:, h * DV : (h + 1) * DV].astype(F32)
        factor_ref[h] = gain_ref[...] * (gate * jax.nn.sigmoid(gate))


def joined(first, later):
    moved = mm(later[:, :DK], first)
    return jnp.concatenate([moved[:, :DK], moved[:, DK:] + later[:, DK:].astype(F32)], axis=1)


def pair_kernel(own_ref, got_ref, out_ref):
    core = lax.axis_index("ctx") % CORES
    for k in range(2):
        own = own_ref[k]
        got = got_ref[k]
        first = jnp.where(core == 0, own, got)
        later = jnp.where(core == 0, got, own)
        out_ref[k] = joined(first, later).astype(BF16)


def row_kernel(own_ref, one_ref, two_ref, three_ref, after_ref, before_ref, total_ref, alone_ref, slots):
    x = (lax.axis_index("ctx") // CORES) % CHIPS_X
    for step, ref in enumerate((own_ref, one_ref, two_ref, three_ref)):
        slots[x ^ step] = ref[...]
    r, c = rows_and_columns((DK, DK + DV))
    start = (r == c).astype(BF16)
    run = [slots[0, k] for k in range(2)]
    before = [jnp.where(x == 0, start, first) for first in run]
    for place in range(1, CHIPS_X):
        run = [joined(run[k], slots[place, k]).astype(BF16) for k in range(2)]
        if place < CHIPS_X - 1:
            before = [jnp.where(x == place + 1, run[k], before[k]) for k in range(2)]
    for k in range(2):
        total_ref[k] = run[k]
        alone_ref[k] = run[k][:, DK:]
        before_ref[k] = before[k]


def state_kernel(
    own_ref, one_ref, two_ref, three_ref, before_ref, mine_ref, other_ref, keep_ref, give_ref, slots
):
    index = lax.axis_index("ctx")
    core = index % CORES
    y = index // (CORES * CHIPS_X)
    for step, ref in enumerate((own_ref, one_ref, two_ref)):
        slots[(y + CHIPS_Y - step) % CHIPS_Y] = ref[...]
    slots[(y + 1) % CHIPS_Y, :, :, DK:] = three_ref[...]

    def passed(block, state):
        return mm(block[:, :DK], state.astype(BF16)) + block[:, DK:].astype(F32)

    states = [jnp.where(y > 0, slots[0, k][:, DK:].astype(F32), 0.0) for k in range(2)]
    for place in range(1, CHIPS_Y - 1):
        moved = [passed(slots[place, k], states[k]) for k in range(2)]
        states = [jnp.where(place < y, moved[k], states[k]) for k in range(2)]
    states = [passed(before_ref[k], states[k]) for k in range(2)]
    blocks = [jnp.where(core == 0, mine_ref[k], other_ref[k]) for k in range(2)]
    after = [passed(blocks[k], states[k]) for k in range(2)]
    for k in range(2):
        keep_ref[k] = jnp.where(core == 0, states[k], after[k]).astype(BF16)
        give_ref[k] = jnp.where(core == 0, after[k], states[k]).astype(BF16)


KEPT = (0, -3, 2)
TO_AHEAD = (1, -2, 3)
TO_BEHIND = (-1, -4)


def mirrored(step):
    return [
        (ctx * 8 + z, ctx * 8 + (z + (-step if ctx % CORES else step)) % 8)
        for ctx in range(CTX)
        for z in range(8)
    ]


def norm_kernel(
    local_ref, reach_ref, mine_ref, got_ref, factor_ref, keep_ref, ahead_ref, behind_ref, normed_ref
):
    core = lax.axis_index("ctx") % CORES
    place = lax.axis_index("head")
    for h in range(HEADS):
        state = jnp.where(core == h // 2, mine_ref[h % 2], got_ref[h % 2])
        heads = local_ref[h] + mm(reach_ref[h], state)
        inv = lax.rsqrt(jnp.mean(heads * heads, axis=-1, keepdims=True) + EPS)
        normed_ref[:, h * DV : (h + 1) * DV] = (heads * inv * factor_ref[h]).astype(BF16)
    rows = TOK // 8
    sign = 1 - 2 * core
    for steps, ref in ((KEPT, keep_ref), (TO_AHEAD, ahead_ref), (TO_BEHIND, behind_ref)):
        for k, step in enumerate(steps):
            top = pl.multiple_of(((place + sign * step + 8) % 8) * rows, rows)
            ref[k * rows : (k + 1) * rows, :] = normed_ref[pl.ds(top, rows), :]


def keep_kernel(keep_ref, weight_ref, out_ref):
    keep = keep_ref[...]
    for part in range(0, weight_ref.shape[1], 512):
        out_ref[:, part : part + 512] = mm(keep, weight_ref[:, part : part + 512])


def remote_kernel(kept_ref, behind_ref, ahead_ref, behind_w_ref, ahead_w_ref, far_ref, near_ref):
    rows = TOK // 8
    behind = behind_ref[rows:, :]
    ahead = ahead_ref[rows:, :]
    for part in range(0, kept_ref.shape[1], 512):
        at = slice(part, part + 512)
        total = kept_ref[rows:, at] + mm(behind, behind_w_ref[:, at])
        far_ref[:, at] = (total[:rows] + mm(ahead, ahead_w_ref[:, at])).astype(BF16)
        near_ref[:, at] = total[rows:].astype(BF16)


def own_kernel(kept_ref, behind_ref, ahead_ref, behind_w_ref, ahead_w_ref, out_ref):
    rows = TOK // 8
    behind = behind_ref[:rows, :]
    ahead = ahead_ref[:rows, :]
    for part in range(0, kept_ref.shape[1], 512):
        at = slice(part, part + 512)
        total = kept_ref[:rows, at] + mm(behind, behind_w_ref[:, at])
        out_ref[:, at] = total + mm(ahead, ahead_w_ref[:, at])


def sum_kernel(own_ref, one_ref, two_ref, out_ref):
    total = own_ref[...]
    for ref in (one_ref, two_ref):
        total = total + ref[...].astype(F32)
    out_ref[...] = total.astype(BF16)


VMEM = pl.BlockSpec(memory_space=pltpu.VMEM)
HBM = pl.BlockSpec(memory_space=pltpu.HBM)


def whole(shape):
    return pl.BlockSpec(shape, lambda i: (0,) * len(shape))


def call(
    kernel, outs, inputs, scratch=(), flops=0, moved=0, limit=32, specs=None, out_specs=None,
    blocked=False,
):
    if blocked:
        specs = [whole(a.shape) for a in inputs]
        out_specs = [whole(s) for s, _ in outs]
    return pl.pallas_call(
        kernel,
        grid=(1,) if blocked else (),
        out_shape=[jax.ShapeDtypeStruct(s, t) for s, t in outs],
        in_specs=[VMEM] * len(inputs) if specs is None else specs,
        out_specs=[VMEM] * len(outs) if out_specs is None else out_specs,
        scratch_shapes=list(scratch),
        compiler_params=pltpu.CompilerParams(vmem_limit_bytes=limit * MIB),
        cost_estimate=pl.CostEstimate(flops=flops, bytes_accessed=moved, transcendentals=0),
    )(*inputs)


def on_device(
    query_in, key_in, value_in, out_gate, log_decay, beta_gate, doc_start,
    conv_query, conv_key, conv_value, norm_gain, out_weight,
):
    doc_row = doc_start.reshape(1, TOK)
    gain_row = norm_gain.reshape(1, DV)
    width = out_weight.shape[1]
    last = TOK // RIM - 1
    edge = pl.pallas_call(
        pack_kernel,
        grid=(1,),
        out_shape=jax.ShapeDtypeStruct((RIM, 1024), BF16),
        in_specs=[pl.BlockSpec((RIM, n), lambda i: (last, 0)) for n in (256, 512, 256)],
        out_specs=pl.BlockSpec((RIM, 1024), lambda i: (0, 0)),
        cost_estimate=pl.CostEstimate(flops=5_000_000_000, bytes_accessed=0, transcendentals=0),
    )(key_in, value_in, query_in)
    near_weight = lax.ppermute(
        lax.optimization_barrier((out_weight, edge))[0], ("ctx", "head"), mirrored(1)
    )
    rim = lax.ppermute(edge, "ctx", [(i, (i + 1) % CTX) for i in range(CTX)])
    wide = (2, DK, DK + DV)
    early = call(
        early_kernel,
        [
            ((GROUPS, TOK, DK), BF16), ((HEADS, TOK, TOK), F32),
            ((HEADS, TOK, 128), F32), ((HEADS, TOK), F32), ((TOK, 128), F32), ((RIM, 256), BF16),
            ((2 * len(LEVELS), HALF, HALF), BF16),
        ],
        [key_in, log_decay, beta_gate, doc_row, conv_key],
        [pltpu.VMEM((8 + TOK, 256), F32)],
        flops=500_000_000, moved=0, limit=48, blocked=True,
    )
    keys, factor, carry, final, start, head, masks = early
    solved, keys, own, give = call(
        map_kernel,
        [((HEADS, TOK, DK + DV), BF16), ((GROUPS, TOK, DK), BF16), (wide, BF16), (wide, BF16)],
        [rim, head, start, keys, value_in, factor, carry, final, beta_gate, conv_key, conv_value, masks],
        [pltpu.VMEM((8 + TOK, HEADS * DV), F32)],
        flops=4_000_000_000, moved=2_000_000,
    )
    other = lax.ppermute(give, "ctx", core_swap())
    (pair,) = call(pair_kernel, [(wide, BF16)], [own, other], flops=20_000_000, moved=400_000)
    near = [lax.ppermute(pair, "ctx", pairs_x(k)) for k in (1, 2, 3)]
    local, reach, factor = call(
        output_kernel,
        [((HEADS, TOK, DV), F32), ((HEADS, TOK, DK), BF16), ((HEADS, TOK, DV), F32)],
        [query_in, rim, log_decay, doc_row, conv_query, keys, solved, out_gate, gain_row],
        [pltpu.VMEM((8 + TOK, 256), F32)],
        flops=2_000_000_000, moved=2_000_000,
    )
    narrow = (2, DK, DV)
    before, total, alone = call(
        row_kernel, [(wide, BF16), (wide, BF16), (narrow, BF16)], [pair] + near + [reach],
        [pltpu.VMEM((CHIPS_X,) + wide, BF16)], flops=60_000_000, moved=800_000,
        specs=[VMEM] * 4 + [HBM],
    )
    far = [
        lax.ppermute(total, "ctx", along_y(1)),
        lax.ppermute(total, "ctx", along_y(2)),
        lax.ppermute(alone, "ctx", along_y(3)),
    ]
    mine, to_other = call(
        state_kernel, [(narrow, BF16), (narrow, BF16)], [total] + far + [before, own, other],
        [pltpu.VMEM((CHIPS_Y,) + wide, BF16)], flops=60_000_000, moved=1_000_000,
    )
    got = lax.ppermute(to_other, "ctx", core_swap())
    late_weight, _ = lax.optimization_barrier((near_weight, got))
    far_weight = lax.ppermute(late_weight, "ctx", core_swap())
    block = TOK // 8

    def normed_rows(steps):
        return ((len(steps) * block, HEADS * DV), BF16)

    keep, to_ahead, to_behind = call(
        norm_kernel, [normed_rows(KEPT), normed_rows(TO_AHEAD), normed_rows(TO_BEHIND)],
        [local, reach, mine, got, factor],
        [pltpu.VMEM((TOK, HEADS * DV), BF16)],
        flops=100_000_000, moved=1_500_000,
    )
    from_behind = lax.ppermute(to_ahead, ("ctx", "head"), mirrored(1))
    from_ahead = lax.ppermute(to_behind, ("ctx", "head"), mirrored(-1))
    (kept,) = call(
        keep_kernel, [((len(KEPT) * block, width), F32)], [keep, out_weight],
        flops=200_000_000, moved=3_000_000,
    )
    gathered = [kept, from_behind, from_ahead, near_weight, far_weight]
    far_part, near_part = call(
        remote_kernel, [((block, width), BF16)] * 2, gathered, flops=200_000_000, moved=4_000_000,
    )
    (own_part,) = call(
        own_kernel, [((block, width), F32)], gathered, flops=200_000_000, moved=4_000_000,
    )
    far_part = lax.ppermute(far_part, ("ctx", "head"), mirrored(-3))
    near_part = lax.ppermute(near_part, ("ctx", "head"), mirrored(2))
    (mixed,) = call(
        sum_kernel, [((block, width), BF16)], [own_part, far_part, near_part],
        flops=1_000_000, moved=800_000,
    )
    return mixed


def solution(mesh):
    placed = (
        P("ctx", "head"),
        P("ctx", "head"),
        P("ctx", "head"),
        P("ctx", "head"),
        P("head", "ctx"),
        P("head", "ctx"),
        P("ctx"),
        P(None, "head"),
        P(None, "head"),
        P(None, "head"),
        P(),
        P("head", None),
    )
    return jax.shard_map(
        on_device, mesh=mesh, in_specs=placed, out_specs=P(("ctx", "head"), None), check_vma=False
    )
```
